32 devices in a mesh: rep: 8 (over y, x, core), exp: 4 (over z).
Axes of the slice: x: 2, y: 2, z: 4, core: 2. Of those that a mesh axis runs over, the one named last changes fastest.
Arguments:
- inputs: bfloat16 [18912, 768], P(('rep', 'exp')), may hold values from -6 to 6
- routes: int32 [18912, 2], P(('rep', 'exp')), may hold values from 0 to 3, all different within a row; in each aligned block of 591 rows (0 to 590, 591 to 1181, ...) at most 591 rows name the same one
- ln1_gain: float32 [768], replicated, may hold values from 0.5 to 1.5
- ln1_bias: float32 [768], replicated, may hold values from -1.5 to 1.5
- w_qkv: bfloat16 [768, 2304], replicated, may hold values from -0.21875 to 0.21875
- query_bias: float32 [768], replicated, may hold values from -2.5 to 2.5
- value_bias: float32 [768], replicated, may hold values from -2.5 to 2.5
- w_out: bfloat16 [768, 768], replicated, may hold values from -1.75 to 1.75
- out_bias: float32 [768], replicated, may hold values from -2.5 to 2.5
- ln2_gain: float32 [768], replicated, may hold values from 0.5 to 1.5
- ln2_bias: float32 [768], replicated, may hold values from -1.5 to 1.5
- router: bfloat16 [768, 4], replicated, may hold values from -0.15625 to 0.15625
- experts_in: bfloat16 [4, 768, 3072], P('exp'), may hold values from -0.21875 to 0.21875
- experts_in_bias: float32 [4, 3072], P('exp'), may hold values from -2.5 to 2.5
- experts_out: bfloat16 [4, 3072, 768], P('exp'), may hold values from -0.875 to 0.875
- experts_out_bias: float32 [4, 768], P('exp'), may hold values from -4 to 4
- cotangent: bfloat16 [18912, 768], P(('rep', 'exp')), may hold values from -6 to 6
Outputs:
- out: bfloat16 [18912, 768], P(('rep', 'exp'))
- grad_inputs: bfloat16 [18912, 768], P(('rep', 'exp'))
- grad_ln1_gain: float32 [768], replicated
- grad_ln1_bias: float32 [768], replicated
- grad_w_qkv: float32 [768, 2304], replicated
- grad_query_bias: float32 [768], replicated
- grad_value_bias: float32 [768], replicated
- grad_w_out: float32 [768, 768], replicated
- grad_out_bias: float32 [768], replicated
- grad_ln2_gain: float32 [768], replicated
- grad_ln2_bias: float32 [768], replicated
- grad_router: float32 [768, 4], replicated
- grad_experts_in: float32 [4, 768, 3072], P('exp')
- grad_experts_in_bias: float32 [4, 3072], P('exp')
- grad_experts_out: float32 [4, 3072, 768], P('exp')
- grad_experts_out_bias: float32 [4, 768], P('exp')
The draws below stay inside these ranges and needn't reach their ends.
Inputs may be any that keep to these rules, and one draw needn't show every extreme that they name: `routes`: each row names 2 different experts. Within the 591 rows of one device, no expert is named more than 591 times, a bound that some block reaches.
All inputs are finite; a program needn't handle non-finite values.
Results may differ from the reference program's by a relative error of at most 0.015.
Values may be sent and summed in bfloat16 or wider, within the bound.
No kernel may reach another device: no remote copies, remote signals or barrier semaphores. Data moves between devices by JAX's collectives and lax.ppermute only.
A program may use at most 256 MiB of HBM per device.

```python
import math
import jax
import jax.numpy as jnp
import numpy as np
from jax import lax

D = 768
HEADS = 12
HEAD_DIM = 64
FF = 3072
SEQ = 197
TOP = 2
TOK_DEV = 591
EXPERTS = 4
CAP = 591
TOKENS = 18912
DEVICES = 32


def shard_levels(rng, dims, pieces, smallest, top_value):
    def one(axis_at, blocks):
        steps = jax.random.uniform(jax.random.fold_in(jax.random.fold_in(rng, 6), axis_at), (blocks,), jnp.float32, smallest / len(pieces), top_value / len(pieces))
        return jnp.repeat(jnp.exp(steps), dims[axis_at] // blocks).reshape((-1,) + (1,) * (len(dims) - axis_at - 1))

    gain = one(*pieces[0])
    for cut in pieces[1:]:
        gain = gain * one(*cut)
    return gain


def routed_block(stream_key, own, number, rows, amount, top, limit, skew):
    sequence = jax.random.permutation(stream_key, amount)
    packed, ordinary = portions_of(amount, rows * top, limit, skew, True), portions_of(amount, rows * top, limit, skew, False)
    places = jnp.arange(amount)

    def named(tallies, turn):
        used = int((tallies > 0).sum())
        fixed = max(1, used // 4)
        shifted = fixed + (places - fixed + turn * (used - fixed)) % max(1, amount - fixed)
        return jnp.zeros((amount,), jnp.int32).at[sequence[jnp.where(places < fixed, places, shifted)]].set(jnp.asarray(tallies, jnp.int32))

    tallies = jnp.where(number % 4 == 0, named(packed, number // 4), named(ordinary, number - number // 4 - 1))
    mixed = jax.random.permutation(jax.random.fold_in(own, 3), amount)
    source_of, sink = mixed[0:amount // 2 * 2:2], mixed[1:amount // 2 * 2:2]
    room = jnp.minimum(tallies[source_of] - 1, limit - tallies[sink]) // 2
    room = jnp.where((source_of == sequence[0]) | (sink == sequence[0]) | (tallies[sink] == 0), 0, jnp.maximum(room, 0))
    shifted = jax.random.randint(jax.random.fold_in(own, 4), (amount // 2,), 0, 1 << 20) % (room + 1)
    tallies = tallies.at[source_of].add(-shifted).at[sink].add(shifted)
    labels = jnp.searchsorted(jnp.cumsum(tallies), jnp.arange(rows * top), side="right").astype(jnp.int32)
    listing = labels.reshape(top, rows).T
    listing = listing[jax.random.permutation(jax.random.fold_in(own, 1), rows)]
    turn = jax.random.randint(jax.random.fold_in(own, 2), (rows, 1), 0, top)
    return jnp.take_along_axis(listing, (jnp.arange(top)[None, :] + turn) % top, axis=1)


def portions_of(amount, total, limit, skew, full):
    portions = [(1 << 20) // math.isqrt(grade ** skew) + 1 for grade in range(1, amount + 1)]
    largest = limit if full else min(limit, max(-(-total // amount), total * portions[0] // sum(portions)))
    least = 1 if total - largest >= amount - 1 else 0
    counts, surplus = [largest] + [least] * (amount - 1), total - largest - least * (amount - 1)
    while surplus > 0:
        movable = [i for i in range(1, amount) if counts[i] < largest] or [i for i in range(1, amount) if counts[i] < limit]
        whole, remaining = sum([portions[i] for i in movable]), surplus
        for i in movable:
            extra = min(limit - counts[i], max(1, remaining * portions[i] // whole), surplus)
            counts[i] = counts[i] + extra
            surplus = surplus - extra
    return np.array(counts)


def noise(key, shape, scale, most, shards=(), kind=jnp.bfloat16):
    drawn = jax.random.normal(key, shape, jnp.float32) * scale
    if len(shards) > 0:
        drawn = shard_levels(key, shape, shards, -0.22, 0.18) * drawn
    return jnp.clip(drawn, min=-most, max=most).astype(kind)


def setup_inputs(seed: int = 0) -> dict:
    key_of = jax.random.split(jax.random.key(seed), 18)
    inputs = noise(key_of[0], (TOKENS, D), 1.0, 6.0, ((0, 32),))
    routes_keys = jax.random.split(jax.random.fold_in(key_of[1], 1), TOKENS // TOK_DEV)
    routes_turns = jax.random.permutation(jax.random.fold_in(key_of[1], 3), TOKENS // TOK_DEV)
    routes = jax.vmap(lambda own, number: routed_block(jax.random.fold_in(key_of[1], 2), own, number, TOK_DEV, EXPERTS, TOP, CAP, 1))(routes_keys, routes_turns).reshape((TOKENS, TOP))
    ln1_gain = jnp.clip(1.0 + 0.1 * jax.random.normal(key_of[2], (D,), jnp.float32), 0.5, 1.5)
    ln1_bias = noise(key_of[3], (D,), 0.3, 1.5, (), jnp.float32)
    w_qkv = noise(key_of[4], (D, 3 * D), D ** -0.5, 0.21875)
    query_bias = noise(key_of[5], (D,), 0.5, 2.5, (), jnp.float32)
    value_bias = noise(key_of[6], (D,), 0.5, 2.5, (), jnp.float32)
    w_out = noise(key_of[7], (D, D), (D // 64) ** -0.5, 1.75)
    out_bias = noise(key_of[8], (D,), 0.5, 2.5, (), jnp.float32)
    ln2_gain = jnp.clip(1.0 + 0.1 * jax.random.normal(key_of[9], (D,), jnp.float32), 0.5, 1.5)
    ln2_bias = noise(key_of[10], (D,), 0.3, 1.5, (), jnp.float32)
    router = noise(key_of[11], (D, EXPERTS), (2 * D) ** -0.5, 0.15625)
    experts_in = noise(key_of[12], (EXPERTS, D, FF), D ** -0.5, 0.21875, ((0, 4),))
    experts_in_bias = noise(key_of[13], (EXPERTS, FF), 0.5, 2.5, ((0, 4),), jnp.float32)
    experts_out = noise(key_of[14], (EXPERTS, FF, D), (FF // 64) ** -0.5, 0.875, ((0, 4),))
    experts_out_bias = noise(key_of[15], (EXPERTS, D), 1.0, 4.0, ((0, 4),), jnp.float32)
    cotangent = noise(key_of[16], (TOKENS, D), 1.0, 6.0, ((0, 32),))
    return dict(inputs=inputs, routes=routes, ln1_gain=ln1_gain, ln1_bias=ln1_bias, w_qkv=w_qkv, query_bias=query_bias, value_bias=value_bias, w_out=w_out, out_bias=out_bias, ln2_gain=ln2_gain, ln2_bias=ln2_bias, router=router, experts_in=experts_in, experts_in_bias=experts_in_bias, experts_out=experts_out, experts_out_bias=experts_out_bias, cotangent=cotangent)


@jax.custom_vjp
def low(v):
    return lax.optimization_barrier(v.astype(jnp.bfloat16)).astype(jnp.float32)

@jax.custom_vjp
def low_back(v):
    return v

def low_keep(v):
    return (low(v), None)

def low_pass(kept, grad):
    return (grad,)

def back_keep(v):
    return (v, None)

def back_low(kept, grad):
    return (low(grad),)
low.defvjp(low_keep, low_pass)
low_back.defvjp(back_keep, back_low)
NORM_EPS = 1e-06
PRECISE = lax.Precision.HIGHEST

def layer_norm(values, gain_vec, offset):
    average = lax.optimization_barrier(jnp.mean(values, axis=-1, keepdims=True))
    centred = values - average
    spread = lax.optimization_barrier(jnp.mean(centred * centred, axis=-1, keepdims=True))
    return centred * lax.rsqrt(spread + NORM_EPS) * gain_vec + offset

def slot_table(route_ids, expert_count, capacity):
    flat_ids = route_ids.reshape(-1).astype(jnp.int32)
    one_hot = (flat_ids[:, None] == jnp.arange(expert_count, dtype=jnp.int32)[None, :]).astype(jnp.int32)
    earlier = jnp.cumsum(one_hot, axis=0) - one_hot
    position = lax.optimization_barrier(jnp.sum(earlier * one_hot, axis=1))
    return (flat_ids * capacity + position).astype(jnp.int32)

def forward_block(params_f, inputs_blk, routes_blk):
    ln1_gain, ln1_bias, w_qkv, query_bias, value_bias, w_out, out_bias, ln2_gain, ln2_bias, router, experts_in, experts_in_bias, experts_out, experts_out_bias = params_f
    tok_count = inputs_blk.shape[0]
    heads_shape = (tok_count // SEQ, SEQ, HEADS, HEAD_DIM)
    normed = low(layer_norm(inputs_blk, ln1_gain, ln1_bias))
    joined = jnp.dot(normed, w_qkv, precision=PRECISE)
    queries = low(low_back(joined[:, :D] + query_bias)).reshape(heads_shape)
    keys_all = low(low_back(joined[:, D:2 * D])).reshape(heads_shape)
    values_all = low(low_back(joined[:, 2 * D:] + value_bias)).reshape(heads_shape)
    scores = low_back(jnp.einsum('bqhd,bkhd->bhqk', queries, keys_all, precision=PRECISE) * HEAD_DIM ** (-0.5))
    probs = jax.nn.softmax(scores, axis=-1)
    context = jnp.einsum('bhqk,bkhd->bqhd', low(probs), values_all, precision=PRECISE)
    context = low(low_back(context.reshape(tok_count, D)))
    attended = low_back(jnp.dot(context, w_out, precision=PRECISE) + out_bias)
    hidden = inputs_blk + attended
    mixed = low(layer_norm(hidden, ln2_gain, ln2_bias))
    logits = low_back(jnp.dot(mixed, router, precision=PRECISE))
    gate_probs = jax.nn.softmax(logits, axis=-1)
    route_hot = (routes_blk[:, :, None] == jnp.arange(EXPERTS, dtype=jnp.int32)[None, None, :]).astype(jnp.float32)
    gate_vals = lax.optimization_barrier(jnp.sum(gate_probs[:, None, :] * route_hot, axis=-1))
    slot_ids = slot_table(routes_blk, EXPERTS, CAP)
    routed = jnp.stack([low_back(mixed) for route_num in range(TOP)], axis=1).reshape(TOP * tok_count, D)
    buffer = jnp.zeros((EXPERTS * CAP, D), jnp.float32).at[slot_ids].set(routed)
    pre_act = jnp.einsum('ecd,edf->ecf', buffer.reshape(EXPERTS, CAP, D), experts_in, precision=PRECISE)
    pre_act = low_back(pre_act + experts_in_bias[:, None, :])
    activ = low(jax.nn.gelu(pre_act, approximate=False))
    expert_out = jnp.einsum('ecf,efd->ecd', activ, experts_out, precision=PRECISE) + experts_out_bias[:, None, :]
    expert_out = low(low_back(expert_out)).reshape(EXPERTS * CAP, D)
    returned = expert_out[slot_ids].reshape(tok_count, TOP, D)
    return hidden + lax.optimization_barrier(jnp.sum(gate_vals[:, :, None] * returned, axis=1))

def reference(inputs, routes, ln1_gain, ln1_bias, w_qkv, query_bias, value_bias, w_out, out_bias, ln2_gain, ln2_bias, router, experts_in, experts_in_bias, experts_out, experts_out_bias, cotangent):
    params_f = tuple((weight_arr.astype(jnp.float32) for weight_arr in (ln1_gain, ln1_bias, w_qkv, query_bias, value_bias, w_out, out_bias, ln2_gain, ln2_bias, router, experts_in, experts_in_bias, experts_out, experts_out_bias)))
    inputs_f = inputs.astype(jnp.float32).reshape(DEVICES, TOK_DEV, D)
    routes_blocks = routes.reshape(DEVICES, TOK_DEV, TOP).astype(jnp.int32)

    def whole(params_in, inputs_in):

        def one_block(pair_in):
            return forward_block(params_in, pair_in[0], pair_in[1])
        return lax.map(jax.checkpoint(one_block), (inputs_in, routes_blocks))
    result, pull_back = jax.vjp(whole, params_f, inputs_f)
    grads_w, grad_in = pull_back(cotangent.astype(jnp.float32).reshape(DEVICES, TOK_DEV, D))
    return (result.reshape(TOKENS, D).astype(jnp.bfloat16), grad_in.reshape(TOKENS, D).astype(jnp.bfloat16), grads_w[0], grads_w[1], grads_w[2], grads_w[3], grads_w[4], grads_w[5], grads_w[6], grads_w[7], grads_w[8], grads_w[9], grads_w[10], grads_w[11], grads_w[12], grads_w[13])
```

```python
import functools

import jax
import jax.numpy as jnp
from jax import lax
from jax.experimental import pallas as pl
from jax.experimental.pallas import tpu as pltpu
from jax.sharding import PartitionSpec as P

HEADS = 12
HEAD_DIM = 64
SEQ = 197
NORM_EPS = 1e-06
F32 = jnp.float32
BF16 = jnp.bfloat16
LANES = 128
PAIR = LANES // HEAD_DIM
SEQ_PAD = 208
FF_TILE = 512
VMEM_BYTES = 58 * 2**20
TAIL_SCALE = 0.305
TAIL_COEFS = (
    0.1216396663821839,
    0.12246803351870969,
    0.10341227166034979,
    0.12105264456174025,
    -0.03803921974174099,
    0.18578799927872533,
    -0.1530311110530253,
    0.03670976324394601,
)
INV_SQRT_2PI = 0.3989422804014327


def dot(lhs, rhs):
    return lax.dot_general(lhs, rhs, (((1,), (0,)), ((), ())), preferred_element_type=F32)


def dot_rt(lhs, rhs):
    return lax.dot_general(lhs, rhs, (((1,), (1,)), ((), ())), preferred_element_type=F32)


def dot_lt(lhs, rhs):
    return lax.dot_general(lhs, rhs, (((0,), (0,)), ((), ())), preferred_element_type=F32)


def row_mean(values):
    return jnp.mean(values, axis=-1, keepdims=True)


def unit_norm(values):
    centred = values - row_mean(values)
    scale = lax.rsqrt(row_mean(centred * centred) + NORM_EPS)
    return centred * scale, scale


def column_sum(values):
    return jnp.sum(values, axis=0, keepdims=True)


def gelu_parts(pre):
    size = jnp.abs(pre)
    bell = jnp.exp(pre * pre * -0.5)
    frac = 1.0 / (1.0 + TAIL_SCALE * size)
    poly = jnp.full_like(pre, TAIL_COEFS[-1])
    for coef in TAIL_COEFS[-2::-1]:
        poly = poly * frac + coef
    tail = bell * (poly * frac)
    return jnp.where(pre >= 0, 1.0 - tail, tail), bell * INV_SQRT_2PI


def pair_masks(rows):
    lane = lax.broadcasted_iota(jnp.int32, (rows, LANES), 1)
    return [(lane >= h * HEAD_DIM) & (lane < (h + 1) * HEAD_DIM) for h in range(PAIR)]


def stack_heads(values, masks):
    return jnp.concatenate([jnp.where(m, values, 0.0) for m in masks], axis=0).astype(BF16)


def unstack_heads(values, masks):
    rows = values.shape[0] // PAIR
    picked = values[:rows]
    for h in range(1, PAIR):
        picked = jnp.where(masks[h], values[h * rows : (h + 1) * rows], picked)
    return picked


def probabilities(scores):
    key_id = lax.broadcasted_iota(jnp.int32, scores.shape, 1)
    scores = jnp.where(key_id < SEQ, scores, -1e30)
    weights = jnp.exp(scores - jnp.max(scores, axis=-1, keepdims=True))
    return weights * (1.0 / jnp.sum(weights, axis=-1, keepdims=True))


def attend_kernel(
    x_ref, g1_ref, b1_ref, wqkv_ref, qb_ref, vb_ref, wout_ref, ob_ref, g2_ref, b2_ref,
    qkv_ref, ctx_ref, hidden_ref, mixed_ref,
    qkv_s, ctx_s,
):
    toks, width = x_ref.shape
    spare = qkv_s.shape[0] - toks
    x = x_ref[...].astype(F32)
    unit, _ = unit_norm(x)
    normed = (unit * g1_ref[...] + b1_ref[...]).astype(BF16)
    for part, bias in ((0, qb_ref), (1, None), (2, vb_ref)):
        cols = pl.ds(part * width, width)
        joined = dot(normed, wqkv_ref[:, cols])
        if bias is not None:
            joined = joined + bias[...]
        joined = joined.astype(BF16)
        qkv_ref[:, cols] = joined
        qkv_s[0:toks, cols] = joined.astype(F32)
    qkv_s[toks:, :] = jnp.zeros((spare, 3 * width), F32)
    masks = pair_masks(SEQ_PAD)
    for img in range(toks // SEQ):
        rows = pl.ds(img * SEQ, SEQ_PAD)
        for at in range(0, width, LANES):
            query = stack_heads(qkv_s[rows, at : at + LANES], masks)
            key = qkv_s[rows, width + at : width + at + LANES].astype(BF16)
            value = qkv_s[rows, 2 * width + at : 2 * width + at + LANES].astype(BF16)
            probs = probabilities(dot_rt(query, key) * HEAD_DIM**-0.5).astype(BF16)
            ctx_s[rows, at : at + LANES] = unstack_heads(dot(probs, value), masks)
    ctx = ctx_s[0:toks, :].astype(BF16)
    ctx_ref[...] = ctx
    hidden = x + dot(ctx, wout_ref[...]) + ob_ref[...]
    hidden_ref[...] = hidden
    unit2, _ = unit_norm(hidden)
    mixed_ref[...] = (unit2 * g2_ref[...] + b2_ref[...]).astype(BF16)


def expert_kernel(
    me_ref,
    x_ref, up_ref, routes_ref, router_ref, router_t_ref, win_ref, bin_ref, wout_ref, bout_ref,
    part_ref, back_ref, activ_ref, gpre_ref, geout_ref, grouter_ref,
    out_s, back_s, probs_s, gate_s,
):
    step = pl.program_id(0)
    me = me_ref[0]

    @pl.when(step == 0)
    def _():
        logits = dot(x_ref[...], router_ref[...])
        weights = jnp.exp(logits - jnp.max(logits, axis=-1, keepdims=True))
        probs = weights / jnp.sum(weights, axis=-1, keepdims=True)
        probs_s[...] = probs
        mine = lax.broadcasted_iota(jnp.int32, probs.shape, 1) == me
        named = jnp.max((routes_ref[...] == me).astype(F32), axis=-1, keepdims=True)
        gate = jnp.sum(jnp.where(mine, probs, 0.0), axis=-1, keepdims=True) * named
        gate_s[...] = gate
        geout_ref[...] = (gate * up_ref[...].astype(F32)).astype(BF16)
        out_s[...] = jnp.zeros_like(out_s)
        back_s[...] = jnp.zeros_like(back_s)

    pre = dot(x_ref[...], win_ref[...]) + bin_ref[...]
    phi, bell = gelu_parts(pre)
    activ = (pre * phi).astype(BF16)
    activ_ref[...] = activ
    gpre = (dot_rt(geout_ref[...], wout_ref[...]) * (phi + pre * bell)).astype(BF16)
    gpre_ref[...] = gpre
    out_s[...] += dot(activ, wout_ref[...])
    back_s[...] += dot_rt(gpre, win_ref[...])

    @pl.when(step == pl.num_programs(0) - 1)
    def _():
        expert_out = (out_s[...] + bout_ref[...]).astype(BF16).astype(F32)
        gate = gate_s[...]
        probs = probs_s[...]
        part_ref[...] = (gate * expert_out).astype(BF16)
        route_grad = jnp.sum(up_ref[...].astype(F32) * expert_out, axis=-1, keepdims=True)
        mine = (lax.broadcasted_iota(jnp.int32, probs.shape, 1) == me).astype(F32)
        glogits = gate * route_grad * (mine - probs)
        back = back_s[...].astype(BF16).astype(F32)
        for other in range(probs.shape[1]):
            back = back + glogits[:, other : other + 1] * router_t_ref[other : other + 1, :]
        back_ref[...] = back.astype(BF16)
        coarse = glogits.astype(BF16)
        fine = (glogits - coarse.astype(F32)).astype(BF16)
        grouter_ref[...] = dot_lt(coarse, x_ref[...]) + dot_lt(fine, x_ref[...])


def expert_weights_kernel(count, *refs):
    tall, wide = refs[:count], refs[count : 2 * count]
    grad_ref = refs[2 * count]
    total = dot_lt(tall[0][...], wide[0][...])
    for lhs, rhs in zip(tall[1:], wide[1:]):
        total = total + dot_lt(lhs[...], rhs[...])
    grad_ref[0 : total.shape[0], :] = total.astype(BF16)


def expert_in_grads_kernel(count, *refs):
    expert_weights_kernel(count, *refs[: 2 * count], refs[3 * count])
    grad_ref = refs[3 * count]
    rows, tile = refs[0].shape[1], grad_ref.shape[1]
    sums = column_sum(refs[count][...].astype(F32))
    for ref in refs[count + 1 : 2 * count]:
        sums = sums + column_sum(ref[...].astype(F32))
    outs = column_sum(refs[2 * count][...].astype(F32))
    for ref in refs[2 * count + 1 : 3 * count]:
        outs = outs + column_sum(ref[...].astype(F32))
    spare = grad_ref.shape[0] - rows
    row_id = lax.broadcasted_iota(jnp.int32, (spare, tile), 0)
    small = jnp.where(row_id == 0, sums, jnp.where(row_id == 1, outs, 0.0))
    grad_ref[rows:, :] = small.astype(BF16)


def attend_back_kernel(
    gmix_ref, up_ref, x_ref, hidden_ref, qkv_ref, ctx_ref, g1_ref, b1_ref, wqkv_ref, wout_ref, g2_ref,
    ginput_ref, grads_ref, small_ref,
    qkv_s, gctx_s, gjoin_s,
):
    toks, width = x_ref.shape
    spare = qkv_s.shape[0] - toks
    gmix = gmix_ref[...].astype(F32)
    unit2, scale2 = unit_norm(hidden_ref[...])
    grad_g2 = column_sum(gmix * unit2)
    grad_b2 = column_sum(gmix)
    m2 = gmix * g2_ref[...]
    ghidden = up_ref[...].astype(F32) + scale2 * (m2 - row_mean(m2) - unit2 * row_mean(m2 * unit2))
    gatt = ghidden.astype(BF16)
    grad_ob = column_sum(gatt.astype(F32))
    grads_ref[0:width, 3 * width :] = dot_lt(ctx_ref[...], gatt).astype(BF16)
    gctx_s[0:toks, :] = dot_rt(gatt, wout_ref[...]).astype(BF16).astype(F32)
    gctx_s[toks:, :] = jnp.zeros((spare, width), F32)
    qkv_s[0:toks, :] = qkv_ref[...].astype(F32)
    qkv_s[toks:, :] = jnp.zeros((spare, 3 * width), F32)
    masks = pair_masks(SEQ_PAD)
    row_ok = lax.broadcasted_iota(jnp.int32, (SEQ_PAD, 1), 0) < SEQ
    for img in range(toks // SEQ):
        rows = pl.ds(img * SEQ, SEQ_PAD)
        for at in range(0, width, LANES):
            query = stack_heads(jnp.where(row_ok, qkv_s[rows, at : at + LANES], 0.0), masks)
            key = qkv_s[rows, width + at : width + at + LANES].astype(BF16)
            value = qkv_s[rows, 2 * width + at : 2 * width + at + LANES].astype(BF16)
            gctx = stack_heads(jnp.where(row_ok, gctx_s[rows, at : at + LANES], 0.0), masks)
            probs = probabilities(dot_rt(query, key) * HEAD_DIM**-0.5)
            gvalue = dot_lt(probs.astype(BF16), gctx)
            gweights = dot_rt(gctx, value)
            inner = jnp.sum(gweights * probs, axis=-1, keepdims=True)
            gscores = (probs * (gweights - inner)).astype(BF16)
            gquery = unstack_heads(dot(gscores, key), masks) * HEAD_DIM**-0.5
            gkey = dot_lt(gscores, query) * HEAD_DIM**-0.5
            gjoin_s[rows, at : at + LANES] = gquery
            gjoin_s[rows, width + at : width + at + LANES] = gkey
            gjoin_s[rows, 2 * width + at : 2 * width + at + LANES] = gvalue
    gjoin = gjoin_s[0:toks, :].astype(BF16)
    grad_qb = column_sum(gjoin[:, :width].astype(F32))
    grad_vb = column_sum(gjoin[:, 2 * width :].astype(F32))
    x = x_ref[...].astype(F32)
    unit1, scale1 = unit_norm(x)
    normed = (unit1 * g1_ref[...] + b1_ref[...]).astype(BF16)
    grads_ref[0:width, 0 : 3 * width] = dot_lt(normed, gjoin).astype(BF16)
    gnormed = dot_rt(gjoin, wqkv_ref[...])
    grad_g1 = column_sum(gnormed * unit1)
    grad_b1 = column_sum(gnormed)
    m1 = gnormed * g1_ref[...]
    ginput = ghidden + scale1 * (m1 - row_mean(m1) - unit1 * row_mean(m1 * unit1))
    ginput_ref[...] = ginput.astype(BF16)
    for at, small in enumerate((grad_g1, grad_b1, grad_qb, grad_vb, grad_ob, grad_g2, grad_b2)):
        small_ref[at : at + 1, :] = small
    small_ref[7:, :] = jnp.zeros((1, width), F32)


def params(**more):
    return pltpu.CompilerParams(vmem_limit_bytes=VMEM_BYTES, **more)


def cost(flops, moved):
    return pl.CostEstimate(flops=flops, bytes_accessed=moved, transcendentals=0)


def whole():
    return pl.BlockSpec(memory_space=pltpu.VMEM)


def attend(inputs, g1, b1, w_qkv, qb, vb, w_out, ob, g2, b2):
    toks, width = inputs.shape
    padded = -(-(toks - SEQ + SEQ_PAD) // 16) * 16
    return pl.pallas_call(
        attend_kernel,
        out_shape=(
            jax.ShapeDtypeStruct((toks, 3 * width), BF16),
            jax.ShapeDtypeStruct((toks, width), BF16),
            jax.ShapeDtypeStruct((toks, width), F32),
            jax.ShapeDtypeStruct((toks, width), BF16),
        ),
        in_specs=[whole()] * 10,
        out_specs=(whole(),) * 4,
        scratch_shapes=[pltpu.VMEM((padded, 3 * width), F32), pltpu.VMEM((padded, width), F32)],
        compiler_params=params(),
        cost_estimate=cost(16 * toks * width * width, 16 * 2**20),
        name="attend",
    )(inputs, g1, b1, w_qkv, qb, vb, w_out, ob, g2, b2)


def attend_back(gmix, up, inputs, hidden, qkv, ctx, g1, b1, w_qkv, w_out, g2):
    toks, width = inputs.shape
    padded = -(-(toks - SEQ + SEQ_PAD) // 16) * 16
    return pl.pallas_call(
        attend_back_kernel,
        out_shape=(
            jax.ShapeDtypeStruct((toks, width), BF16),
            jax.ShapeDtypeStruct((width, 4 * width), BF16),
            jax.ShapeDtypeStruct((8, width), F32),
        ),
        in_specs=[whole()] * 11,
        out_specs=(whole(),) * 3,
        scratch_shapes=[
            pltpu.VMEM((padded, 3 * width), F32),
            pltpu.VMEM((padded, width), F32),
            pltpu.VMEM((padded, 3 * width), F32),
        ],
        compiler_params=params(),
        cost_estimate=cost(32 * toks * width * width, 20 * 2**20),
        name="attend_back",
    )(gmix, up, inputs, hidden, qkv, ctx, g1, b1, w_qkv, w_out, g2)


def expert_block(me, rows, up, routes, router, router_t, w_in, b_in, w_out, b_out):
    toks, width = rows.shape
    experts = router.shape[1]
    hidden = w_in.shape[1]
    fixed = lambda shape: pl.BlockSpec(shape, lambda f, m: (0, 0))
    return pl.pallas_call(
        expert_kernel,
        out_shape=(
            jax.ShapeDtypeStruct((toks, width), BF16),
            jax.ShapeDtypeStruct((toks, width), BF16),
            jax.ShapeDtypeStruct((toks, hidden), BF16),
            jax.ShapeDtypeStruct((toks, hidden), BF16),
            jax.ShapeDtypeStruct((toks, width), BF16),
            jax.ShapeDtypeStruct((experts, width), F32),
        ),
        grid_spec=pltpu.PrefetchScalarGridSpec(
            num_scalar_prefetch=1,
            grid=(hidden // FF_TILE,),
            in_specs=[
                fixed((toks, width)),
                fixed((toks, width)),
                fixed(routes.shape),
                fixed(router.shape),
                fixed(router_t.shape),
                pl.BlockSpec((width, FF_TILE), lambda f, m: (0, f)),
                pl.BlockSpec((1, FF_TILE), lambda f, m: (0, f)),
                pl.BlockSpec((FF_TILE, width), lambda f, m: (f, 0)),
                fixed((1, width)),
            ],
            out_specs=(
                fixed((toks, width)),
                fixed((toks, width)),
                pl.BlockSpec((toks, FF_TILE), lambda f, m: (0, f)),
                pl.BlockSpec((toks, FF_TILE), lambda f, m: (0, f)),
                fixed((toks, width)),
                fixed((experts, width)),
            ),
            scratch_shapes=[
                pltpu.VMEM((toks, width), F32),
                pltpu.VMEM((toks, width), F32),
                pltpu.VMEM((toks, experts), F32),
                pltpu.VMEM((toks, 1), F32),
            ],
        ),
        compiler_params=params(),
        cost_estimate=cost(8 * toks * width * hidden, 20 * 2**20),
        name="expert_block",
    )(me, rows, up, routes, router, router_t, w_in, b_in, w_out, b_out)


def expert_out_grads(activs, geouts):
    count = len(activs)
    toks, hidden = activs[0].shape
    width = geouts[0].shape[1]
    return pl.pallas_call(
        functools.partial(expert_weights_kernel, count),
        out_shape=jax.ShapeDtypeStruct((width, hidden), BF16),
        grid=(hidden // width,),
        in_specs=[pl.BlockSpec((toks, width), lambda f: (0, f))] * count
        + [pl.BlockSpec((toks, width), lambda f: (0, 0))] * count,
        out_specs=pl.BlockSpec((width, width), lambda f: (0, f)),
        compiler_params=params(),
        cost_estimate=cost(2 * count * toks * width * hidden, 20 * 2**20),
        name="expert_out_grads",
    )(*activs, *geouts)


def expert_in_grads(rows, gpres, geouts, grad_rows):
    count = len(rows)
    toks, hidden = gpres[0].shape
    width = rows[0].shape[1]
    return pl.pallas_call(
        functools.partial(expert_in_grads_kernel, count),
        out_shape=jax.ShapeDtypeStruct((grad_rows, hidden), BF16),
        grid=(hidden // width,),
        in_specs=[pl.BlockSpec((toks, width), lambda f: (0, 0))] * count
        + [pl.BlockSpec((toks, width), lambda f: (0, f))] * count
        + [pl.BlockSpec((toks, width), lambda f: (0, 0))] * count,
        out_specs=pl.BlockSpec((grad_rows, width), lambda f: (0, f)),
        compiler_params=params(),
        cost_estimate=cost(2 * count * toks * width * hidden, 20 * 2**20),
        name="expert_in_grads",
    )(*rows, *gpres, *geouts)


def shift(values, axis, by):
    size = lax.axis_size(axis)
    return lax.ppermute(values, axis, [(i, (i + by) % size) for i in range(size)])


def ring_gather(values, axis):
    size = lax.axis_size(axis)
    found = {0: values}
    ahead = behind = values
    for k in range(1, (size + 1) // 2):
        ahead, behind = shift(ahead, axis, 1), shift(behind, axis, -1)
        found[k], found[size - k] = ahead, behind
    if size % 2 == 0:
        cut = middle_cut(values.shape[0])
        found[size // 2] = jnp.concatenate(
            [shift(ahead[:cut], axis, 1), shift(behind[cut:], axis, -1)], axis=0
        )
    return [found[k] for k in range(size)]


def middle_cut(rows):
    return rows // 16 * 8


def ring_return(values, axis):
    size = lax.axis_size(axis)
    back = [values[0]]
    for k in range(1, size):
        if 2 * k != size:
            back.append(shift(values[k], axis, -k))
            continue
        cut = middle_cut(values[k].shape[0])
        low, high = values[k][:cut], values[k][cut:]
        for _ in range(k):
            low, high = shift(low, axis, -1), shift(high, axis, 1)
        back.append(jnp.concatenate([low, high], axis=0))
    return back


def swap(values, axis, bit):
    return lax.ppermute(values, axis, [(i, i ^ bit) for i in range(lax.axis_size(axis))])


def half_of(values, dim, which):
    size = values.shape[dim] // 2
    return lax.dynamic_slice_in_dim(values, which * size, size, dim)


def halve(values, axis, bit, dim):
    mine = (lax.axis_index(axis) // bit) % 2
    got = swap(half_of(values, dim, 1 - mine), axis, bit)
    return (half_of(values, dim, mine).astype(F32) + got.astype(F32)).astype(values.dtype)


def unhalve(values, axis, bit, dim):
    mine = (lax.axis_index(axis) // bit) % 2
    got = swap(values, axis, bit)
    return jnp.where(
        mine == 0,
        jnp.concatenate([values, got], axis=dim),
        jnp.concatenate([got, values], axis=dim),
    )


def sum_over(values, axis, inner=None):
    size = lax.axis_size(axis)
    bits = [1 << b for b in range(size.bit_length() - 1)]
    first, rest = bits[:1], bits[1:]
    for bit in first:
        values = halve(values, axis, bit, 0)
    cut = values.shape[1] // 2
    parts = []
    for piece, order in ((values[:, :cut], rest), (values[:, cut:], rest[::-1])):
        for bit in order:
            piece = halve(piece, axis, bit, 1)
        parts.append(piece)
    if inner is not None:
        joined = inner(jnp.concatenate(parts, axis=1))
        width = parts[0].shape[1]
        parts = [joined[:, :width], joined[:, width:]]
    done = []
    for piece, order in zip(parts, (rest, rest[::-1])):
        for bit in order[::-1]:
            piece = unhalve(piece, axis, bit, 1)
        done.append(piece)
    values = jnp.concatenate(done, axis=1)
    for bit in first:
        values = unhalve(values, axis, bit, 0)
    return values


def sum_direct(values, axis):
    size = lax.axis_size(axis)
    me = lax.axis_index(axis)
    share = values.shape[0] // size
    take = lambda owner: lax.dynamic_slice_in_dim(values, (owner % size) * share, share, 0)
    total = take(me).astype(F32)
    for k in range(1, size):
        total = total + shift(take(me + k), axis, k).astype(F32)
    total = total.astype(values.dtype)
    result = jnp.zeros_like(values)
    result = lax.dynamic_update_slice_in_dim(result, total, me * share, 0)
    for k in range(1, size):
        result = lax.dynamic_update_slice_in_dim(
            result, shift(total, axis, k), ((me - k) % size) * share, 0
        )
    return result


def sum_small(values):
    for bit in [1 << b for b in range(lax.axis_size("rep").bit_length() - 1)]:
        values = values + swap(values, "rep", bit)
    return sum([shift(values, "exp", k) for k in range(1, lax.axis_size("exp"))], values)


def on_device(
    inputs,
    routes,
    ln1_gain,
    ln1_bias,
    w_qkv,
    query_bias,
    value_bias,
    w_out,
    out_bias,
    ln2_gain,
    ln2_bias,
    router,
    experts_in,
    experts_in_bias,
    experts_out,
    experts_out_bias,
    cotangent,
):
    width = inputs.shape[1]
    hidden_units = experts_in.shape[2]
    me = lax.axis_index("exp").astype(jnp.int32).reshape(1)
    row = lambda vec: vec.reshape(1, -1)
    g1, b1, g2, b2 = row(ln1_gain), row(ln1_bias), row(ln2_gain), row(ln2_bias)

    ups = ring_gather(cotangent, "exp")
    routes_all = ring_gather_small(routes, "exp")
    qkv, ctx, hidden, mixed = attend(
        inputs, g1, b1, w_qkv, row(query_bias), row(value_bias), w_out, row(out_bias), g2, b2
    )
    mixes = ring_gather(mixed, "exp")

    router_t = router.T.astype(F32)
    w_in, w_mid = experts_in[0], experts_out[0]
    blocks = [
        expert_block(
            me, mixes[k], ups[k], routes_all[k], router, router_t, w_in, experts_in_bias, w_mid, experts_out_bias
        )
        for k in range(len(mixes))
    ]
    parts, backs, activs, gpres, geouts, grouters = zip(*blocks)
    backs = ring_return(backs, "exp")
    parts = ring_return(parts, "exp")
    gmix = sum(b.astype(F32) for b in backs)
    result = (hidden + sum(p.astype(F32) for p in parts)).astype(BF16)
    grouter = sum_small(sum(grouters))

    out_grads = expert_out_grads(activs, geouts)
    in_grads = expert_in_grads(mixes, gpres, geouts, width + 16)
    out_sum = sum_over(out_grads, "rep").astype(F32)
    in_sum = sum_over(in_grads, "rep").astype(F32)
    blocks_down = hidden_units // width
    grad_experts_out = jnp.concatenate(
        [out_sum[:, j * width : (j + 1) * width] for j in range(blocks_down)], axis=0
    )[None]

    grad_inputs, dense, small = attend_back(
        gmix, cotangent, inputs, hidden, qkv, ctx, g1, b1, w_qkv, w_out, g2
    )
    dense = sum_over(dense, "rep", functools.partial(sum_direct, axis="exp")).astype(F32)
    small = sum_small(small)
    return (
        result,
        grad_inputs,
        small[0],
        small[1],
        dense[:, : 3 * width],
        small[2],
        small[3],
        dense[:, 3 * width :],
        small[4],
        small[5],
        small[6],
        grouter.T,
        in_sum[None, :width],
        in_sum[width : width + 1],
        grad_experts_out,
        in_sum[width + 1 : width + 2, :width],
    )


def ring_gather_small(values, axis):
    return [values] + [shift(values, axis, k) for k in range(1, lax.axis_size(axis))]


def solution(mesh):
    tokens = P(("rep", "exp"), None)
    expert3, expert2 = P("exp", None, None), P("exp", None)
    return jax.shard_map(
        on_device,
        mesh=mesh,
        in_specs=(tokens, tokens) + (P(),) * 10 + (expert3, expert2) * 2 + (tokens,),
        out_specs=(tokens, tokens) + (P(),) * 10 + (expert3, expert2) * 2,
        check_vma=False,
    )
```

```python
import functools

import jax
import jax.numpy as jnp
from jax import lax
from jax.experimental import pallas as pl
from jax.experimental.pallas import tpu as pltpu
from jax.sharding import PartitionSpec as P

HEADS = 12
HEAD_DIM = 64
SEQ = 197
NORM_EPS = 1e-06
F32 = jnp.float32
BF16 = jnp.bfloat16
LANES = 128
PAIR = LANES // HEAD_DIM
SEQ_PAD = 208
FF_TILE = 512
ROUTE_ROWS = 16
VMEM_BYTES = 58 * 2**20
COST_FLOPS = 4e8
FINAL_COST = 4
BACK_COST = 28
TAIL_SCALE = 0.305
TAIL_COEFS = (
    0.1216396663821839,
    0.12246803351870969,
    0.10341227166034979,
    0.12105264456174025,
    -0.03803921974174099,
    0.18578799927872533,
    -0.1530311110530253,
    0.03670976324394601,
)
INV_SQRT_2PI = 0.3989422804014327
VECS = ("g1", "b1", "qb", "vb", "ob", "g2", "b2", "none")


def dot(lhs, rhs):
    return lax.dot_general(lhs, rhs, (((1,), (0,)), ((), ())), preferred_element_type=F32)


def dot_rt(lhs, rhs):
    return lax.dot_general(lhs, rhs, (((1,), (1,)), ((), ())), preferred_element_type=F32)


def dot_lt(lhs, rhs):
    return lax.dot_general(lhs, rhs, (((0,), (0,)), ((), ())), preferred_element_type=F32)


def row_mean(values):
    return jnp.mean(values, axis=-1, keepdims=True)


def unit_norm(values):
    centred = values - row_mean(values)
    scale = lax.rsqrt(row_mean(centred * centred) + NORM_EPS)
    return centred * scale, scale


def column_sum(values):
    return jnp.sum(values, axis=0, keepdims=True)


def gelu_parts(pre):
    size = jnp.abs(pre)
    bell = jnp.exp(pre * pre * -0.5)
    frac = 1.0 / (1.0 + TAIL_SCALE * size)
    poly = jnp.full_like(pre, TAIL_COEFS[-1])
    for coef in TAIL_COEFS[-2::-1]:
        poly = poly * frac + coef
    tail = bell * (poly * frac)
    return jnp.where(pre >= 0, 1.0 - tail, tail), bell * INV_SQRT_2PI


def pair_masks(rows):
    lane = lax.broadcasted_iota(jnp.int32, (rows, LANES), 1)
    return [(lane >= h * HEAD_DIM) & (lane < (h + 1) * HEAD_DIM) for h in range(PAIR)]


def stack_heads(values, masks):
    return jnp.concatenate([jnp.where(m, values, 0.0) for m in masks], axis=0).astype(BF16)


def unstack_heads(values, masks):
    rows = values.shape[0] // PAIR
    picked = values[:rows]
    for h in range(1, PAIR):
        picked = jnp.where(masks[h], values[h * rows : (h + 1) * rows], picked)
    return picked


def probabilities(scores):
    key_id = lax.broadcasted_iota(jnp.int32, scores.shape, 1)
    scores = jnp.where(key_id < SEQ, scores, -1e30)
    weights = jnp.exp(scores - jnp.max(scores, axis=-1, keepdims=True))
    return weights * (1.0 / jnp.sum(weights, axis=-1, keepdims=True))


def attend_kernel(
    x_ref, vecs_ref, wqkv_ref, wout_ref,
    qkv_ref, ctx_ref, hidden_ref, mixed_ref,
    qkv_s, ctx_s,
):
    toks, width = x_ref.shape
    spare = qkv_s.shape[0] - toks
    x = x_ref[...].astype(F32)
    vec = lambda name: vecs_ref[VECS.index(name) : VECS.index(name) + 1, :]
    unit, _ = unit_norm(x)
    normed = (unit * vec("g1") + vec("b1")).astype(BF16)
    for part, bias in ((0, "qb"), (1, None), (2, "vb")):
        cols = pl.ds(part * width, width)
        joined = dot(normed, wqkv_ref[:, cols])
        if bias is not None:
            joined = joined + vec(bias)
        joined = joined.astype(BF16)
        qkv_ref[:, cols] = joined
        qkv_s[0:toks, cols] = joined.astype(F32)
    qkv_s[toks:, :] = jnp.zeros((spare, 3 * width), F32)
    masks = pair_masks(SEQ_PAD)
    for img in range(toks // SEQ):
        rows = pl.ds(img * SEQ, SEQ_PAD)
        for at in range(0, width, LANES):
            query = stack_heads(qkv_s[rows, at : at + LANES], masks)
            key = qkv_s[rows, width + at : width + at + LANES].astype(BF16)
            value = qkv_s[rows, 2 * width + at : 2 * width + at + LANES].astype(BF16)
            probs = probabilities(dot_rt(query, key) * HEAD_DIM**-0.5).astype(BF16)
            ctx_s[rows, at : at + LANES] = unstack_heads(dot(probs, value), masks)
    ctx = ctx_s[0:toks, :].astype(BF16)
    ctx_ref[...] = ctx
    hidden = x + dot(ctx, wout_ref[...]) + vec("ob")
    hidden_ref[...] = hidden
    unit2, _ = unit_norm(hidden)
    mixed_ref[...] = (unit2 * vec("g2") + vec("b2")).astype(BF16)


def expert_kernel(
    waits, me_ref, *refs,
):
    expert_body(me_ref, *refs[:8], *refs[8 + waits :])


def expert_body(
    me_ref,
    x_ref, up_ref, router_ref, router_t_ref, win_ref, bin_ref, wout_ref, bout_ref,
    part_ref, back_ref, activ_ref, gpre_ref, geout_ref, grouter_ref, gin_bias_ref, gout_bias_ref,
    out_s, back_s, probs_s, gate_s,
):
    step = pl.program_id(0)
    me = me_ref[0]
    toks = x_ref.shape[0]
    tail = up_ref.shape[0] - ROUTE_ROWS

    @pl.when(step == 0)
    def _():
        named = column_sum((up_ref[tail:, :].astype(F32) == me.astype(F32)).astype(F32))
        named = jnp.transpose(jnp.broadcast_to(named, (8, named.shape[1])))[:toks, 0:1]
        logits = dot(x_ref[...], router_ref[...])
        weights = jnp.exp(logits - jnp.max(logits, axis=-1, keepdims=True))
        probs = weights / jnp.sum(weights, axis=-1, keepdims=True)
        probs_s[...] = probs
        mine = lax.broadcasted_iota(jnp.int32, probs.shape, 1) == me
        gate = jnp.sum(jnp.where(mine, probs, 0.0), axis=-1, keepdims=True) * named
        gate_s[...] = gate
        geout = (gate * up_ref[0:toks, :].astype(F32)).astype(BF16)
        geout_ref[...] = geout
        gout_bias_ref[...] = column_sum(geout.astype(F32))
        out_s[...] = jnp.zeros_like(out_s)
        back_s[...] = jnp.zeros_like(back_s)

    pre = dot(x_ref[...], win_ref[...]) + bin_ref[...]
    phi, bell = gelu_parts(pre)
    activ = (pre * phi).astype(BF16)
    activ_ref[...] = activ
    gpre = (dot_rt(geout_ref[...], wout_ref[...]) * (phi + pre * bell)).astype(BF16)
    gpre_ref[...] = gpre
    gin_bias_ref[...] = column_sum(gpre.astype(F32))
    out_s[...] += dot(activ, wout_ref[...])
    back_s[...] += dot_rt(gpre, win_ref[...])

    @pl.when(step == pl.num_programs(0) - 1)
    def _():
        expert_out = (out_s[...] + bout_ref[...]).astype(BF16).astype(F32)
        gate = gate_s[...]
        probs = probs_s[...]
        part_ref[...] = (gate * expert_out).astype(BF16)
        route_grad = jnp.sum(up_ref[0:toks, :].astype(F32) * expert_out, axis=-1, keepdims=True)
        mine = (lax.broadcasted_iota(jnp.int32, probs.shape, 1) == me).astype(F32)
        glogits = gate * route_grad * (mine - probs)
        back = back_s[...].astype(BF16).astype(F32)
        for other in range(probs.shape[1]):
            back = back + glogits[:, other : other + 1] * router_t_ref[other : other + 1, :]
        back_ref[...] = back.astype(BF16)
        coarse = glogits.astype(BF16)
        fine = (glogits - coarse.astype(F32)).astype(BF16)
        grouter_ref[...] = dot_lt(coarse, x_ref[...]) + dot_lt(fine, x_ref[...])


def partial_grads_kernel(count, *refs):
    totals = [None, None]
    for k in range(count):
        rows, gpre, activ, geout = (refs[which * count + k][...] for which in range(4))
        for at, term in enumerate((dot_lt(rows, gpre), dot_lt(activ, geout))):
            totals[at] = term if totals[at] is None else totals[at] + term
    refs = refs[4 * count :]
    for at in range(2):
        refs[at][...] = totals[at]


def final_grads_kernel(count, half_ref, *refs):
    grad_ref = refs[-1]
    pieces, _, share, _ = grad_ref.shape
    grad_in, grad_out = refs[4 * count][...], refs[4 * count + 1][...]
    for k in range(count):
        rows, gpre, activ, geout = (refs[which * count + k][...] for which in range(4))
        grad_in = grad_in + dot_lt(rows, gpre)
        grad_out = grad_out + dot_lt(activ, geout)
    for piece in range(pieces):
        grad_ref[piece, 0] = grad_in[piece * share : (piece + 1) * share].astype(BF16)
        grad_ref[piece, 1] = grad_out[piece * share : (piece + 1) * share].astype(BF16)


def assemble_kernel(write, count, ids_ref, *refs):
    outs = refs[len(refs) - count :]
    at = pl.program_id(0)
    chosen = ((at // 2) ^ ids_ref[0]) * 2 + at % 2
    for which in range(4):

        @pl.when(chosen == which)
        def _(which=which):
            for piece in range(refs[which].shape[0]):
                write(refs[which][piece ^ ids_ref[1 + which % 2]].astype(F32), piece, *outs)


def write_dense(values, piece, qkv_ref, out_ref):
    share, cut = values.shape[0], qkv_ref.shape[1]
    rows = slice(piece * share, (piece + 1) * share)
    qkv_ref[rows, :] = values[:, :cut]
    out_ref[rows, :] = values[:, cut:]


def write_expert(values, piece, in_ref, out_ref):
    share, width = values.shape[1], out_ref.shape[2]
    rows = slice(piece * share, (piece + 1) * share)
    in_ref[rows, :] = values[0]
    for tile in range(out_ref.shape[0]):
        out_ref[tile, rows, :] = values[1, :, tile * width : (tile + 1) * width]


def attend_back_kernel(
    count, sums, core_ref, up_ref, x_ref, hidden_ref, qkv_ref, ctx_ref, vecs_ref, wqkv_ref, wout_ref, *refs,
):
    *refs, ginput_ref, keep_ref, send_ref, small_ref, qkv_s, gctx_s, gjoin_s = refs
    gmix_refs, refs = refs[:sums], refs[sums:]
    toks, width = x_ref.shape
    spare = qkv_s.shape[0] - toks
    vec = lambda name: vecs_ref[VECS.index(name) : VECS.index(name) + 1, :]

    def put(values, start):
        cols = slice(start, start + values.shape[1])
        pieces, share = keep_ref.shape[:2]
        for first, halves in ((0, (keep_ref, send_ref)), (1, (send_ref, keep_ref))):

            @pl.when(core_ref[0] == first)
            def _(halves=halves):
                for piece in range(2 * pieces):
                    rows = slice(piece * share, (piece + 1) * share)
                    halves[piece // pieces][piece % pieces, :, cols] = values[rows].astype(BF16)

    gmix = gmix_refs[0][...].astype(F32)
    for ref in gmix_refs[1:]:
        gmix = gmix + ref[...].astype(F32)
    unit2, scale2 = unit_norm(hidden_ref[...])
    grad_g2 = column_sum(gmix * unit2)
    grad_b2 = column_sum(gmix)
    m2 = gmix * vec("g2")
    ghidden = up_ref[...].astype(F32) + scale2 * (m2 - row_mean(m2) - unit2 * row_mean(m2 * unit2))
    gatt = ghidden.astype(BF16)
    grad_ob = column_sum(gatt.astype(F32))
    put(dot_lt(ctx_ref[...], gatt), 3 * width)
    gctx_s[0:toks, :] = dot_rt(gatt, wout_ref[...]).astype(BF16).astype(F32)
    gctx_s[toks:, :] = jnp.zeros((spare, width), F32)
    qkv_s[0:toks, :] = qkv_ref[...].astype(F32)
    qkv_s[toks:, :] = jnp.zeros((spare, 3 * width), F32)
    masks = pair_masks(SEQ_PAD)
    row_ok = lax.broadcasted_iota(jnp.int32, (SEQ_PAD, 1), 0) < SEQ
    for img in range(toks // SEQ):
        rows = pl.ds(img * SEQ, SEQ_PAD)
        for at in range(0, width, LANES):
            query = stack_heads(jnp.where(row_ok, qkv_s[rows, at : at + LANES], 0.0), masks)
            key = qkv_s[rows, width + at : width + at + LANES].astype(BF16)
            value = qkv_s[rows, 2 * width + at : 2 * width + at + LANES].astype(BF16)
            gctx = stack_heads(jnp.where(row_ok, gctx_s[rows, at : at + LANES], 0.0), masks)
            probs = probabilities(dot_rt(query, key) * HEAD_DIM**-0.5)
            gvalue = dot_lt(probs.astype(BF16), gctx)
            gweights = dot_rt(gctx, value)
            inner = jnp.sum(gweights * probs, axis=-1, keepdims=True)
            gscores = (probs * (gweights - inner)).astype(BF16)
            gquery = unstack_heads(dot(gscores, key), masks) * HEAD_DIM**-0.5
            gkey = dot_lt(gscores, query) * HEAD_DIM**-0.5
            gjoin_s[rows, at : at + LANES] = gquery
            gjoin_s[rows, width + at : width + at + LANES] = gkey
            gjoin_s[rows, 2 * width + at : 2 * width + at + LANES] = gvalue
    gjoin = gjoin_s[0:toks, :].astype(BF16)
    grad_qb = column_sum(gjoin[:, :width].astype(F32))
    grad_vb = column_sum(gjoin[:, 2 * width :].astype(F32))
    x = x_ref[...].astype(F32)
    unit1, scale1 = unit_norm(x)
    normed = (unit1 * vec("g1") + vec("b1")).astype(BF16)
    put(dot_lt(normed, gjoin), 0)
    gnormed = dot_rt(gjoin, wqkv_ref[...])
    grad_g1 = column_sum(gnormed * unit1)
    grad_b1 = column_sum(gnormed)
    m1 = gnormed * vec("g1")
    ginput = ghidden + scale1 * (m1 - row_mean(m1) - unit1 * row_mean(m1 * unit1))
    ginput_ref[...] = ginput.astype(BF16)
    for at, small in enumerate((grad_g1, grad_b1, grad_qb, grad_vb, grad_ob, grad_g2, grad_b2)):
        small_ref[at : at + 1, :] = small
    small_ref[7:, :] = jnp.zeros((small_ref.shape[0] - 7, width), F32)
    total = lambda which: sum((ref[...] for ref in refs[which:count:3][1:]), refs[which][...])
    router_sum, in_sum, out_sum = (total(which) for which in range(3))
    small_ref[8 : 8 + router_sum.shape[0], :] = router_sum
    at = 8 + -(-router_sum.shape[0] // 8) * 8
    for tile in range(in_sum.shape[1] // width):
        small_ref[at + tile : at + tile + 1, :] = in_sum[:, tile * width : (tile + 1) * width]
    at += in_sum.shape[1] // width
    small_ref[at : at + 1, :] = out_sum


def params(**more):
    return pltpu.CompilerParams(vmem_limit_bytes=VMEM_BYTES, **more)


def cost(micros):
    return pl.CostEstimate(flops=int(micros * COST_FLOPS), bytes_accessed=1024, transcendentals=0)


def whole():
    return pl.BlockSpec(memory_space=pltpu.VMEM)


def scalars():
    return pl.BlockSpec(memory_space=pltpu.SMEM)


def attend(inputs, vecs, w_qkv, w_out):
    toks, width = inputs.shape
    padded = -(-(toks - SEQ + SEQ_PAD) // 16) * 16
    return pl.pallas_call(
        attend_kernel,
        out_shape=(
            jax.ShapeDtypeStruct((toks, 3 * width), BF16),
            jax.ShapeDtypeStruct((toks, width), BF16),
            jax.ShapeDtypeStruct((toks, width), F32),
            jax.ShapeDtypeStruct((toks, width), BF16),
        ),
        in_specs=[whole()] * 4,
        out_specs=(whole(),) * 4,
        scratch_shapes=[pltpu.VMEM((padded, 3 * width), F32), pltpu.VMEM((padded, width), F32)],
        compiler_params=params(),
        cost_estimate=cost(12),
        name="attend",
    )(inputs, vecs, w_qkv, w_out)


def attend_back(core, gmixes, up, inputs, hidden, qkv, ctx, vecs, w_qkv, w_out, smalls, small_rows, pieces, after):
    toks, width = inputs.shape
    padded = -(-(toks - SEQ + SEQ_PAD) // 16) * 16
    half = jax.ShapeDtypeStruct((pieces, width // (2 * pieces), 4 * width), BF16)
    return pl.pallas_call(
        functools.partial(attend_back_kernel, len(smalls), len(gmixes)),
        out_shape=(
            jax.ShapeDtypeStruct((toks, width), BF16),
            half,
            half,
            jax.ShapeDtypeStruct((small_rows, width), F32),
        ),
        in_specs=[scalars()] + [whole()] * (8 + len(gmixes) + len(smalls)) + [pl.BlockSpec(memory_space=pl.ANY)] * len(after),
        out_specs=(whole(),) * 4,
        scratch_shapes=[
            pltpu.VMEM((padded, 3 * width), F32),
            pltpu.VMEM((padded, width), F32),
            pltpu.VMEM((padded, 3 * width), F32),
        ],
        compiler_params=params(),
        cost_estimate=cost(BACK_COST),
        name="attend_back",
    )(core, up, inputs, hidden, qkv, ctx, vecs, w_qkv, w_out, *gmixes, *smalls, *after)


def expert_block(me, rows, up, router, router_t, w_in, b_in, w_out, b_out, after=()):
    toks, width = rows.shape
    experts = router.shape[1]
    hidden = w_in.shape[1]
    fixed = lambda shape: pl.BlockSpec(shape, lambda f, m: (0, 0))
    return pl.pallas_call(
        functools.partial(expert_kernel, len(after)),
        out_shape=(
            jax.ShapeDtypeStruct((toks, width), BF16),
            jax.ShapeDtypeStruct((toks, width), BF16),
            jax.ShapeDtypeStruct((toks, hidden), BF16),
            jax.ShapeDtypeStruct((toks, hidden), BF16),
            jax.ShapeDtypeStruct((toks, width), BF16),
            jax.ShapeDtypeStruct((experts, width), F32),
            jax.ShapeDtypeStruct((1, hidden), F32),
            jax.ShapeDtypeStruct((1, width), F32),
        ),
        grid_spec=pltpu.PrefetchScalarGridSpec(
            num_scalar_prefetch=1,
            grid=(hidden // FF_TILE,),
            in_specs=[
                fixed((toks, width)),
                fixed(up.shape),
                fixed(router.shape),
                fixed(router_t.shape),
                pl.BlockSpec((width, FF_TILE), lambda f, m: (0, f)),
                pl.BlockSpec((1, FF_TILE), lambda f, m: (0, f)),
                pl.BlockSpec((FF_TILE, width), lambda f, m: (f, 0)),
                fixed((1, width)),
            ]
            + [pl.BlockSpec(memory_space=pl.ANY)] * len(after),
            out_specs=(
                fixed((toks, width)),
                fixed((toks, width)),
                pl.BlockSpec((toks, FF_TILE), lambda f, m: (0, f)),
                pl.BlockSpec((toks, FF_TILE), lambda f, m: (0, f)),
                fixed((toks, width)),
                fixed((experts, width)),
                pl.BlockSpec((1, FF_TILE), lambda f, m: (0, f)),
                fixed((1, width)),
            ),
            scratch_shapes=[
                pltpu.VMEM((toks, width), F32),
                pltpu.VMEM((toks, width), F32),
                pltpu.VMEM((toks, experts), F32),
                pltpu.VMEM((toks, 1), F32),
            ],
        ),
        compiler_params=params(),
        cost_estimate=cost(24),
        name="expert_block",
    )(me, rows, up, router, router_t, w_in, b_in, w_out, b_out, *after)


def partial_grads(rows, gpres, activs, geouts):
    count = len(rows)
    toks, width = rows[0].shape
    hidden = gpres[0].shape[1]
    fixed = pl.BlockSpec((toks, width), lambda f: (0, 0))
    tile = pl.BlockSpec((toks, width), lambda f: (0, f))
    total = pl.BlockSpec((width, width), lambda f: (0, f))
    return pl.pallas_call(
        functools.partial(partial_grads_kernel, count),
        out_shape=(jax.ShapeDtypeStruct((width, hidden), F32),) * 2,
        grid=(hidden // width,),
        in_specs=[fixed] * count + [tile] * (2 * count) + [fixed] * count,
        out_specs=(total,) * 2,
        compiler_params=params(),
        cost_estimate=cost(12 * count),
        name="partial_grads",
    )(*rows, *gpres, *activs, *geouts)


def final_grads(half, rows, gpres, activs, geouts, started, pieces, after=()):
    count = len(rows)
    toks, width = rows[0].shape
    hidden = gpres[0].shape[1]
    share = width // (2 * pieces)
    total = pl.BlockSpec((width // 2, width), lambda f, h: (h[0], f))
    return pl.pallas_call(
        functools.partial(final_grads_kernel, count),
        out_shape=jax.ShapeDtypeStruct((pieces, 2, share, hidden), BF16),
        grid_spec=pltpu.PrefetchScalarGridSpec(
            num_scalar_prefetch=1,
            grid=(hidden // width,),
            in_specs=[pl.BlockSpec((toks, width // 2), lambda f, h: (0, h[0]))] * count
            + [pl.BlockSpec((toks, width), lambda f, h: (0, f))] * count
            + [pl.BlockSpec((toks, width // 2), lambda f, h: (0, 2 * f + h[0]))] * count
            + [pl.BlockSpec((toks, width), lambda f, h: (0, 0))] * count
            + [total] * 2
            + [pl.BlockSpec(memory_space=pl.ANY)] * len(after),
            out_specs=pl.BlockSpec((pieces, 2, share, width), lambda f, h: (0, 0, 0, f)),
        ),
        compiler_params=params(),
        cost_estimate=cost(FINAL_COST),
        name="final_grads",
    )(half, *rows, *gpres, *activs, *geouts, *started, *after)


def assemble(ids, groups, write, outs, after):
    blocks = []
    for shape, dim in outs:
        block = tuple(n // 4 if d == dim else n for d, n in enumerate(shape))
        place = lambda at, ids, dim=dim, rank=len(shape): tuple(at if d == dim else 0 for d in range(rank))
        blocks.append(pl.BlockSpec(block, place))
    rank = groups[0].ndim
    return pl.pallas_call(
        functools.partial(assemble_kernel, write, len(outs)),
        out_shape=tuple(jax.ShapeDtypeStruct(shape, F32) for shape, _ in outs),
        grid_spec=pltpu.PrefetchScalarGridSpec(
            num_scalar_prefetch=1,
            grid=(4,),
            in_specs=[pl.BlockSpec(groups[0].shape, lambda at, ids: (0,) * rank)] * 4
            + [pl.BlockSpec(memory_space=pl.ANY)] * len(after),
            out_specs=tuple(blocks),
        ),
        compiler_params=params(),
        cost_estimate=cost(5),
        name="assemble",
    )(ids, *groups, *after)


def shift(values, axis, by):
    size = lax.axis_size(axis)
    return lax.ppermute(values, axis, [(i, (i + by) % size) for i in range(size)])


INNER_SWAP = [(1, 2), (2, 1)]
OUTWARD = [(1, 0), (2, 3)]


def at_end(axis):
    place = lax.axis_index(axis)
    return (place == 0) | (place == lax.axis_size(axis) - 1)


def gather_blocks(values, axis, hold=None):
    if lax.axis_size(axis) != 4:
        return ring_gather(values, axis), ()
    near = swap(values, axis, 1)
    inner = lax.ppermute(values, axis, INNER_SWAP)
    if hold is not None:
        near, inner = hold(near, inner)
    far = lax.ppermute(near, axis, INNER_SWAP)
    end = at_end(axis)
    second = jnp.where(end, lax.ppermute(inner, axis, OUTWARD), far)
    third = jnp.where(end, lax.ppermute(far, axis, OUTWARD), inner)
    return [values, near, second, third], (near, inner)


INWARD = [(0, 1), (3, 2)]


class Returns:
    def __init__(self, own, axis):
        self.axis, self.line = axis, lax.axis_size(axis) == 4
        self.sums, self.sent = [own], []

    def add(self, k, values, *hold):
        if not self.line:
            self.sums.append(shift(values, self.axis, -k))
        elif k == 1:
            self.near = values
            self.sent = [lax.ppermute(values, self.axis, INWARD)]
            self.sums += self.sent
        elif k == 2:
            if hold:
                values, *_ = lax.optimization_barrier((values, *hold))
            self.through = lax.ppermute(values, self.axis, INWARD)
            inner = lax.ppermute(values, self.axis, INNER_SWAP)
            self.sent = [self.through, inner]
            self.outward = add_rounded(self.near, inner)
        else:
            self.sums.append(swap(add_rounded(values, self.through), self.axis, 3))

    def send_outward(self, *before):
        if self.line:
            outward, *_ = lax.optimization_barrier((self.outward, *before))
            self.sums.append(lax.ppermute(outward, self.axis, OUTWARD))
            self.sent.append(self.sums[-1])


def ring_gather(values, axis):
    size = lax.axis_size(axis)
    found = {0: values}
    ahead = behind = values
    for k in range(1, (size + 1) // 2):
        ahead, behind = shift(ahead, axis, 1), shift(behind, axis, -1)
        found[k], found[size - k] = ahead, behind
    if size % 2 == 0:
        cut = middle_cut(values.shape[0])
        found[size // 2] = jnp.concatenate(
            [shift(ahead[:cut], axis, 1), shift(behind[cut:], axis, -1)], axis=0
        )
    return [found[k] for k in range(size)]


def middle_cut(rows):
    return rows // 16 * 8


def swap(values, axis, bit):
    return lax.ppermute(values, axis, [(i, i ^ bit) for i in range(lax.axis_size(axis))])


def axis_bit(axis, bit):
    return ((lax.axis_index(axis) // bit) % 2).astype(jnp.int32)


def halve(values, axis, bit):
    mine = axis_bit(axis, bit)
    size = values.shape[0] // 2
    part = lambda which: lax.dynamic_slice_in_dim(values, which * size, size, 0)
    got = swap(part(1 - mine), axis, bit)
    return add_rounded(part(mine), got)


def add_rounded(one, other):
    return (one.astype(F32) + other.astype(F32)).astype(one.dtype)


def sum_over(keep, send, axis, write, outs, inner=None, after=(), before_end=()):
    core = 1
    values = add_rounded(keep, swap(send, axis, core))
    if after:
        values, *_ = lax.optimization_barrier((values, *after))
    return values, lambda: sum_rest(values, axis, write, outs, inner, before_end)


def sum_rest(values, axis, write, outs, inner, before_end):
    size = lax.axis_size(axis)
    core, *rest = [1 << b for b in range(size.bit_length() - 1)]
    pieces = 1 << len(rest)
    orders = (rest, rest[::-1])
    parts = []
    for part, order in zip((values[:pieces], values[pieces:]), orders):
        for bit in order:
            part = halve(part, axis, bit)
        parts.append(part)
    if inner is not None:
        joined = jnp.concatenate(parts, axis=0)
        joined = inner(joined.reshape(-1, joined.shape[-1])).reshape(joined.shape)
        parts = [joined[:1], joined[1:]]
    ids = [axis_bit(axis, core)]
    done = []
    for part, order in zip(parts, orders):
        for bit in order[::-1]:
            part = jnp.concatenate([part, swap(part, axis, bit)], axis=0)
        done.append(part)
        ids.append(sum(axis_bit(axis, bit) * (pieces >> at + 1) for at, bit in enumerate(order)))
    got = [swap(part, axis, core) for part in done]
    return assemble(jnp.stack(ids), done + got, write, outs, before_end)


def sum_direct(values, axis):
    size = lax.axis_size(axis)
    me = lax.axis_index(axis)
    share = values.shape[0] // size
    take = lambda owner: lax.dynamic_slice_in_dim(values, (owner % size) * share, share, 0)
    total = take(me).astype(F32)
    for k in range(1, size):
        total = total + shift(take(me + k), axis, k).astype(F32)
    total = total.astype(values.dtype)
    result = jnp.zeros_like(values)
    result = lax.dynamic_update_slice_in_dim(result, total, me * share, 0)
    for k in range(1, size):
        result = lax.dynamic_update_slice_in_dim(
            result, shift(total, axis, k), ((me - k) % size) * share, 0
        )
    return result


def sum_small(values, local_rows):
    for bit in [1 << b for b in range(lax.axis_size("rep").bit_length() - 1)]:
        values = values + swap(values, "rep", bit)
    shared = values[: values.shape[0] - local_rows]
    shared = sum([shift(shared, "exp", k) for k in range(1, lax.axis_size("exp"))], shared)
    return shared, values[values.shape[0] - local_rows :]


def on_device(
    inputs,
    routes,
    ln1_gain,
    ln1_bias,
    w_qkv,
    query_bias,
    value_bias,
    w_out,
    out_bias,
    ln2_gain,
    ln2_bias,
    router,
    experts_in,
    experts_in_bias,
    experts_out,
    experts_out_bias,
    cotangent,
):
    toks, width = inputs.shape
    experts = router.shape[1]
    hidden_units = experts_in.shape[2]
    me = lax.axis_index("exp").astype(jnp.int32).reshape(1)
    core = axis_bit("rep", 1).reshape(1)
    vecs = jnp.stack(
        [ln1_gain, ln1_bias, query_bias, value_bias, out_bias, ln2_gain, ln2_bias, jnp.zeros_like(ln1_gain)]
    )
    tail = -(-toks // 16) * 16
    named = jnp.full((tail - toks + ROUTE_ROWS, width), -1.0, BF16)
    named = named.at[tail - toks : tail - toks + routes.shape[1], :toks].set(routes.T.astype(BF16))

    pieces = lax.axis_size("rep")
    ups, first_ups = gather_blocks(jnp.concatenate([cotangent, named], axis=0), "exp")
    qkv, ctx, hidden, mixed = attend(inputs, vecs, w_qkv, w_out)
    router_t = router.T.astype(F32)
    w_in, w_mid = experts_in[0], experts_out[0]
    run_block = lambda rows, up, after: expert_block(
        me, rows, up, router, router_t, w_in, experts_in_bias, w_mid, experts_out_bias, after
    )
    blocks, sums = [run_block(mixed, ups[0], first_ups)], None
    mixes, _ = gather_blocks(mixed, "exp", lambda *got: lax.optimization_barrier((*got, blocks[0][0]))[:2])
    last = len(mixes) - 1
    backs, parts = Returns(blocks[0][1], "exp"), Returns(blocks[0][0], "exp")
    sums, early = None, ()
    for k in range(1, last + 1):
        blocks.append(run_block(mixes[k], ups[k], early))
        hold = (mixes[last], ups[last]) if k == last - 1 else ()
        backs.add(k, blocks[k][1], *hold)
        if k < last:
            parts.add(k, blocks[k][0], *hold)
        if k == last - 2:
            listed = lambda which: [mixes[j] if which is None else blocks[j][which] for j in range(k + 1)]
            sums = partial_grads(listed(None), listed(3), listed(2), listed(4))
            early = (sums[0], *backs.sent, *parts.sent)
        elif k == last - 1:
            backs.send_outward(mixes[last], ups[last])
            early, middle_sent = (), tuple(backs.sent + parts.sent)
    _, _, activs, gpres, geouts, grouters, gin_bias, gout_bias = zip(*blocks)
    final = lambda half, after: final_grads(
        half, mixes[-2:], gpres[-2:], activs[-2:], geouts[-2:], sums, pieces, after
    )
    send = final(1 - core, middle_sent)
    keep = final(core, (send,))
    parts.add(last, lax.optimization_barrier((blocks[last][0], keep))[0])
    parts.send_outward(keep)
    result = sum((values.astype(F32) for values in parts.sums), hidden).astype(BF16)
    core_sum, expert_rest = sum_over(
        keep,
        send,
        "rep",
        write_expert,
        (((width, hidden_units), 0), ((hidden_units // width, width, width), 1)),
    )

    smalls = [part for trio in zip(grouters, gin_bias, gout_bias) for part in trio]
    shared_rows = 8 + -(-experts // 8) * 8
    small_rows = shared_rows + -(-(hidden_units // width + 1) // 8) * 8
    grad_inputs, dense_keep, dense_send, small = attend_back(
        core, backs.sums, cotangent, inputs, hidden, qkv, ctx, vecs, w_qkv, w_out,
        smalls, small_rows, pieces, (core_sum,),
    )
    grad_experts_in, grad_experts_out = expert_rest()
    _, dense_rest = sum_over(
        dense_keep,
        dense_send,
        "rep",
        write_dense,
        (((width, 3 * width), 0), ((width, width), 0)),
        functools.partial(sum_direct, axis="exp"),
        tuple(parts.sums[1:]),
        [grad_experts_out],
    )
    grad_qkv, grad_out = dense_rest()
    small, own = sum_small(small, small_rows - shared_rows)
    return (
        result,
        grad_inputs,
        small[0],
        small[1],
        grad_qkv,
        small[2],
        small[3],
        grad_out,
        small[4],
        small[5],
        small[6],
        small[8 : 8 + experts].T,
        grad_experts_in[None],
        own[: hidden_units // width].reshape(1, hidden_units),
        grad_experts_out.reshape(1, hidden_units, width),
        own[hidden_units // width : hidden_units // width + 1],
    )


def solution(mesh):
    tokens = P(("rep", "exp"), None)
    expert3, expert2 = P("exp", None, None), P("exp", None)
    return jax.shard_map(
        on_device,
        mesh=mesh,
        in_specs=(tokens, tokens) + (P(),) * 10 + (expert3, expert2) * 2 + (tokens,),
        out_specs=(tokens, tokens) + (P(),) * 10 + (expert3, expert2) * 2,
        check_vma=False,
    )
```

```python
import functools

import jax
import jax.numpy as jnp
from jax import lax
from jax.experimental import pallas as pl
from jax.experimental.pallas import tpu as pltpu
from jax.sharding import PartitionSpec as P

HEADS = 12
HEAD_DIM = 64
SEQ = 197
NORM_EPS = 1e-06
F32 = jnp.float32
BF16 = jnp.bfloat16
LANES = 128
PAIR = LANES // HEAD_DIM
SEQ_PAD = 208
FF_TILE = 512
ROUTE_ROWS = 16
VMEM_BYTES = 58 * 2**20
COST_FLOPS = 4e8
FINAL_COST = 4
BACK_COST = 28
TAIL_SCALE = 0.305
TAIL_COEFS = (
    0.1216396663821839,
    0.12246803351870969,
    0.10341227166034979,
    0.12105264456174025,
    -0.03803921974174099,
    0.18578799927872533,
    -0.1530311110530253,
    0.03670976324394601,
)
INV_SQRT_2PI = 0.3989422804014327
VECS = ("g1", "b1", "qb", "vb", "ob", "g2", "b2", "none")


def dot(lhs, rhs):
    return lax.dot_general(lhs, rhs, (((1,), (0,)), ((), ())), preferred_element_type=F32)


def dot_rt(lhs, rhs):
    return lax.dot_general(lhs, rhs, (((1,), (1,)), ((), ())), preferred_element_type=F32)


def dot_lt(lhs, rhs):
    return lax.dot_general(lhs, rhs, (((0,), (0,)), ((), ())), preferred_element_type=F32)


def row_mean(values):
    return jnp.mean(values, axis=-1, keepdims=True)


def unit_norm(values):
    centred = values - row_mean(values)
    scale = lax.rsqrt(row_mean(centred * centred) + NORM_EPS)
    return centred * scale, scale


def column_sum(values):
    return jnp.sum(values, axis=0, keepdims=True)


def gelu_parts(pre):
    size = jnp.abs(pre)
    bell = jnp.exp(pre * pre * -0.5)
    frac = 1.0 / (1.0 + TAIL_SCALE * size)
    poly = jnp.full_like(pre, TAIL_COEFS[-1])
    for coef in TAIL_COEFS[-2::-1]:
        poly = poly * frac + coef
    tail = bell * (poly * frac)
    return jnp.where(pre >= 0, 1.0 - tail, tail), bell * INV_SQRT_2PI


def pair_masks(rows):
    lane = lax.broadcasted_iota(jnp.int32, (rows, LANES), 1)
    return [(lane >= h * HEAD_DIM) & (lane < (h + 1) * HEAD_DIM) for h in range(PAIR)]


def stack_heads(values, masks):
    return jnp.concatenate([jnp.where(m, values, 0.0) for m in masks], axis=0).astype(BF16)


def unstack_heads(values, masks):
    rows = values.shape[0] // PAIR
    picked = values[:rows]
    for h in range(1, PAIR):
        picked = jnp.where(masks[h], values[h * rows : (h + 1) * rows], picked)
    return picked


def probabilities(scores):
    key_id = lax.broadcasted_iota(jnp.int32, scores.shape, 1)
    scores = jnp.where(key_id < SEQ, scores, -1e30)
    weights = jnp.exp(scores - jnp.max(scores, axis=-1, keepdims=True))
    return weights * (1.0 / jnp.sum(weights, axis=-1, keepdims=True))


def attend_kernel(
    x_ref, vecs_ref, wqkv_ref, wout_ref,
    qkv_ref, ctx_ref, hidden_ref, mixed_ref,
    qkv_s, ctx_s,
):
    toks, width = x_ref.shape
    spare = qkv_s.shape[0] - toks
    x = x_ref[...].astype(F32)
    vec = lambda name: vecs_ref[VECS.index(name) : VECS.index(name) + 1, :]
    unit, _ = unit_norm(x)
    normed = (unit * vec("g1") + vec("b1")).astype(BF16)
    for part, bias in ((0, "qb"), (1, None), (2, "vb")):
        cols = pl.ds(part * width, width)
        joined = dot(normed, wqkv_ref[:, cols])
        if bias is not None:
            joined = joined + vec(bias)
        joined = joined.astype(BF16)
        qkv_ref[:, cols] = joined
        qkv_s[0:toks, cols] = joined.astype(F32)
    qkv_s[toks:, :] = jnp.zeros((spare, 3 * width), F32)
    masks = pair_masks(SEQ_PAD)
    for img in range(toks // SEQ):
        rows = pl.ds(img * SEQ, SEQ_PAD)
        for at in range(0, width, LANES):
            query = stack_heads(qkv_s[rows, at : at + LANES], masks)
            key = qkv_s[rows, width + at : width + at + LANES].astype(BF16)
            value = qkv_s[rows, 2 * width + at : 2 * width + at + LANES].astype(BF16)
            probs = probabilities(dot_rt(query, key) * HEAD_DIM**-0.5).astype(BF16)
            ctx_s[rows, at : at + LANES] = unstack_heads(dot(probs, value), masks)
    ctx = ctx_s[0:toks, :].astype(BF16)
    ctx_ref[...] = ctx
    hidden = x + dot(ctx, wout_ref[...]) + vec("ob")
    hidden_ref[...] = hidden
    unit2, _ = unit_norm(hidden)
    mixed_ref[...] = (unit2 * vec("g2") + vec("b2")).astype(BF16)


def expert_kernel(
    waits, me_ref, *refs,
):
    expert_body(me_ref, *refs[:8], *refs[8 + waits :])


def expert_body(
    me_ref,
    x_ref, up_ref, router_ref, router_t_ref, win_ref, bin_ref, wout_ref, bout_ref,
    part_ref, back_ref, activ_ref, gpre_ref, geout_ref, grouter_ref, gin_bias_ref, gout_bias_ref,
    out_s, back_s, probs_s, gate_s,
):
    step = pl.program_id(0)
    me = me_ref[0]
    toks = x_ref.shape[0]
    tail = up_ref.shape[0] - ROUTE_ROWS

    @pl.when(step == 0)
    def _():
        named = column_sum((up_ref[tail:, :].astype(F32) == me.astype(F32)).astype(F32))
        named = jnp.transpose(jnp.broadcast_to(named, (8, named.shape[1])))[:toks, 0:1]
        logits = dot(x_ref[...], router_ref[...])
        weights = jnp.exp(logits - jnp.max(logits, axis=-1, keepdims=True))
        probs = weights / jnp.sum(weights, axis=-1, keepdims=True)
        probs_s[...] = probs
        mine = lax.broadcasted_iota(jnp.int32, probs.shape, 1) == me
        gate = jnp.sum(jnp.where(mine, probs, 0.0), axis=-1, keepdims=True) * named
        gate_s[...] = gate
        geout = (gate * up_ref[0:toks, :].astype(F32)).astype(BF16)
        geout_ref[...] = geout
        gout_bias_ref[...] = column_sum(geout.astype(F32))
        out_s[...] = jnp.zeros_like(out_s)
        back_s[...] = jnp.zeros_like(back_s)

    pre = dot(x_ref[...], win_ref[...]) + bin_ref[...]
    phi, bell = gelu_parts(pre)
    activ = (pre * phi).astype(BF16)
    activ_ref[...] = activ
    gpre = (dot_rt(geout_ref[...], wout_ref[...]) * (phi + pre * bell)).astype(BF16)
    gpre_ref[...] = gpre
    gin_bias_ref[...] = column_sum(gpre.astype(F32))
    out_s[...] += dot(activ, wout_ref[...])
    back_s[...] += dot_rt(gpre, win_ref[...])

    @pl.when(step == pl.num_programs(0) - 1)
    def _():
        expert_out = (out_s[...] + bout_ref[...]).astype(BF16).astype(F32)
        gate = gate_s[...]
        probs = probs_s[...]
        part_ref[...] = (gate * expert_out).astype(BF16)
        route_grad = jnp.sum(up_ref[0:toks, :].astype(F32) * expert_out, axis=-1, keepdims=True)
        mine = (lax.broadcasted_iota(jnp.int32, probs.shape, 1) == me).astype(F32)
        glogits = gate * route_grad * (mine - probs)
        back = back_s[...].astype(BF16).astype(F32)
        for other in range(probs.shape[1]):
            back = back + glogits[:, other : other + 1] * router_t_ref[other : other + 1, :]
        back_ref[...] = back.astype(BF16)
        coarse = glogits.astype(BF16)
        fine = (glogits - coarse.astype(F32)).astype(BF16)
        grouter_ref[...] = dot_lt(coarse, x_ref[...]) + dot_lt(fine, x_ref[...])


def partial_grads_kernel(count, *refs):
    totals = [None, None]
    for k in range(count):
        rows, gpre, activ, geout = (refs[which * count + k][...] for which in range(4))
        for at, term in enumerate((dot_lt(rows, gpre), dot_lt(activ, geout))):
            totals[at] = term if totals[at] is None else totals[at] + term
    refs = refs[4 * count :]
    for at in range(2):
        refs[at][...] = totals[at]


def final_grads_kernel(count, half_ref, *refs):
    grad_ref = refs[-1]
    pieces, _, share, _ = grad_ref.shape
    grad_in, grad_out = refs[4 * count][...], refs[4 * count + 1][...]
    for k in range(count):
        rows, gpre, activ, geout = (refs[which * count + k][...] for which in range(4))
        grad_in = grad_in + dot_lt(rows, gpre)
        grad_out = grad_out + dot_lt(activ, geout)
    for piece in range(pieces):
        grad_ref[piece, 0] = grad_in[piece * share : (piece + 1) * share].astype(BF16)
        grad_ref[piece, 1] = grad_out[piece * share : (piece + 1) * share].astype(BF16)


def assemble_kernel(write, ids_ref, *refs):
    outs = refs[4:]
    at = pl.program_id(0)
    chosen = ((at // 2) ^ ids_ref[0]) * 2 + at % 2
    for which in range(4):

        @pl.when(chosen == which)
        def _(which=which):
            for piece in range(refs[which].shape[0]):
                write(refs[which][piece ^ ids_ref[1 + which % 2]].astype(F32), piece, *outs)


def write_dense(values, piece, qkv_ref, out_ref):
    share, cut = values.shape[0], qkv_ref.shape[1]
    rows = slice(piece * share, (piece + 1) * share)
    qkv_ref[rows, :] = values[:, :cut]
    out_ref[rows, :] = values[:, cut:]


def write_expert(values, piece, in_ref, out_ref):
    share, width = values.shape[1], out_ref.shape[2]
    rows = slice(piece * share, (piece + 1) * share)
    in_ref[rows, :] = values[0]
    for tile in range(out_ref.shape[0]):
        out_ref[tile, rows, :] = values[1, :, tile * width : (tile + 1) * width]


def attend_back_kernel(
    count, sums, core_ref, up_ref, x_ref, hidden_ref, qkv_ref, ctx_ref, vecs_ref, wqkv_ref, wout_ref, *refs,
):
    *refs, ginput_ref, keep_ref, send_ref, small_ref, qkv_s, gctx_s, gjoin_s = refs
    gmix_refs, refs = refs[:sums], refs[sums:]
    toks, width = x_ref.shape
    spare = qkv_s.shape[0] - toks
    vec = lambda name: vecs_ref[VECS.index(name) : VECS.index(name) + 1, :]

    def put(values, start):
        cols = slice(start, start + values.shape[1])
        pieces, share = keep_ref.shape[:2]
        for first, halves in ((0, (keep_ref, send_ref)), (1, (send_ref, keep_ref))):

            @pl.when(core_ref[0] == first)
            def _(halves=halves):
                for piece in range(2 * pieces):
                    rows = slice(piece * share, (piece + 1) * share)
                    halves[piece // pieces][piece % pieces, :, cols] = values[rows].astype(BF16)

    gmix = gmix_refs[0][...].astype(F32)
    for ref in gmix_refs[1:]:
        gmix = gmix + ref[...].astype(F32)
    unit2, scale2 = unit_norm(hidden_ref[...])
    grad_g2 = column_sum(gmix * unit2)
    grad_b2 = column_sum(gmix)
    m2 = gmix * vec("g2")
    ghidden = up_ref[...].astype(F32) + scale2 * (m2 - row_mean(m2) - unit2 * row_mean(m2 * unit2))
    gatt = ghidden.astype(BF16)
    grad_ob = column_sum(gatt.astype(F32))
    put(dot_lt(ctx_ref[...], gatt), 3 * width)
    gctx_s[0:toks, :] = dot_rt(gatt, wout_ref[...]).astype(BF16).astype(F32)
    gctx_s[toks:, :] = jnp.zeros((spare, width), F32)
    qkv_s[0:toks, :] = qkv_ref[...].astype(F32)
    qkv_s[toks:, :] = jnp.zeros((spare, 3 * width), F32)
    masks = pair_masks(SEQ_PAD)
    row_ok = lax.broadcasted_iota(jnp.int32, (SEQ_PAD, 1), 0) < SEQ
    for img in range(toks // SEQ):
        rows = pl.ds(img * SEQ, SEQ_PAD)
        for at in range(0, width, LANES):
            query = stack_heads(jnp.where(row_ok, qkv_s[rows, at : at + LANES], 0.0), masks)
            key = qkv_s[rows, width + at : width + at + LANES].astype(BF16)
            value = qkv_s[rows, 2 * width + at : 2 * width + at + LANES].astype(BF16)
            gctx = stack_heads(jnp.where(row_ok, gctx_s[rows, at : at + LANES], 0.0), masks)
            probs = probabilities(dot_rt(query, key) * HEAD_DIM**-0.5)
            gvalue = dot_lt(probs.astype(BF16), gctx)
            gweights = dot_rt(gctx, value)
            inner = jnp.sum(gweights * probs, axis=-1, keepdims=True)
            gscores = (probs * (gweights - inner)).astype(BF16)
            gquery = unstack_heads(dot(gscores, key), masks) * HEAD_DIM**-0.5
            gkey = dot_lt(gscores, query) * HEAD_DIM**-0.5
            gjoin_s[rows, at : at + LANES] = gquery
            gjoin_s[rows, width + at : width + at + LANES] = gkey
            gjoin_s[rows, 2 * width + at : 2 * width + at + LANES] = gvalue
    gjoin = gjoin_s[0:toks, :].astype(BF16)
    grad_qb = column_sum(gjoin[:, :width].astype(F32))
    grad_vb = column_sum(gjoin[:, 2 * width :].astype(F32))
    x = x_ref[...].astype(F32)
    unit1, scale1 = unit_norm(x)
    normed = (unit1 * vec("g1") + vec("b1")).astype(BF16)
    put(dot_lt(normed, gjoin), 0)
    gnormed = dot_rt(gjoin, wqkv_ref[...])
    grad_g1 = column_sum(gnormed * unit1)
    grad_b1 = column_sum(gnormed)
    m1 = gnormed * vec("g1")
    ginput = ghidden + scale1 * (m1 - row_mean(m1) - unit1 * row_mean(m1 * unit1))
    ginput_ref[...] = ginput.astype(BF16)
    for at, small in enumerate((grad_g1, grad_b1, grad_qb, grad_vb, grad_ob, grad_g2, grad_b2)):
        small_ref[at : at + 1, :] = small
    small_ref[7:, :] = jnp.zeros((small_ref.shape[0] - 7, width), F32)
    total = lambda which: sum((ref[...] for ref in refs[which:count:3][1:]), refs[which][...])
    router_sum, in_sum, out_sum = (total(which) for which in range(3))
    small_ref[8 : 8 + router_sum.shape[0], :] = router_sum
    at = 8 + -(-router_sum.shape[0] // 8) * 8
    for tile in range(in_sum.shape[1] // width):
        small_ref[at + tile : at + tile + 1, :] = in_sum[:, tile * width : (tile + 1) * width]
    at += in_sum.shape[1] // width
    small_ref[at : at + 1, :] = out_sum


def params(**more):
    return pltpu.CompilerParams(vmem_limit_bytes=VMEM_BYTES, **more)


def cost(micros):
    return pl.CostEstimate(flops=int(micros * COST_FLOPS), bytes_accessed=1024, transcendentals=0)


def whole():
    return pl.BlockSpec(memory_space=pltpu.VMEM)


def scalars():
    return pl.BlockSpec(memory_space=pltpu.SMEM)


def attend(inputs, vecs, w_qkv, w_out):
    toks, width = inputs.shape
    padded = -(-(toks - SEQ + SEQ_PAD) // 16) * 16
    return pl.pallas_call(
        attend_kernel,
        out_shape=(
            jax.ShapeDtypeStruct((toks, 3 * width), BF16),
            jax.ShapeDtypeStruct((toks, width), BF16),
            jax.ShapeDtypeStruct((toks, width), F32),
            jax.ShapeDtypeStruct((toks, width), BF16),
        ),
        in_specs=[whole()] * 4,
        out_specs=(whole(),) * 4,
        scratch_shapes=[pltpu.VMEM((padded, 3 * width), F32), pltpu.VMEM((padded, width), F32)],
        compiler_params=params(),
        cost_estimate=cost(12),
        name="attend",
    )(inputs, vecs, w_qkv, w_out)


def attend_back(core, gmixes, up, inputs, hidden, qkv, ctx, vecs, w_qkv, w_out, smalls, small_rows, pieces, after):
    toks, width = inputs.shape
    padded = -(-(toks - SEQ + SEQ_PAD) // 16) * 16
    half = jax.ShapeDtypeStruct((pieces, width // (2 * pieces), 4 * width), BF16)
    return pl.pallas_call(
        functools.partial(attend_back_kernel, len(smalls), len(gmixes)),
        out_shape=(
            jax.ShapeDtypeStruct((toks, width), BF16),
            half,
            half,
            jax.ShapeDtypeStruct((small_rows, width), F32),
        ),
        in_specs=[scalars()] + [whole()] * (8 + len(gmixes) + len(smalls)) + [pl.BlockSpec(memory_space=pl.ANY)] * len(after),
        out_specs=(whole(),) * 4,
        scratch_shapes=[
            pltpu.VMEM((padded, 3 * width), F32),
            pltpu.VMEM((padded, width), F32),
            pltpu.VMEM((padded, 3 * width), F32),
        ],
        compiler_params=params(),
        cost_estimate=cost(BACK_COST),
        name="attend_back",
    )(core, up, inputs, hidden, qkv, ctx, vecs, w_qkv, w_out, *gmixes, *smalls, *after)


def expert_block(me, rows, up, router, router_t, w_in, b_in, w_out, b_out, after=()):
    toks, width = rows.shape
    experts = router.shape[1]
    hidden = w_in.shape[1]
    fixed = lambda shape: pl.BlockSpec(shape, lambda f, m: (0, 0))
    return pl.pallas_call(
        functools.partial(expert_kernel, len(after)),
        out_shape=(
            jax.ShapeDtypeStruct((toks, width), BF16),
            jax.ShapeDtypeStruct((toks, width), BF16),
            jax.ShapeDtypeStruct((toks, hidden), BF16),
            jax.ShapeDtypeStruct((toks, hidden), BF16),
            jax.ShapeDtypeStruct((toks, width), BF16),
            jax.ShapeDtypeStruct((experts, width), F32),
            jax.ShapeDtypeStruct((1, hidden), F32),
            jax.ShapeDtypeStruct((1, width), F32),
        ),
        grid_spec=pltpu.PrefetchScalarGridSpec(
            num_scalar_prefetch=1,
            grid=(hidden // FF_TILE,),
            in_specs=[
                fixed((toks, width)),
                fixed(up.shape),
                fixed(router.shape),
                fixed(router_t.shape),
                pl.BlockSpec((width, FF_TILE), lambda f, m: (0, f)),
                pl.BlockSpec((1, FF_TILE), lambda f, m: (0, f)),
                pl.BlockSpec((FF_TILE, width), lambda f, m: (f, 0)),
                fixed((1, width)),
            ]
            + [pl.BlockSpec(memory_space=pl.ANY)] * len(after),
            out_specs=(
                fixed((toks, width)),
                fixed((toks, width)),
                pl.BlockSpec((toks, FF_TILE), lambda f, m: (0, f)),
                pl.BlockSpec((toks, FF_TILE), lambda f, m: (0, f)),
                fixed((toks, width)),
                fixed((experts, width)),
                pl.BlockSpec((1, FF_TILE), lambda f, m: (0, f)),
                fixed((1, width)),
            ),
            scratch_shapes=[
                pltpu.VMEM((toks, width), F32),
                pltpu.VMEM((toks, width), F32),
                pltpu.VMEM((toks, experts), F32),
                pltpu.VMEM((toks, 1), F32),
            ],
        ),
        compiler_params=params(),
        cost_estimate=cost(24),
        name="expert_block",
    )(me, rows, up, router, router_t, w_in, b_in, w_out, b_out, *after)


def partial_grads(rows, gpres, activs, geouts):
    count = len(rows)
    toks, width = rows[0].shape
    hidden = gpres[0].shape[1]
    fixed = pl.BlockSpec((toks, width), lambda f: (0, 0))
    tile = pl.BlockSpec((toks, width), lambda f: (0, f))
    total = pl.BlockSpec((width, width), lambda f: (0, f))
    return pl.pallas_call(
        functools.partial(partial_grads_kernel, count),
        out_shape=(jax.ShapeDtypeStruct((width, hidden), F32),) * 2,
        grid=(hidden // width,),
        in_specs=[fixed] * count + [tile] * (2 * count) + [fixed] * count,
        out_specs=(total,) * 2,
        compiler_params=params(),
        cost_estimate=cost(12 * count),
        name="partial_grads",
    )(*rows, *gpres, *activs, *geouts)


def final_grads(half, rows, gpres, activs, geouts, started, pieces, after=()):
    count = len(rows)
    toks, width = rows[0].shape
    hidden = gpres[0].shape[1]
    share = width // (2 * pieces)
    total = pl.BlockSpec((width // 2, width), lambda f, h: (h[0], f))
    return pl.pallas_call(
        functools.partial(final_grads_kernel, count),
        out_shape=jax.ShapeDtypeStruct((pieces, 2, share, hidden), BF16),
        grid_spec=pltpu.PrefetchScalarGridSpec(
            num_scalar_prefetch=1,
            grid=(hidden // width,),
            in_specs=[pl.BlockSpec((toks, width // 2), lambda f, h: (0, h[0]))] * count
            + [pl.BlockSpec((toks, width), lambda f, h: (0, f))] * count
            + [pl.BlockSpec((toks, width // 2), lambda f, h: (0, 2 * f + h[0]))] * count
            + [pl.BlockSpec((toks, width), lambda f, h: (0, 0))] * count
            + [total] * 2
            + [pl.BlockSpec(memory_space=pl.ANY)] * len(after),
            out_specs=pl.BlockSpec((pieces, 2, share, width), lambda f, h: (0, 0, 0, f)),
        ),
        compiler_params=params(),
        cost_estimate=cost(FINAL_COST),
        name="final_grads",
    )(half, *rows, *gpres, *activs, *geouts, *started, *after)


def assemble(ids, groups, write, outs):
    blocks = []
    for shape, dim in outs:
        block = tuple(n // 4 if d == dim else n for d, n in enumerate(shape))
        place = lambda at, ids, dim=dim, rank=len(shape): tuple(at if d == dim else 0 for d in range(rank))
        blocks.append(pl.BlockSpec(block, place))
    rank = groups[0].ndim
    return pl.pallas_call(
        functools.partial(assemble_kernel, write),
        out_shape=tuple(jax.ShapeDtypeStruct(shape, F32) for shape, _ in outs),
        grid_spec=pltpu.PrefetchScalarGridSpec(
            num_scalar_prefetch=1,
            grid=(4,),
            in_specs=[pl.BlockSpec(groups[0].shape, lambda at, ids: (0,) * rank)] * 4,
            out_specs=tuple(blocks),
        ),
        compiler_params=params(),
        cost_estimate=cost(5),
        name="assemble",
    )(ids, *groups)


def shift(values, axis, by):
    size = lax.axis_size(axis)
    return lax.ppermute(values, axis, [(i, (i + by) % size) for i in range(size)])


INNER_SWAP = [(1, 2), (2, 1)]
OUTWARD = [(1, 0), (2, 3)]


def at_end(axis):
    place = lax.axis_index(axis)
    return (place == 0) | (place == lax.axis_size(axis) - 1)


def gather_blocks(values, axis, hold=None):
    if lax.axis_size(axis) != 4:
        return ring_gather(values, axis), ()
    near = swap(values, axis, 1)
    inner = lax.ppermute(values, axis, INNER_SWAP)
    if hold is not None:
        near, inner = hold(near, inner)
    far = lax.ppermute(near, axis, INNER_SWAP)
    end = at_end(axis)
    second = jnp.where(end, lax.ppermute(inner, axis, OUTWARD), far)
    third = jnp.where(end, lax.ppermute(far, axis, OUTWARD), inner)
    return [values, near, second, third], (near, inner)


INWARD = [(0, 1), (3, 2)]


class Returns:
    def __init__(self, own, axis):
        self.axis, self.line = axis, lax.axis_size(axis) == 4
        self.sums, self.sent = [own], []

    def add(self, k, values, *hold):
        if not self.line:
            self.sums.append(shift(values, self.axis, -k))
        elif k == 1:
            self.near = values
            self.sent = [lax.ppermute(values, self.axis, INWARD)]
            self.sums += self.sent
        elif k == 2:
            if hold:
                values, *_ = lax.optimization_barrier((values, *hold))
            self.through = lax.ppermute(values, self.axis, INWARD)
            inner = lax.ppermute(values, self.axis, INNER_SWAP)
            self.sent = [self.through, inner]
            self.outward = add_rounded(self.near, inner)
        else:
            self.sums.append(swap(add_rounded(values, self.through), self.axis, 3))

    def send_outward(self, *before):
        if self.line:
            outward, *_ = lax.optimization_barrier((self.outward, *before))
            self.sums.append(lax.ppermute(outward, self.axis, OUTWARD))
            self.sent.append(self.sums[-1])


def ring_gather(values, axis):
    size = lax.axis_size(axis)
    found = {0: values}
    ahead = behind = values
    for k in range(1, (size + 1) // 2):
        ahead, behind = shift(ahead, axis, 1), shift(behind, axis, -1)
        found[k], found[size - k] = ahead, behind
    if size % 2 == 0:
        cut = middle_cut(values.shape[0])
        found[size // 2] = jnp.concatenate(
            [shift(ahead[:cut], axis, 1), shift(behind[cut:], axis, -1)], axis=0
        )
    return [found[k] for k in range(size)]


def middle_cut(rows):
    return rows // 16 * 8


def swap(values, axis, bit):
    return lax.ppermute(values, axis, [(i, i ^ bit) for i in range(lax.axis_size(axis))])


def axis_bit(axis, bit):
    return ((lax.axis_index(axis) // bit) % 2).astype(jnp.int32)


def halves(values, axis, bit):
    mine = axis_bit(axis, bit)
    size = values.shape[0] // 2
    part = lambda which: lax.dynamic_slice_in_dim(values, which * size, size, 0)
    return part(mine), part(1 - mine)


def add_rounded(one, other):
    return (one.astype(F32) + other.astype(F32)).astype(one.dtype)


def together(*trees):
    return lax.optimization_barrier(trees)


class PieceSum:
    def __init__(self, core_sum, axis):
        self.axis = axis
        bits = [1 << b for b in range(1, lax.axis_size(axis).bit_length() - 1)]
        self.orders = (bits, bits[::-1])
        self.steps = len(bits)
        self.pieces = 1 << self.steps
        self.parts = (core_sum[: self.pieces], core_sum[self.pieces :])

    def down(self, step):
        done = []
        for part, order in zip(self.parts, self.orders):
            keep, give = halves(part, self.axis, order[step])
            done.append(add_rounded(keep, swap(give, self.axis, order[step])))
        self.parts = tuple(done)

    def up(self, step):
        self.parts = tuple(
            jnp.concatenate([part, swap(part, self.axis, order[::-1][step])], axis=0)
            for part, order in zip(self.parts, self.orders)
        )

    def place(self, write, outs, got):
        ids = [axis_bit(self.axis, 1)]
        for order in self.orders:
            ids.append(sum(axis_bit(self.axis, bit) * (self.pieces >> at + 1) for at, bit in enumerate(order)))
        return assemble(jnp.stack(ids), (*self.parts, *got), write, outs)


def sum_gradients(expert, dense_keep, dense_send, small, shared_rows, expert_out, dense_out, parts):
    rep, exp = "rep", "exp"
    last = expert.steps - 1
    expert.down(0)
    expert.parts, dense_send, small = together(expert.parts, dense_send, small)
    for step in range(1, last + 1):
        expert.down(step)
    dense_sum = add_rounded(dense_keep, swap(dense_send, rep, 1))
    small = small + swap(small, rep, 1)

    expert.parts, dense_sum, small = together(expert.parts, dense_sum, small)
    dense = PieceSum(dense_sum, rep)
    for step in range(last):
        expert.up(step)
        dense.down(step)
        small = small + swap(small, rep, 2 << step)
        expert.parts, dense.parts, small = together(expert.parts, dense.parts, small)
    dense.down(last)
    small = small + swap(small, rep, 2 << last)

    dense.parts, small, expert.parts, parts = together(dense.parts, small, expert.parts, parts)
    expert.up(last)
    shape = (2, -1, *dense.parts[0].shape[1:])
    joined = jnp.concatenate(dense.parts, axis=0).reshape(-1, shape[-1])
    share = share_sum(joined, exp)
    share, small = together(share, small)
    joined = share_collect(share, exp).reshape(shape)
    shared = small[:shared_rows]
    shared = sum([shift(shared, exp, k) for k in range(1, lax.axis_size(exp))], shared)
    dense.parts = (joined[0], joined[1])

    dense.parts, shared, expert.parts = together(dense.parts, shared, expert.parts)
    got = [swap(part, rep, 1) for part in expert.parts]
    for step in range(last):
        dense.up(step)
    dense.parts, got, expert.parts = together(dense.parts, got, expert.parts)
    dense.up(last)
    placed = expert.place(*expert_out, got)
    dense.parts, placed = together(dense.parts, placed)
    got = [swap(part, rep, 1) for part in dense.parts]
    return placed, dense.place(*dense_out, got), shared, small[shared_rows:], parts


def share_sum(values, axis):
    size, me = lax.axis_size(axis), lax.axis_index(axis)
    share = values.shape[0] // size
    take = lambda owner: lax.dynamic_slice_in_dim(values, (owner % size) * share, share, 0)
    total = take(me).astype(F32)
    for k in range(1, size):
        total = total + shift(take(me + k), axis, k).astype(F32)
    return total.astype(values.dtype)


def share_collect(share, axis):
    size, me = lax.axis_size(axis), lax.axis_index(axis)
    rows = share.shape[0]
    result = jnp.zeros((size * rows, share.shape[1]), share.dtype)
    result = lax.dynamic_update_slice_in_dim(result, share, me * rows, 0)
    for k in range(1, size):
        result = lax.dynamic_update_slice_in_dim(result, shift(share, axis, k), ((me - k) % size) * rows, 0)
    return result


def on_device(
    inputs,
    routes,
    ln1_gain,
    ln1_bias,
    w_qkv,
    query_bias,
    value_bias,
    w_out,
    out_bias,
    ln2_gain,
    ln2_bias,
    router,
    experts_in,
    experts_in_bias,
    experts_out,
    experts_out_bias,
    cotangent,
):
    toks, width = inputs.shape
    experts = router.shape[1]
    hidden_units = experts_in.shape[2]
    me = lax.axis_index("exp").astype(jnp.int32).reshape(1)
    core = axis_bit("rep", 1).reshape(1)
    vecs = jnp.stack(
        [ln1_gain, ln1_bias, query_bias, value_bias, out_bias, ln2_gain, ln2_bias, jnp.zeros_like(ln1_gain)]
    )
    tail = -(-toks // 16) * 16
    named = jnp.full((tail - toks + ROUTE_ROWS, width), -1.0, BF16)
    named = named.at[tail - toks : tail - toks + routes.shape[1], :toks].set(routes.T.astype(BF16))

    pieces = lax.axis_size("rep")
    ups, first_ups = gather_blocks(jnp.concatenate([cotangent, named], axis=0), "exp")
    qkv, ctx, hidden, mixed = attend(inputs, vecs, w_qkv, w_out)
    router_t = router.T.astype(F32)
    w_in, w_mid = experts_in[0], experts_out[0]
    run_block = lambda rows, up, after: expert_block(
        me, rows, up, router, router_t, w_in, experts_in_bias, w_mid, experts_out_bias, after
    )
    blocks, sums = [run_block(mixed, ups[0], first_ups)], None
    mixes, _ = gather_blocks(mixed, "exp", lambda *got: lax.optimization_barrier((*got, blocks[0][0]))[:2])
    last = len(mixes) - 1
    backs, parts = Returns(blocks[0][1], "exp"), Returns(blocks[0][0], "exp")
    sums, early = None, ()
    for k in range(1, last + 1):
        blocks.append(run_block(mixes[k], ups[k], early))
        hold = (mixes[last], ups[last]) if k == last - 1 else ()
        backs.add(k, blocks[k][1], *hold)
        if k < last:
            parts.add(k, blocks[k][0], *hold)
        if k == last - 2:
            listed = lambda which: [mixes[j] if which is None else blocks[j][which] for j in range(k + 1)]
            sums = partial_grads(listed(None), listed(3), listed(2), listed(4))
            early = (sums[0], *backs.sent, *parts.sent)
        elif k == last - 1:
            early, middle_sent = (), tuple(backs.sent + parts.sent)
    backs.send_outward(blocks[last][1])
    _, _, activs, gpres, geouts, grouters, gin_bias, gout_bias = zip(*blocks)
    final = lambda half, after: final_grads(
        half, mixes[-2:], gpres[-2:], activs[-2:], geouts[-2:], sums, pieces, after
    )
    send = final(1 - core, middle_sent)
    keep = final(core, (send,))
    core_sum = add_rounded(keep, swap(send, "rep", 1))
    expert = PieceSum(core_sum, "rep")

    smalls = [part for trio in zip(grouters, gin_bias, gout_bias) for part in trio]
    shared_rows = 8 + -(-experts // 8) * 8
    small_rows = shared_rows + -(-(hidden_units // width + 1) // 8) * 8
    grad_inputs, dense_keep, dense_send, small = attend_back(
        core, backs.sums, cotangent, inputs, hidden, qkv, ctx, vecs, w_qkv, w_out,
        smalls, small_rows, pieces, (core_sum,),
    )
    parts.add(last, together(blocks[last][0], grad_inputs)[0])
    parts.send_outward(grad_inputs)
    (grad_experts_in, grad_experts_out), (grad_qkv, grad_out), small, own, returned = sum_gradients(
        expert,
        dense_keep,
        dense_send,
        small,
        shared_rows,
        (write_expert, (((width, hidden_units), 0), ((hidden_units // width, width, width), 1))),
        (write_dense, (((width, 3 * width), 0), ((width, width), 0))),
        parts.sums,
    )
    result = sum((values.astype(F32) for values in returned), hidden).astype(BF16)
    return (
        result,
        grad_inputs,
        small[0],
        small[1],
        grad_qkv,
        small[2],
        small[3],
        grad_out,
        small[4],
        small[5],
        small[6],
        small[8 : 8 + experts].T,
        grad_experts_in[None],
        own[: hidden_units // width].reshape(1, hidden_units),
        grad_experts_out.reshape(1, hidden_units, width),
        own[hidden_units // width : hidden_units // width + 1],
    )


def solution(mesh):
    tokens = P(("rep", "exp"), None)
    expert3, expert2 = P("exp", None, None), P("exp", None)
    return jax.shard_map(
        on_device,
        mesh=mesh,
        in_specs=(tokens, tokens) + (P(),) * 10 + (expert3, expert2) * 2 + (tokens,),
        out_specs=(tokens, tokens) + (P(),) * 10 + (expert3, expert2) * 2,
        check_vma=False,
    )
```

```python
import functools

import jax
import jax.numpy as jnp
from jax import lax
from jax.experimental import pallas as pl
from jax.experimental.pallas import tpu as pltpu
from jax.sharding import PartitionSpec as P

HEADS = 12
HEAD_DIM = 64
SEQ = 197
NORM_EPS = 1e-06
F32 = jnp.float32
BF16 = jnp.bfloat16
LANES = 128
PAIR = LANES // HEAD_DIM
SEQ_PAD = 208
FF_TILE = 768
ROUTE_ROWS = 16
VMEM_BYTES = 58 * 2**20
COST_FLOPS = 4e8
OWN_COST = 24
NEAR_COST = 24
OTHER_COST = 1
PARTIAL_COST = 1
FINAL_COST = 4
BACK_COST = 28
TAIL_SCALE = 0.305
TAIL_COEFS = (
    0.1216396663821839,
    0.12246803351870969,
    0.10341227166034979,
    0.12105264456174025,
    -0.03803921974174099,
    0.18578799927872533,
    -0.1530311110530253,
    0.03670976324394601,
)
INV_SQRT_2PI = 0.3989422804014327
VECS = ("g1", "b1", "qb", "vb", "ob", "g2", "b2", "none")


def dot(lhs, rhs):
    return lax.dot_general(lhs, rhs, (((1,), (0,)), ((), ())), preferred_element_type=F32)


def dot_rt(lhs, rhs):
    return lax.dot_general(lhs, rhs, (((1,), (1,)), ((), ())), preferred_element_type=F32)


def dot_lt(lhs, rhs):
    return lax.dot_general(lhs, rhs, (((0,), (0,)), ((), ())), preferred_element_type=F32)


def row_mean(values):
    return jnp.mean(values, axis=-1, keepdims=True)


def unit_norm(values):
    centred = values - row_mean(values)
    scale = lax.rsqrt(row_mean(centred * centred) + NORM_EPS)
    return centred * scale, scale


def column_sum(values):
    return jnp.sum(values, axis=0, keepdims=True)


def gelu_parts(pre):
    size = jnp.abs(pre)
    bell = jnp.exp(pre * pre * -0.5)
    frac = 1.0 / (1.0 + TAIL_SCALE * size)
    poly = jnp.full_like(pre, TAIL_COEFS[-1])
    for coef in TAIL_COEFS[-2::-1]:
        poly = poly * frac + coef
    tail = bell * (poly * frac)
    return jnp.where(pre >= 0, 1.0 - tail, tail), bell * INV_SQRT_2PI


def pair_masks(rows):
    lane = lax.broadcasted_iota(jnp.int32, (rows, LANES), 1)
    return [(lane >= h * HEAD_DIM) & (lane < (h + 1) * HEAD_DIM) for h in range(PAIR)]


def stack_heads(values, masks):
    return jnp.concatenate([jnp.where(m, values, 0.0) for m in masks], axis=0).astype(BF16)


def unstack_heads(values, masks):
    rows = values.shape[0] // PAIR
    picked = values[:rows]
    for h in range(1, PAIR):
        picked = jnp.where(masks[h], values[h * rows : (h + 1) * rows], picked)
    return picked


def probabilities(scores):
    key_id = lax.broadcasted_iota(jnp.int32, scores.shape, 1)
    scores = jnp.where(key_id < SEQ, scores, -1e30)
    weights = jnp.exp(scores - jnp.max(scores, axis=-1, keepdims=True))
    return weights * (1.0 / jnp.sum(weights, axis=-1, keepdims=True))


def attend_kernel(
    x_ref, vecs_ref, wqkv_ref, wout_ref,
    qkv_ref, ctx_ref, hidden_ref, mixed_ref,
    qkv_s, ctx_s,
):
    toks, width = x_ref.shape
    spare = qkv_s.shape[0] - toks
    x = x_ref[...].astype(F32)
    vec = lambda name: vecs_ref[VECS.index(name) : VECS.index(name) + 1, :]
    unit, _ = unit_norm(x)
    normed = (unit * vec("g1") + vec("b1")).astype(BF16)
    for part, bias in ((0, "qb"), (1, None), (2, "vb")):
        cols = pl.ds(part * width, width)
        joined = dot(normed, wqkv_ref[:, cols])
        if bias is not None:
            joined = joined + vec(bias)
        joined = joined.astype(BF16)
        qkv_ref[:, cols] = joined
        qkv_s[0:toks, cols] = joined.astype(F32)
    qkv_s[toks:, :] = jnp.zeros((spare, 3 * width), F32)
    masks = pair_masks(SEQ_PAD)
    for img in range(toks // SEQ):
        rows = pl.ds(img * SEQ, SEQ_PAD)
        for at in range(0, width, LANES):
            query = stack_heads(qkv_s[rows, at : at + LANES], masks)
            key = qkv_s[rows, width + at : width + at + LANES].astype(BF16)
            value = qkv_s[rows, 2 * width + at : 2 * width + at + LANES].astype(BF16)
            probs = probabilities(dot_rt(query, key) * HEAD_DIM**-0.5).astype(BF16)
            ctx_s[rows, at : at + LANES] = unstack_heads(dot(probs, value), masks)
    ctx = ctx_s[0:toks, :].astype(BF16)
    ctx_ref[...] = ctx
    hidden = x + dot(ctx, wout_ref[...]) + vec("ob")
    hidden_ref[...] = hidden
    unit2, _ = unit_norm(hidden)
    mixed_ref[...] = (unit2 * vec("g2") + vec("b2")).astype(BF16)


def expert_kernel(
    waits, me_ref, *refs,
):
    expert_body(me_ref, *refs[:8], *refs[8 + waits :])


def expert_body(
    me_ref,
    x_ref, up_ref, router_ref, router_t_ref, win_ref, bin_ref, wout_ref, bout_ref,
    part_ref, back_ref, activ_ref, gpre_ref, geout_ref, grouter_ref, gin_bias_ref, gout_bias_ref,
    out_s, back_s, probs_s, gate_s,
):
    step = pl.program_id(0)
    me = me_ref[0]
    toks = x_ref.shape[0]
    tail = up_ref.shape[0] - ROUTE_ROWS

    @pl.when(step == 0)
    def _():
        named = column_sum((up_ref[tail:, :].astype(F32) == me.astype(F32)).astype(F32))
        named = jnp.transpose(jnp.broadcast_to(named, (8, named.shape[1])))[:toks, 0:1]
        logits = dot(x_ref[...], router_ref[...])
        weights = jnp.exp(logits - jnp.max(logits, axis=-1, keepdims=True))
        probs = weights / jnp.sum(weights, axis=-1, keepdims=True)
        probs_s[...] = probs
        mine = lax.broadcasted_iota(jnp.int32, probs.shape, 1) == me
        gate = jnp.sum(jnp.where(mine, probs, 0.0), axis=-1, keepdims=True) * named
        gate_s[...] = gate
        geout = (gate * up_ref[0:toks, :].astype(F32)).astype(BF16)
        geout_ref[...] = geout
        gout_bias_ref[...] = column_sum(geout.astype(F32))
        out_s[...] = jnp.zeros_like(out_s)
        back_s[...] = jnp.zeros_like(back_s)

    pre = dot(x_ref[...], win_ref[...]) + bin_ref[...]
    phi, bell = gelu_parts(pre)
    activ = (pre * phi).astype(BF16)
    activ_ref[...] = activ
    gpre = (dot_rt(geout_ref[...], wout_ref[...]) * (phi + pre * bell)).astype(BF16)
    gpre_ref[...] = gpre
    gin_bias_ref[...] = column_sum(gpre.astype(F32))
    out_s[...] += dot(activ, wout_ref[...])
    back_s[...] += dot_rt(gpre, win_ref[...])

    @pl.when(step == pl.num_programs(0) - 1)
    def _():
        expert_out = (out_s[...] + bout_ref[...]).astype(BF16).astype(F32)
        gate = gate_s[...]
        probs = probs_s[...]
        part_ref[...] = (gate * expert_out).astype(BF16)
        route_grad = jnp.sum(up_ref[0:toks, :].astype(F32) * expert_out, axis=-1, keepdims=True)
        mine = (lax.broadcasted_iota(jnp.int32, probs.shape, 1) == me).astype(F32)
        glogits = gate * route_grad * (mine - probs)
        back = back_s[...].astype(BF16).astype(F32)
        for other in range(probs.shape[1]):
            back = back + glogits[:, other : other + 1] * router_t_ref[other : other + 1, :]
        back_ref[...] = back.astype(BF16)
        coarse = glogits.astype(BF16)
        fine = (glogits - coarse.astype(F32)).astype(BF16)
        grouter_ref[...] = dot_lt(coarse, x_ref[...]) + dot_lt(fine, x_ref[...])


def partial_grads_kernel(count, *refs):
    totals = [None, None]
    for k in range(count):
        rows, gpre, activ, geout = (refs[which * count + k][...] for which in range(4))
        for at, term in enumerate((dot_lt(rows, gpre), dot_lt(activ, geout))):
            totals[at] = term if totals[at] is None else totals[at] + term
    refs = refs[4 * count :]
    for at in range(2):
        refs[at][...] = totals[at]


def final_grads_kernel(count, half_ref, *refs):
    grad_ref = refs[-1]
    pieces, _, share, _ = grad_ref.shape
    grad_in, grad_out = refs[4 * count][...], refs[4 * count + 1][...]
    for k in range(count):
        rows, gpre, activ, geout = (refs[which * count + k][...] for which in range(4))
        grad_in = grad_in + dot_lt(rows, gpre)
        grad_out = grad_out + dot_lt(activ, geout)
    for piece in range(pieces):
        grad_ref[piece, 0] = grad_in[piece * share : (piece + 1) * share].astype(BF16)
        grad_ref[piece, 1] = grad_out[piece * share : (piece + 1) * share].astype(BF16)


def assemble_kernel(write, ids_ref, *refs):
    outs = refs[4:]
    at = pl.program_id(0)
    chosen = ((at // 2) ^ ids_ref[0]) * 2 + at % 2
    for which in range(4):

        @pl.when(chosen == which)
        def _(which=which):
            for piece in range(refs[which].shape[0]):
                write(refs[which][piece ^ ids_ref[1 + which % 2]].astype(F32), piece, *outs)


def write_dense(values, piece, qkv_ref, out_ref):
    share, cut = values.shape[0], qkv_ref.shape[1]
    rows = slice(piece * share, (piece + 1) * share)
    qkv_ref[rows, :] = values[:, :cut]
    out_ref[rows, :] = values[:, cut:]


def write_expert(values, piece, in_ref, out_ref):
    share, width = values.shape[1], out_ref.shape[2]
    rows = slice(piece * share, (piece + 1) * share)
    in_ref[rows, :] = values[0]
    for tile in range(out_ref.shape[0]):
        out_ref[tile, rows, :] = values[1, :, tile * width : (tile + 1) * width]


def attend_back_kernel(
    count, sums, core_ref, up_ref, x_ref, hidden_ref, qkv_ref, ctx_ref, vecs_ref, wqkv_ref, wout_ref, *refs,
):
    *refs, ginput_ref, keep_ref, send_ref, small_ref, qkv_s, gctx_s, gjoin_s = refs
    gmix_refs, refs = refs[:sums], refs[sums:]
    toks, width = x_ref.shape
    spare = qkv_s.shape[0] - toks
    vec = lambda name: vecs_ref[VECS.index(name) : VECS.index(name) + 1, :]

    def put(values, start):
        cols = slice(start, start + values.shape[1])
        pieces, share = keep_ref.shape[:2]
        for first, halves in ((0, (keep_ref, send_ref)), (1, (send_ref, keep_ref))):

            @pl.when(core_ref[0] == first)
            def _(halves=halves):
                for piece in range(2 * pieces):
                    rows = slice(piece * share, (piece + 1) * share)
                    halves[piece // pieces][piece % pieces, :, cols] = values[rows].astype(BF16)

    gmix = gmix_refs[0][...].astype(F32)
    for ref in gmix_refs[1:]:
        gmix = gmix + ref[...].astype(F32)
    unit2, scale2 = unit_norm(hidden_ref[...])
    grad_g2 = column_sum(gmix * unit2)
    grad_b2 = column_sum(gmix)
    m2 = gmix * vec("g2")
    ghidden = up_ref[...].astype(F32) + scale2 * (m2 - row_mean(m2) - unit2 * row_mean(m2 * unit2))
    gatt = ghidden.astype(BF16)
    grad_ob = column_sum(gatt.astype(F32))
    put(dot_lt(ctx_ref[...], gatt), 3 * width)
    gctx_s[0:toks, :] = dot_rt(gatt, wout_ref[...]).astype(BF16).astype(F32)
    gctx_s[toks:, :] = jnp.zeros((spare, width), F32)
    qkv_s[0:toks, :] = qkv_ref[...].astype(F32)
    qkv_s[toks:, :] = jnp.zeros((spare, 3 * width), F32)
    masks = pair_masks(SEQ_PAD)
    row_ok = lax.broadcasted_iota(jnp.int32, (SEQ_PAD, 1), 0) < SEQ
    for img in range(toks // SEQ):
        rows = pl.ds(img * SEQ, SEQ_PAD)
        for at in range(0, width, LANES):
            query = stack_heads(jnp.where(row_ok, qkv_s[rows, at : at + LANES], 0.0), masks)
            key = qkv_s[rows, width + at : width + at + LANES].astype(BF16)
            value = qkv_s[rows, 2 * width + at : 2 * width + at + LANES].astype(BF16)
            gctx = stack_heads(jnp.where(row_ok, gctx_s[rows, at : at + LANES], 0.0), masks)
            probs = probabilities(dot_rt(query, key) * HEAD_DIM**-0.5)
            gvalue = dot_lt(probs.astype(BF16), gctx)
            gweights = dot_rt(gctx, value)
            inner = jnp.sum(gweights * probs, axis=-1, keepdims=True)
            gscores = (probs * (gweights - inner)).astype(BF16)
            gquery = unstack_heads(dot(gscores, key), masks) * HEAD_DIM**-0.5
            gkey = dot_lt(gscores, query) * HEAD_DIM**-0.5
            gjoin_s[rows, at : at + LANES] = gquery
            gjoin_s[rows, width + at : width + at + LANES] = gkey
            gjoin_s[rows, 2 * width + at : 2 * width + at + LANES] = gvalue
    gjoin = gjoin_s[0:toks, :].astype(BF16)
    grad_qb = column_sum(gjoin[:, :width].astype(F32))
    grad_vb = column_sum(gjoin[:, 2 * width :].astype(F32))
    x = x_ref[...].astype(F32)
    unit1, scale1 = unit_norm(x)
    normed = (unit1 * vec("g1") + vec("b1")).astype(BF16)
    put(dot_lt(normed, gjoin), 0)
    gnormed = dot_rt(gjoin, wqkv_ref[...])
    grad_g1 = column_sum(gnormed * unit1)
    grad_b1 = column_sum(gnormed)
    m1 = gnormed * vec("g1")
    ginput = ghidden + scale1 * (m1 - row_mean(m1) - unit1 * row_mean(m1 * unit1))
    ginput_ref[...] = ginput.astype(BF16)
    for at, small in enumerate((grad_g1, grad_b1, grad_qb, grad_vb, grad_ob, grad_g2, grad_b2)):
        small_ref[at : at + 1, :] = small
    small_ref[7:, :] = jnp.zeros((small_ref.shape[0] - 7, width), F32)
    total = lambda which: sum((ref[...] for ref in refs[which:count:3][1:]), refs[which][...])
    router_sum, in_sum, out_sum = (total(which) for which in range(3))
    small_ref[8 : 8 + router_sum.shape[0], :] = router_sum
    at = 8 + -(-router_sum.shape[0] // 8) * 8
    for tile in range(in_sum.shape[1] // width):
        small_ref[at + tile : at + tile + 1, :] = in_sum[:, tile * width : (tile + 1) * width]
    at += in_sum.shape[1] // width
    small_ref[at : at + 1, :] = out_sum


def params(**more):
    return pltpu.CompilerParams(vmem_limit_bytes=VMEM_BYTES, **more)


def cost(micros):
    return pl.CostEstimate(flops=int(micros * COST_FLOPS), bytes_accessed=1024, transcendentals=0)


def whole():
    return pl.BlockSpec(memory_space=pltpu.VMEM)


def scalars():
    return pl.BlockSpec(memory_space=pltpu.SMEM)


def attend(inputs, vecs, w_qkv, w_out):
    toks, width = inputs.shape
    padded = -(-(toks - SEQ + SEQ_PAD) // 16) * 16
    return pl.pallas_call(
        attend_kernel,
        out_shape=(
            jax.ShapeDtypeStruct((toks, 3 * width), BF16),
            jax.ShapeDtypeStruct((toks, width), BF16),
            jax.ShapeDtypeStruct((toks, width), F32),
            jax.ShapeDtypeStruct((toks, width), BF16),
        ),
        in_specs=[whole()] * 4,
        out_specs=(whole(),) * 4,
        scratch_shapes=[pltpu.VMEM((padded, 3 * width), F32), pltpu.VMEM((padded, width), F32)],
        compiler_params=params(),
        cost_estimate=cost(12),
        name="attend",
    )(inputs, vecs, w_qkv, w_out)


def attend_back(core, gmixes, up, inputs, hidden, qkv, ctx, vecs, w_qkv, w_out, smalls, small_rows, pieces, after):
    toks, width = inputs.shape
    padded = -(-(toks - SEQ + SEQ_PAD) // 16) * 16
    half = jax.ShapeDtypeStruct((pieces, width // (2 * pieces), 4 * width), BF16)
    return pl.pallas_call(
        functools.partial(attend_back_kernel, len(smalls), len(gmixes)),
        out_shape=(
            jax.ShapeDtypeStruct((toks, width), BF16),
            half,
            half,
            jax.ShapeDtypeStruct((small_rows, width), F32),
        ),
        in_specs=[scalars()] + [whole()] * (8 + len(gmixes) + len(smalls)) + [pl.BlockSpec(memory_space=pl.ANY)] * len(after),
        out_specs=(whole(),) * 4,
        scratch_shapes=[
            pltpu.VMEM((padded, 3 * width), F32),
            pltpu.VMEM((padded, width), F32),
            pltpu.VMEM((padded, 3 * width), F32),
        ],
        compiler_params=params(),
        cost_estimate=cost(BACK_COST),
        name="attend_back",
    )(core, up, inputs, hidden, qkv, ctx, vecs, w_qkv, w_out, *gmixes, *smalls, *after)


def expert_block(me, rows, up, router, router_t, w_in, b_in, w_out, b_out, after=(), micros=1):
    toks, width = rows.shape
    experts = router.shape[1]
    hidden = w_in.shape[1]
    fixed = lambda shape: pl.BlockSpec(shape, lambda f, m: (0, 0))
    return pl.pallas_call(
        functools.partial(expert_kernel, len(after)),
        out_shape=(
            jax.ShapeDtypeStruct((toks, width), BF16),
            jax.ShapeDtypeStruct((toks, width), BF16),
            jax.ShapeDtypeStruct((toks, hidden), BF16),
            jax.ShapeDtypeStruct((toks, hidden), BF16),
            jax.ShapeDtypeStruct((toks, width), BF16),
            jax.ShapeDtypeStruct((experts, width), F32),
            jax.ShapeDtypeStruct((1, hidden), F32),
            jax.ShapeDtypeStruct((1, width), F32),
        ),
        grid_spec=pltpu.PrefetchScalarGridSpec(
            num_scalar_prefetch=1,
            grid=(hidden // FF_TILE,),
            in_specs=[
                fixed((toks, width)),
                fixed(up.shape),
                fixed(router.shape),
                fixed(router_t.shape),
                pl.BlockSpec((width, FF_TILE), lambda f, m: (0, f)),
                pl.BlockSpec((1, FF_TILE), lambda f, m: (0, f)),
                pl.BlockSpec((FF_TILE, width), lambda f, m: (f, 0)),
                fixed((1, width)),
            ]
            + [pl.BlockSpec(memory_space=pl.ANY)] * len(after),
            out_specs=(
                fixed((toks, width)),
                fixed((toks, width)),
                pl.BlockSpec((toks, FF_TILE), lambda f, m: (0, f)),
                pl.BlockSpec((toks, FF_TILE), lambda f, m: (0, f)),
                fixed((toks, width)),
                fixed((experts, width)),
                pl.BlockSpec((1, FF_TILE), lambda f, m: (0, f)),
                fixed((1, width)),
            ),
            scratch_shapes=[
                pltpu.VMEM((toks, width), F32),
                pltpu.VMEM((toks, width), F32),
                pltpu.VMEM((toks, experts), F32),
                pltpu.VMEM((toks, 1), F32),
            ],
        ),
        compiler_params=params(),
        cost_estimate=cost(micros),
        name="expert_block",
    )(me, rows, up, router, router_t, w_in, b_in, w_out, b_out, *after)


def partial_grads(rows, gpres, activs, geouts):
    count = len(rows)
    toks, width = rows[0].shape
    hidden = gpres[0].shape[1]
    fixed = pl.BlockSpec((toks, width), lambda f: (0, 0))
    tile = pl.BlockSpec((toks, width), lambda f: (0, f))
    total = pl.BlockSpec((width, width), lambda f: (0, f))
    return pl.pallas_call(
        functools.partial(partial_grads_kernel, count),
        out_shape=(jax.ShapeDtypeStruct((width, hidden), F32),) * 2,
        grid=(hidden // width,),
        in_specs=[fixed] * count + [tile] * (2 * count) + [fixed] * count,
        out_specs=(total,) * 2,
        compiler_params=params(),
        cost_estimate=cost(PARTIAL_COST),
        name="partial_grads",
    )(*rows, *gpres, *activs, *geouts)


def final_grads(half, rows, gpres, activs, geouts, started, pieces, after=()):
    count = len(rows)
    toks, width = rows[0].shape
    hidden = gpres[0].shape[1]
    share = width // (2 * pieces)
    total = pl.BlockSpec((width // 2, width), lambda f, h: (h[0], f))
    return pl.pallas_call(
        functools.partial(final_grads_kernel, count),
        out_shape=jax.ShapeDtypeStruct((pieces, 2, share, hidden), BF16),
        grid_spec=pltpu.PrefetchScalarGridSpec(
            num_scalar_prefetch=1,
            grid=(hidden // width,),
            in_specs=[pl.BlockSpec((toks, width // 2), lambda f, h: (0, h[0]))] * count
            + [pl.BlockSpec((toks, width), lambda f, h: (0, f))] * count
            + [pl.BlockSpec((toks, width // 2), lambda f, h: (0, 2 * f + h[0]))] * count
            + [pl.BlockSpec((toks, width), lambda f, h: (0, 0))] * count
            + [total] * 2
            + [pl.BlockSpec(memory_space=pl.ANY)] * len(after),
            out_specs=pl.BlockSpec((pieces, 2, share, width), lambda f, h: (0, 0, 0, f)),
        ),
        compiler_params=params(),
        cost_estimate=cost(FINAL_COST),
        name="final_grads",
    )(half, *rows, *gpres, *activs, *geouts, *started, *after)


def assemble(ids, groups, write, outs):
    blocks = []
    for shape, dim in outs:
        block = tuple(n // 4 if d == dim else n for d, n in enumerate(shape))
        place = lambda at, ids, dim=dim, rank=len(shape): tuple(at if d == dim else 0 for d in range(rank))
        blocks.append(pl.BlockSpec(block, place))
    rank = groups[0].ndim
    return pl.pallas_call(
        functools.partial(assemble_kernel, write),
        out_shape=tuple(jax.ShapeDtypeStruct(shape, F32) for shape, _ in outs),
        grid_spec=pltpu.PrefetchScalarGridSpec(
            num_scalar_prefetch=1,
            grid=(4,),
            in_specs=[pl.BlockSpec(groups[0].shape, lambda at, ids: (0,) * rank)] * 4,
            out_specs=tuple(blocks),
        ),
        compiler_params=params(),
        cost_estimate=cost(5),
        name="assemble",
    )(ids, *groups)


def shift(values, axis, by):
    size = lax.axis_size(axis)
    return lax.ppermute(values, axis, [(i, (i + by) % size) for i in range(size)])


INNER_SWAP = [(1, 2), (2, 1)]
OUTWARD = [(1, 0), (2, 3)]


def at_end(axis):
    place = lax.axis_index(axis)
    return (place == 0) | (place == lax.axis_size(axis) - 1)


class LineGather:
    def __init__(self, values, axis):
        self.axis, self.own = axis, values
        self.near = swap(values, axis, 1)
        self.inner = lax.ppermute(values, axis, INNER_SWAP)

    def pass_on(self, *before):
        self.near, self.inner, *_ = together(self.near, self.inner, *before)
        self.far = lax.ppermute(self.near, self.axis, INNER_SWAP)
        self.outer = lax.ppermute(self.inner, self.axis, OUTWARD)

    def finish(self, *before):
        self.far, *_ = together(self.far, *before)
        last = lax.ppermute(self.far, self.axis, OUTWARD)
        end = at_end(self.axis)
        return jnp.where(end, self.outer, self.far), jnp.where(end, last, self.inner)


INWARD = [(0, 1), (3, 2)]


class Returns:
    def __init__(self, own, axis):
        self.axis, self.line = axis, lax.axis_size(axis) == 4
        self.sums, self.sent = [own], []

    def add(self, k, values, *hold):
        if not self.line:
            self.sums.append(shift(values, self.axis, -k))
        elif k == 1:
            self.near = values
            self.sent = [lax.ppermute(values, self.axis, INWARD)]
            self.sums += self.sent
        elif k == 2:
            if hold:
                values, *_ = lax.optimization_barrier((values, *hold))
            self.through = lax.ppermute(values, self.axis, INWARD)
            inner = lax.ppermute(values, self.axis, INNER_SWAP)
            self.sent = [self.through, inner]
            self.outward = add_rounded(self.near, inner)
        else:
            self.sums.append(swap(add_rounded(values, self.through), self.axis, 3))

    def send_outward(self, *before):
        if self.line:
            outward, *_ = lax.optimization_barrier((self.outward, *before))
            self.sums.append(lax.ppermute(outward, self.axis, OUTWARD))
            self.sent.append(self.sums[-1])


def ring_gather(values, axis):
    size = lax.axis_size(axis)
    found = {0: values}
    ahead = behind = values
    for k in range(1, (size + 1) // 2):
        ahead, behind = shift(ahead, axis, 1), shift(behind, axis, -1)
        found[k], found[size - k] = ahead, behind
    if size % 2 == 0:
        cut = middle_cut(values.shape[0])
        found[size // 2] = jnp.concatenate(
            [shift(ahead[:cut], axis, 1), shift(behind[cut:], axis, -1)], axis=0
        )
    return [found[k] for k in range(size)]


def middle_cut(rows):
    return rows // 16 * 8


def swap(values, axis, bit):
    return lax.ppermute(values, axis, [(i, i ^ bit) for i in range(lax.axis_size(axis))])


def axis_bit(axis, bit):
    return ((lax.axis_index(axis) // bit) % 2).astype(jnp.int32)


def halves(values, axis, bit):
    mine = axis_bit(axis, bit)
    size = values.shape[0] // 2
    part = lambda which: lax.dynamic_slice_in_dim(values, which * size, size, 0)
    return part(mine), part(1 - mine)


def add_rounded(one, other):
    return (one.astype(F32) + other.astype(F32)).astype(one.dtype)


def together(*trees):
    return lax.optimization_barrier(trees)


class PieceSum:
    def __init__(self, core_sum, axis):
        self.axis = axis
        bits = [1 << b for b in range(1, lax.axis_size(axis).bit_length() - 1)]
        self.orders = (bits, bits[::-1])
        self.steps = len(bits)
        self.pieces = 1 << self.steps
        self.parts = (core_sum[: self.pieces], core_sum[self.pieces :])

    def down(self, step):
        done = []
        for part, order in zip(self.parts, self.orders):
            keep, give = halves(part, self.axis, order[step])
            done.append(add_rounded(keep, swap(give, self.axis, order[step])))
        self.parts = tuple(done)

    def up(self, step):
        self.parts = tuple(
            jnp.concatenate([part, swap(part, self.axis, order[::-1][step])], axis=0)
            for part, order in zip(self.parts, self.orders)
        )

    def place(self, write, outs, got):
        ids = [axis_bit(self.axis, 1)]
        for order in self.orders:
            ids.append(sum(axis_bit(self.axis, bit) * (self.pieces >> at + 1) for at, bit in enumerate(order)))
        return assemble(jnp.stack(ids), (*self.parts, *got), write, outs)


def sum_gradients(expert, dense_keep, dense_send, small, shared_rows, expert_out, dense_out, parts):
    rep, exp = "rep", "exp"
    last = expert.steps - 1
    expert.down(0)
    expert.parts, dense_send, small = together(expert.parts, dense_send, small)
    for step in range(1, last + 1):
        expert.down(step)
    dense_sum = add_rounded(dense_keep, swap(dense_send, rep, 1))
    small = small + swap(small, rep, 1)

    expert.parts, dense_sum, small = together(expert.parts, dense_sum, small)
    dense = PieceSum(dense_sum, rep)
    for step in range(last):
        expert.up(step)
        dense.down(step)
        small = small + swap(small, rep, 2 << step)
        expert.parts, dense.parts, small = together(expert.parts, dense.parts, small)
    dense.down(last)
    small = small + swap(small, rep, 2 << last)

    dense.parts, small, expert.parts, parts = together(dense.parts, small, expert.parts, parts)
    expert.up(last)
    shape = (2, -1, *dense.parts[0].shape[1:])
    joined = jnp.concatenate(dense.parts, axis=0).reshape(-1, shape[-1])
    share = share_sum(joined, exp)
    share, small = together(share, small)
    joined = share_collect(share, exp).reshape(shape)
    shared = small[:shared_rows]
    shared = sum([shift(shared, exp, k) for k in range(1, lax.axis_size(exp))], shared)
    dense.parts = (joined[0], joined[1])

    dense.parts, shared, expert.parts = together(dense.parts, shared, expert.parts)
    got = [swap(part, rep, 1) for part in expert.parts]
    for step in range(last):
        dense.up(step)
    dense.parts, got, expert.parts = together(dense.parts, got, expert.parts)
    dense.up(last)
    placed = expert.place(*expert_out, got)
    dense.parts, placed = together(dense.parts, placed)
    got = [swap(part, rep, 1) for part in dense.parts]
    return placed, dense.place(*dense_out, got), shared, small[shared_rows:], parts


def share_sum(values, axis):
    size, me = lax.axis_size(axis), lax.axis_index(axis)
    share = values.shape[0] // size
    take = lambda owner: lax.dynamic_slice_in_dim(values, (owner % size) * share, share, 0)
    total = take(me).astype(F32)
    for k in range(1, size):
        total = total + shift(take(me + k), axis, k).astype(F32)
    return total.astype(values.dtype)


def share_collect(share, axis):
    size, me = lax.axis_size(axis), lax.axis_index(axis)
    rows = share.shape[0]
    result = jnp.zeros((size * rows, share.shape[1]), share.dtype)
    result = lax.dynamic_update_slice_in_dim(result, share, me * rows, 0)
    for k in range(1, size):
        result = lax.dynamic_update_slice_in_dim(result, shift(share, axis, k), ((me - k) % size) * rows, 0)
    return result


def on_device(
    inputs,
    routes,
    ln1_gain,
    ln1_bias,
    w_qkv,
    query_bias,
    value_bias,
    w_out,
    out_bias,
    ln2_gain,
    ln2_bias,
    router,
    experts_in,
    experts_in_bias,
    experts_out,
    experts_out_bias,
    cotangent,
):
    toks, width = inputs.shape
    experts = router.shape[1]
    hidden_units = experts_in.shape[2]
    me = lax.axis_index("exp").astype(jnp.int32).reshape(1)
    core = axis_bit("rep", 1).reshape(1)
    vecs = jnp.stack(
        [ln1_gain, ln1_bias, query_bias, value_bias, out_bias, ln2_gain, ln2_bias, jnp.zeros_like(ln1_gain)]
    )
    tail = -(-toks // 16) * 16
    named = jnp.full((tail - toks + ROUTE_ROWS, width), -1.0, BF16)
    named = named.at[tail - toks : tail - toks + routes.shape[1], :toks].set(routes.T.astype(BF16))

    pieces = lax.axis_size("rep")
    up_rows = jnp.concatenate([cotangent, named], axis=0)
    line = lax.axis_size("exp") == 4
    up_line = LineGather(up_rows, "exp") if line else None
    qkv, ctx, hidden, mixed = attend(inputs, vecs, w_qkv, w_out)
    mixed_line = LineGather(mixed, "exp") if line else None

    router_t = router.T.astype(F32)
    w_in, w_mid = experts_in[0], experts_out[0]
    run_block = lambda rows, up, after, micros: expert_block(
        me, rows, up, router, router_t, w_in, experts_in_bias, w_mid, experts_out_bias, after, micros
    )
    if line:
        up_line.pass_on()
        blocks = [run_block(mixed, up_rows, (up_line.near, up_line.inner), OWN_COST)]
        mixed_line.pass_on(blocks[0][0])
        mixes, ups = [mixed, mixed_line.near], [up_rows, up_line.near]
    else:
        mixes, ups = ring_gather(mixed, "exp"), ring_gather(up_rows, "exp")
        blocks = [run_block(mixed, up_rows, (), OWN_COST)]
    last = lax.axis_size("exp") - 1
    backs, parts = Returns(blocks[0][1], "exp"), Returns(blocks[0][0], "exp")
    sums, early = None, ()
    for k in range(1, last + 1):
        blocks.append(run_block(mixes[k], ups[k], early, NEAR_COST if k == 1 else OTHER_COST))
        if k == 1 and last == 3:
            ups += up_line.finish(blocks[1][0])
            mixes += mixed_line.finish(blocks[1][0])
        hold = (mixes[last], ups[last]) if k == last - 1 else ()
        backs.add(k, blocks[k][1], *hold)
        if k < last:
            parts.add(k, blocks[k][0], *hold)
        if k == last - 2:
            listed = lambda which: [mixes[j] if which is None else blocks[j][which] for j in range(k + 1)]
            sums = partial_grads(listed(None), listed(3), listed(2), listed(4))
            early = (sums[0],)
            near_sent = (*backs.sent, *parts.sent)
        elif k == last - 1:
            early, middle_sent = near_sent, tuple(backs.sent + parts.sent)
    backs.send_outward(blocks[last][1])
    _, _, activs, gpres, geouts, grouters, gin_bias, gout_bias = zip(*blocks)
    final = lambda half, after: final_grads(
        half, mixes[-2:], gpres[-2:], activs[-2:], geouts[-2:], sums, pieces, after
    )
    send = final(1 - core, middle_sent)
    keep = final(core, (send,))
    core_sum = add_rounded(keep, swap(send, "rep", 1))
    expert = PieceSum(core_sum, "rep")

    smalls = [part for trio in zip(grouters, gin_bias, gout_bias) for part in trio]
    shared_rows = 8 + -(-experts // 8) * 8
    small_rows = shared_rows + -(-(hidden_units // width + 1) // 8) * 8
    grad_inputs, dense_keep, dense_send, small = attend_back(
        core, backs.sums, cotangent, inputs, hidden, qkv, ctx, vecs, w_qkv, w_out,
        smalls, small_rows, pieces, (core_sum,),
    )
    parts.add(last, together(blocks[last][0], grad_inputs)[0])
    parts.send_outward(grad_inputs)
    (grad_experts_in, grad_experts_out), (grad_qkv, grad_out), small, own, returned = sum_gradients(
        expert,
        dense_keep,
        dense_send,
        small,
        shared_rows,
        (write_expert, (((width, hidden_units), 0), ((hidden_units // width, width, width), 1))),
        (write_dense, (((width, 3 * width), 0), ((width, width), 0))),
        parts.sums,
    )
    result = sum((values.astype(F32) for values in returned), hidden).astype(BF16)
    return (
        result,
        grad_inputs,
        small[0],
        small[1],
        grad_qkv,
        small[2],
        small[3],
        grad_out,
        small[4],
        small[5],
        small[6],
        small[8 : 8 + experts].T,
        grad_experts_in[None],
        own[: hidden_units // width].reshape(1, hidden_units),
        grad_experts_out.reshape(1, hidden_units, width),
        own[hidden_units // width : hidden_units // width + 1],
    )


def solution(mesh):
    tokens = P(("rep", "exp"), None)
    expert3, expert2 = P("exp", None, None), P("exp", None)
    return jax.shard_map(
        on_device,
        mesh=mesh,
        in_specs=(tokens, tokens) + (P(),) * 10 + (expert3, expert2) * 2 + (tokens,),
        out_specs=(tokens, tokens) + (P(),) * 10 + (expert3, expert2) * 2,
        check_vma=False,
    )
```

```python
import functools

import jax
import jax.numpy as jnp
from jax import lax
from jax.experimental import pallas as pl
from jax.experimental.pallas import tpu as pltpu
from jax.sharding import PartitionSpec as P

HEADS = 12
HEAD_DIM = 64
SEQ = 197
NORM_EPS = 1e-06
F32 = jnp.float32
BF16 = jnp.bfloat16
LANES = 128
PAIR = LANES // HEAD_DIM
SEQ_PAD = 208
FF_TILE = 768
ROUTE_ROWS = 16
VMEM_BYTES = 58 * 2**20
COST_FLOPS = 4e8
OWN_COST = 24
NEAR_COST = 24
OTHER_COST = 1
PARTIAL_COST = 1
FINAL_COST = 4
BACK_COST = 28
MARK_COST = 400
TAIL_SCALE = 0.305
TAIL_COEFS = (
    0.1216396663821839,
    0.12246803351870969,
    0.10341227166034979,
    0.12105264456174025,
    -0.03803921974174099,
    0.18578799927872533,
    -0.1530311110530253,
    0.03670976324394601,
)
INV_SQRT_2PI = 0.3989422804014327
VECS = ("g1", "b1", "qb", "vb", "ob", "g2", "b2", "none")


def dot(lhs, rhs):
    return lax.dot_general(lhs, rhs, (((1,), (0,)), ((), ())), preferred_element_type=F32)


def dot_rt(lhs, rhs):
    return lax.dot_general(lhs, rhs, (((1,), (1,)), ((), ())), preferred_element_type=F32)


def dot_lt(lhs, rhs):
    return lax.dot_general(lhs, rhs, (((0,), (0,)), ((), ())), preferred_element_type=F32)


def row_mean(values):
    return jnp.mean(values, axis=-1, keepdims=True)


def unit_norm(values):
    centred = values - row_mean(values)
    scale = lax.rsqrt(row_mean(centred * centred) + NORM_EPS)
    return centred * scale, scale


def column_sum(values):
    return jnp.sum(values, axis=0, keepdims=True)


def gelu_parts(pre):
    size = jnp.abs(pre)
    bell = jnp.exp(pre * pre * -0.5)
    frac = 1.0 / (1.0 + TAIL_SCALE * size)
    poly = jnp.full_like(pre, TAIL_COEFS[-1])
    for coef in TAIL_COEFS[-2::-1]:
        poly = poly * frac + coef
    tail = bell * (poly * frac)
    return jnp.where(pre >= 0, 1.0 - tail, tail), bell * INV_SQRT_2PI


def pair_masks(rows):
    lane = lax.broadcasted_iota(jnp.int32, (rows, LANES), 1)
    return [(lane >= h * HEAD_DIM) & (lane < (h + 1) * HEAD_DIM) for h in range(PAIR)]


def stack_heads(values, masks):
    return jnp.concatenate([jnp.where(m, values, 0.0) for m in masks], axis=0).astype(BF16)


def unstack_heads(values, masks):
    rows = values.shape[0] // PAIR
    picked = values[:rows]
    for h in range(1, PAIR):
        picked = jnp.where(masks[h], values[h * rows : (h + 1) * rows], picked)
    return picked


def probabilities(scores):
    key_id = lax.broadcasted_iota(jnp.int32, scores.shape, 1)
    scores = jnp.where(key_id < SEQ, scores, -1e30)
    weights = jnp.exp(scores - jnp.max(scores, axis=-1, keepdims=True))
    return weights * (1.0 / jnp.sum(weights, axis=-1, keepdims=True))


class Fetch:
    def __init__(self, pairs, sems, first=0):
        self.copies = [
            pltpu.make_async_copy(source, target, sems.at[first + at]) for at, (source, target) in enumerate(pairs)
        ]
        for copy in self.copies:
            copy.start()

    def wait(self, *which):
        for at in which:
            self.copies[at].wait()


def attend_kernel(
    x_hbm, vecs_ref, wqkv_hbm, wout_hbm,
    qkv_hbm, ctx_ref, hidden_ref, mixed_ref,
    qkv_s, ctx_s, x_ref, wqkv_ref, wout_ref, qkv_ref, sems,
):
    fetch = Fetch(((x_hbm, x_ref), (wqkv_hbm, wqkv_ref), (wout_hbm, wout_ref)), sems)
    fetch.wait(0)
    toks, width = x_ref.shape
    spare = qkv_s.shape[0] - toks
    x = x_ref[...].astype(F32)
    vec = lambda name: vecs_ref[VECS.index(name) : VECS.index(name) + 1, :]
    unit, _ = unit_norm(x)
    normed = (unit * vec("g1") + vec("b1")).astype(BF16)
    fetch.wait(1)
    for part, bias in ((0, "qb"), (1, None), (2, "vb")):
        cols = pl.ds(part * width, width)
        joined = dot(normed, wqkv_ref[:, cols])
        if bias is not None:
            joined = joined + vec(bias)
        joined = joined.astype(BF16)
        qkv_ref[:, cols] = joined
        qkv_s[0:toks, cols] = joined.astype(F32)
    store = Fetch(((qkv_ref, qkv_hbm),), sems, 3)
    qkv_s[toks:, :] = jnp.zeros((spare, 3 * width), F32)
    masks = pair_masks(SEQ_PAD)
    for img in range(toks // SEQ):
        rows = pl.ds(img * SEQ, SEQ_PAD)
        for at in range(0, width, LANES):
            query = stack_heads(qkv_s[rows, at : at + LANES], masks)
            key = qkv_s[rows, width + at : width + at + LANES].astype(BF16)
            value = qkv_s[rows, 2 * width + at : 2 * width + at + LANES].astype(BF16)
            probs = probabilities(dot_rt(query, key) * HEAD_DIM**-0.5).astype(BF16)
            ctx_s[rows, at : at + LANES] = unstack_heads(dot(probs, value), masks)
    ctx = ctx_s[0:toks, :].astype(BF16)
    ctx_ref[...] = ctx
    fetch.wait(2)
    hidden = x + dot(ctx, wout_ref[...]) + vec("ob")
    hidden_ref[...] = hidden
    unit2, _ = unit_norm(hidden)
    mixed_ref[...] = (unit2 * vec("g2") + vec("b2")).astype(BF16)
    store.wait(0)


def expert_kernel(
    waits, me_ref, *refs,
):
    expert_body(me_ref, *refs[:8], *refs[8 + waits :])


def expert_body(
    me_ref,
    x_ref, up_ref, router_ref, router_t_ref, win_ref, bin_ref, wout_ref, bout_ref,
    part_ref, back_ref, activ_ref, gpre_ref, geout_ref, grouter_ref, gin_bias_ref, gout_bias_ref,
    out_s, back_s, probs_s, gate_s,
):
    step = pl.program_id(0)
    me = me_ref[0]
    toks = x_ref.shape[0]
    tail = up_ref.shape[0] - ROUTE_ROWS

    @pl.when(step == 0)
    def _():
        named = column_sum((up_ref[tail:, :].astype(F32) == me.astype(F32)).astype(F32))
        named = jnp.transpose(jnp.broadcast_to(named, (8, named.shape[1])))[:toks, 0:1]
        logits = dot(x_ref[...], router_ref[...])
        weights = jnp.exp(logits - jnp.max(logits, axis=-1, keepdims=True))
        probs = weights / jnp.sum(weights, axis=-1, keepdims=True)
        probs_s[...] = probs
        mine = lax.broadcasted_iota(jnp.int32, probs.shape, 1) == me
        gate = jnp.sum(jnp.where(mine, probs, 0.0), axis=-1, keepdims=True) * named
        gate_s[...] = gate
        geout = (gate * up_ref[0:toks, :].astype(F32)).astype(BF16)
        geout_ref[...] = geout
        gout_bias_ref[...] = column_sum(geout.astype(F32))
        out_s[...] = jnp.zeros_like(out_s)
        back_s[...] = jnp.zeros_like(back_s)

    pre = dot(x_ref[...], win_ref[...]) + bin_ref[...]
    phi, bell = gelu_parts(pre)
    activ = (pre * phi).astype(BF16)
    activ_ref[...] = activ
    gpre = (dot_rt(geout_ref[...], wout_ref[...]) * (phi + pre * bell)).astype(BF16)
    gpre_ref[...] = gpre
    gin_bias_ref[...] = column_sum(gpre.astype(F32))
    out_s[...] += dot(activ, wout_ref[...])
    back_s[...] += dot_rt(gpre, win_ref[...])

    @pl.when(step == pl.num_programs(0) - 1)
    def _():
        expert_out = (out_s[...] + bout_ref[...]).astype(BF16).astype(F32)
        gate = gate_s[...]
        probs = probs_s[...]
        part_ref[...] = (gate * expert_out).astype(BF16)
        route_grad = jnp.sum(up_ref[0:toks, :].astype(F32) * expert_out, axis=-1, keepdims=True)
        mine = (lax.broadcasted_iota(jnp.int32, probs.shape, 1) == me).astype(F32)
        glogits = gate * route_grad * (mine - probs)
        back = back_s[...].astype(BF16).astype(F32)
        for other in range(probs.shape[1]):
            back = back + glogits[:, other : other + 1] * router_t_ref[other : other + 1, :]
        back_ref[...] = back.astype(BF16)
        coarse = glogits.astype(BF16)
        fine = (glogits - coarse.astype(F32)).astype(BF16)
        grouter_ref[...] = dot_lt(coarse, x_ref[...]) + dot_lt(fine, x_ref[...])


def partial_grads_kernel(count, *refs):
    totals = [None, None]
    for k in range(count):
        rows, gpre, activ, geout = (refs[which * count + k][...] for which in range(4))
        for at, term in enumerate((dot_lt(rows, gpre), dot_lt(activ, geout))):
            totals[at] = term if totals[at] is None else totals[at] + term
    refs = refs[4 * count :]
    for at in range(2):
        refs[at][...] = totals[at]


def final_grads_kernel(count, half_ref, *refs):
    grad_ref = refs[-1]
    pieces, _, share, _ = grad_ref.shape
    grad_in, grad_out = refs[4 * count][...], refs[4 * count + 1][...]
    for k in range(count):
        rows, gpre, activ, geout = (refs[which * count + k][...] for which in range(4))
        grad_in = grad_in + dot_lt(rows, gpre)
        grad_out = grad_out + dot_lt(activ, geout)
    for piece in range(pieces):
        grad_ref[piece, 0] = grad_in[piece * share : (piece + 1) * share].astype(BF16)
        grad_ref[piece, 1] = grad_out[piece * share : (piece + 1) * share].astype(BF16)


def assemble_kernel(write, ids_ref, *refs):
    outs = refs[4:]
    at = pl.program_id(0)
    chosen = ((at // 2) ^ ids_ref[0]) * 2 + at % 2
    for which in range(4):

        @pl.when(chosen == which)
        def _(which=which):
            for piece in range(refs[which].shape[0]):
                write(refs[which][piece ^ ids_ref[1 + which % 2]].astype(F32), piece, *outs)


def write_dense(values, piece, qkv_ref, out_ref):
    share, cut = values.shape[0], qkv_ref.shape[1]
    rows = slice(piece * share, (piece + 1) * share)
    qkv_ref[rows, :] = values[:, :cut]
    out_ref[rows, :] = values[:, cut:]


def write_expert(values, piece, in_ref, out_ref):
    share, width = values.shape[1], out_ref.shape[2]
    rows = slice(piece * share, (piece + 1) * share)
    in_ref[rows, :] = values[0]
    for tile in range(out_ref.shape[0]):
        out_ref[tile, rows, :] = values[1, :, tile * width : (tile + 1) * width]


def attend_back_kernel(
    count, sums, core_ref, vecs_ref, *refs,
):
    loaded = sums + 7
    *refs, sems = refs
    refs, held = refs[:-loaded], refs[-loaded:]
    *refs, ginput_ref, keep_hbm, send_hbm, small_ref, qkv_s, gctx_s, gjoin_s, keep_ref, send_ref = refs
    fetch = Fetch(zip(refs[:loaded], held), sems)
    refs = refs[loaded:]
    gmix_refs = held[:sums]
    hidden_ref, up_ref, wout_ref, ctx_ref, qkv_ref, x_ref, wqkv_ref = held[sums:]
    fetch.wait(*range(sums + 2))
    toks, width = x_ref.shape
    spare = qkv_s.shape[0] - toks
    vec = lambda name: vecs_ref[VECS.index(name) : VECS.index(name) + 1, :]

    def put(values, start):
        cols = slice(start, start + values.shape[1])
        pieces, share = keep_ref.shape[:2]
        for first, halves in ((0, (keep_ref, send_ref)), (1, (send_ref, keep_ref))):

            @pl.when(core_ref[0] == first)
            def _(halves=halves):
                for piece in range(2 * pieces):
                    rows = slice(piece * share, (piece + 1) * share)
                    halves[piece // pieces][piece % pieces, :, cols] = values[rows].astype(BF16)

    gmix = gmix_refs[0][...].astype(F32)
    for ref in gmix_refs[1:]:
        gmix = gmix + ref[...].astype(F32)
    unit2, scale2 = unit_norm(hidden_ref[...])
    grad_g2 = column_sum(gmix * unit2)
    grad_b2 = column_sum(gmix)
    m2 = gmix * vec("g2")
    ghidden = up_ref[...].astype(F32) + scale2 * (m2 - row_mean(m2) - unit2 * row_mean(m2 * unit2))
    gatt = ghidden.astype(BF16)
    fetch.wait(sums + 2, sums + 3)
    grad_ob = column_sum(gatt.astype(F32))
    put(dot_lt(ctx_ref[...], gatt), 3 * width)
    gctx_s[0:toks, :] = dot_rt(gatt, wout_ref[...]).astype(BF16).astype(F32)
    gctx_s[toks:, :] = jnp.zeros((spare, width), F32)
    fetch.wait(sums + 4)
    qkv_s[0:toks, :] = qkv_ref[...].astype(F32)
    qkv_s[toks:, :] = jnp.zeros((spare, 3 * width), F32)
    masks = pair_masks(SEQ_PAD)
    row_ok = lax.broadcasted_iota(jnp.int32, (SEQ_PAD, 1), 0) < SEQ
    for img in range(toks // SEQ):
        rows = pl.ds(img * SEQ, SEQ_PAD)
        for at in range(0, width, LANES):
            query = stack_heads(jnp.where(row_ok, qkv_s[rows, at : at + LANES], 0.0), masks)
            key = qkv_s[rows, width + at : width + at + LANES].astype(BF16)
            value = qkv_s[rows, 2 * width + at : 2 * width + at + LANES].astype(BF16)
            gctx = stack_heads(jnp.where(row_ok, gctx_s[rows, at : at + LANES], 0.0), masks)
            probs = probabilities(dot_rt(query, key) * HEAD_DIM**-0.5)
            gvalue = dot_lt(probs.astype(BF16), gctx)
            gweights = dot_rt(gctx, value)
            inner = jnp.sum(gweights * probs, axis=-1, keepdims=True)
            gscores = (probs * (gweights - inner)).astype(BF16)
            gquery = unstack_heads(dot(gscores, key), masks) * HEAD_DIM**-0.5
            gkey = dot_lt(gscores, query) * HEAD_DIM**-0.5
            gjoin_s[rows, at : at + LANES] = gquery
            gjoin_s[rows, width + at : width + at + LANES] = gkey
            gjoin_s[rows, 2 * width + at : 2 * width + at + LANES] = gvalue
    gjoin = gjoin_s[0:toks, :].astype(BF16)
    grad_qb = column_sum(gjoin[:, :width].astype(F32))
    grad_vb = column_sum(gjoin[:, 2 * width :].astype(F32))
    fetch.wait(sums + 5, sums + 6)
    x = x_ref[...].astype(F32)
    unit1, scale1 = unit_norm(x)
    normed = (unit1 * vec("g1") + vec("b1")).astype(BF16)
    put(dot_lt(normed, gjoin), 0)
    store = Fetch(((keep_ref, keep_hbm), (send_ref, send_hbm)), sems, loaded)
    gnormed = dot_rt(gjoin, wqkv_ref[...])
    grad_g1 = column_sum(gnormed * unit1)
    grad_b1 = column_sum(gnormed)
    m1 = gnormed * vec("g1")
    ginput = ghidden + scale1 * (m1 - row_mean(m1) - unit1 * row_mean(m1 * unit1))
    ginput_ref[...] = ginput.astype(BF16)
    for at, small in enumerate((grad_g1, grad_b1, grad_qb, grad_vb, grad_ob, grad_g2, grad_b2)):
        small_ref[at : at + 1, :] = small
    small_ref[7:, :] = jnp.zeros((small_ref.shape[0] - 7, width), F32)
    total = lambda which: sum((ref[...] for ref in refs[which:count:3][1:]), refs[which][...])
    router_sum, in_sum, out_sum = (total(which) for which in range(3))
    small_ref[8 : 8 + router_sum.shape[0], :] = router_sum
    at = 8 + -(-router_sum.shape[0] // 8) * 8
    for tile in range(in_sum.shape[1] // width):
        small_ref[at + tile : at + tile + 1, :] = in_sum[:, tile * width : (tile + 1) * width]
    at += in_sum.shape[1] // width
    small_ref[at : at + 1, :] = out_sum
    store.wait(0, 1)


def params(**more):
    return pltpu.CompilerParams(vmem_limit_bytes=VMEM_BYTES, **more)


def cost(micros):
    return pl.CostEstimate(flops=int(micros * COST_FLOPS), bytes_accessed=1024, transcendentals=0)


def whole():
    return pl.BlockSpec(memory_space=pltpu.VMEM)


def outside():
    return pl.BlockSpec(memory_space=pl.ANY)


def scalars():
    return pl.BlockSpec(memory_space=pltpu.SMEM)


def attend(inputs, vecs, w_qkv, w_out):
    toks, width = inputs.shape
    padded = -(-(toks - SEQ + SEQ_PAD) // 16) * 16
    return pl.pallas_call(
        attend_kernel,
        out_shape=(
            jax.ShapeDtypeStruct((toks, 3 * width), BF16),
            jax.ShapeDtypeStruct((toks, width), BF16),
            jax.ShapeDtypeStruct((toks, width), F32),
            jax.ShapeDtypeStruct((toks, width), BF16),
        ),
        in_specs=[outside(), whole(), outside(), outside()],
        out_specs=(outside(), whole(), whole(), whole()),
        scratch_shapes=[
            pltpu.VMEM((padded, 3 * width), F32),
            pltpu.VMEM((padded, width), F32),
            pltpu.VMEM((toks, width), BF16),
            pltpu.VMEM((width, 3 * width), BF16),
            pltpu.VMEM((width, width), BF16),
            pltpu.VMEM((toks, 3 * width), BF16),
            pltpu.SemaphoreType.DMA((4,)),
        ],
        compiler_params=params(),
        cost_estimate=cost(12),
        name="attend",
    )(inputs, vecs, w_qkv, w_out)


def attend_back(core, gmixes, up, inputs, hidden, qkv, ctx, vecs, w_qkv, w_out, smalls, small_rows, pieces, after):
    toks, width = inputs.shape
    padded = -(-(toks - SEQ + SEQ_PAD) // 16) * 16
    loaded = (*gmixes, hidden, up, w_out, ctx, qkv, inputs, w_qkv)
    half = jax.ShapeDtypeStruct((pieces, width // (2 * pieces), 4 * width), BF16)
    return pl.pallas_call(
        functools.partial(attend_back_kernel, len(smalls), len(gmixes)),
        out_shape=(
            jax.ShapeDtypeStruct((toks, width), BF16),
            half,
            half,
            jax.ShapeDtypeStruct((small_rows, width), F32),
        ),
        in_specs=[scalars(), whole()]
        + [outside()] * len(loaded)
        + [whole()] * len(smalls)
        + [outside()] * len(after),
        out_specs=(whole(), outside(), outside(), whole()),
        scratch_shapes=[
            pltpu.VMEM((padded, 3 * width), F32),
            pltpu.VMEM((padded, width), F32),
            pltpu.VMEM((padded, 3 * width), F32),
            pltpu.VMEM(half.shape, BF16),
            pltpu.VMEM(half.shape, BF16),
            *(pltpu.VMEM(array.shape, array.dtype) for array in loaded),
            pltpu.SemaphoreType.DMA((len(loaded) + 2,)),
        ],
        compiler_params=params(),
        cost_estimate=cost(BACK_COST),
        name="attend_back",
    )(core, vecs, *loaded, *smalls, *after)


def marker_kernel(*refs):
    refs[-1][...] = jnp.zeros_like(refs[-1])


def marker(micros, *arrays):
    return pl.pallas_call(
        marker_kernel,
        out_shape=jax.ShapeDtypeStruct((8, LANES), F32),
        in_specs=[outside()] * len(arrays),
        out_specs=whole(),
        compiler_params=params(),
        cost_estimate=cost(micros),
        name="marker",
    )(*arrays)


def expert_block(me, rows, up, router, router_t, w_in, b_in, w_out, b_out, after=(), micros=1):
    toks, width = rows.shape
    experts = router.shape[1]
    hidden = w_in.shape[1]
    fixed = lambda shape: pl.BlockSpec(shape, lambda f, m: (0, 0))
    return pl.pallas_call(
        functools.partial(expert_kernel, len(after)),
        out_shape=(
            jax.ShapeDtypeStruct((toks, width), BF16),
            jax.ShapeDtypeStruct((toks, width), BF16),
            jax.ShapeDtypeStruct((toks, hidden), BF16),
            jax.ShapeDtypeStruct((toks, hidden), BF16),
            jax.ShapeDtypeStruct((toks, width), BF16),
            jax.ShapeDtypeStruct((experts, width), F32),
            jax.ShapeDtypeStruct((1, hidden), F32),
            jax.ShapeDtypeStruct((1, width), F32),
        ),
        grid_spec=pltpu.PrefetchScalarGridSpec(
            num_scalar_prefetch=1,
            grid=(hidden // FF_TILE,),
            in_specs=[
                fixed((toks, width)),
                fixed(up.shape),
                fixed(router.shape),
                fixed(router_t.shape),
                pl.BlockSpec((width, FF_TILE), lambda f, m: (0, f)),
                pl.BlockSpec((1, FF_TILE), lambda f, m: (0, f)),
                pl.BlockSpec((FF_TILE, width), lambda f, m: (f, 0)),
                fixed((1, width)),
            ]
            + [pl.BlockSpec(memory_space=pl.ANY)] * len(after),
            out_specs=(
                fixed((toks, width)),
                fixed((toks, width)),
                pl.BlockSpec((toks, FF_TILE), lambda f, m: (0, f)),
                pl.BlockSpec((toks, FF_TILE), lambda f, m: (0, f)),
                fixed((toks, width)),
                fixed((experts, width)),
                pl.BlockSpec((1, FF_TILE), lambda f, m: (0, f)),
                fixed((1, width)),
            ),
            scratch_shapes=[
                pltpu.VMEM((toks, width), F32),
                pltpu.VMEM((toks, width), F32),
                pltpu.VMEM((toks, experts), F32),
                pltpu.VMEM((toks, 1), F32),
            ],
        ),
        compiler_params=params(),
        cost_estimate=cost(micros),
        name="expert_block",
    )(me, rows, up, router, router_t, w_in, b_in, w_out, b_out, *after)


def partial_grads(rows, gpres, activs, geouts):
    count = len(rows)
    toks, width = rows[0].shape
    hidden = gpres[0].shape[1]
    fixed = pl.BlockSpec((toks, width), lambda f: (0, 0))
    tile = pl.BlockSpec((toks, width), lambda f: (0, f))
    total = pl.BlockSpec((width, width), lambda f: (0, f))
    return pl.pallas_call(
        functools.partial(partial_grads_kernel, count),
        out_shape=(jax.ShapeDtypeStruct((width, hidden), F32),) * 2,
        grid=(hidden // width,),
        in_specs=[fixed] * count + [tile] * (2 * count) + [fixed] * count,
        out_specs=(total,) * 2,
        compiler_params=params(),
        cost_estimate=cost(PARTIAL_COST),
        name="partial_grads",
    )(*rows, *gpres, *activs, *geouts)


def final_grads(half, rows, gpres, activs, geouts, started, pieces, after=()):
    count = len(rows)
    toks, width = rows[0].shape
    hidden = gpres[0].shape[1]
    share = width // (2 * pieces)
    total = pl.BlockSpec((width // 2, width), lambda f, h: (h[0], f))
    return pl.pallas_call(
        functools.partial(final_grads_kernel, count),
        out_shape=jax.ShapeDtypeStruct((pieces, 2, share, hidden), BF16),
        grid_spec=pltpu.PrefetchScalarGridSpec(
            num_scalar_prefetch=1,
            grid=(hidden // width,),
            in_specs=[pl.BlockSpec((toks, width // 2), lambda f, h: (0, h[0]))] * count
            + [pl.BlockSpec((toks, width), lambda f, h: (0, f))] * count
            + [pl.BlockSpec((toks, width // 2), lambda f, h: (0, 2 * f + h[0]))] * count
            + [pl.BlockSpec((toks, width), lambda f, h: (0, 0))] * count
            + [total] * 2
            + [pl.BlockSpec(memory_space=pl.ANY)] * len(after),
            out_specs=pl.BlockSpec((pieces, 2, share, width), lambda f, h: (0, 0, 0, f)),
        ),
        compiler_params=params(),
        cost_estimate=cost(FINAL_COST),
        name="final_grads",
    )(half, *rows, *gpres, *activs, *geouts, *started, *after)


def assemble(ids, groups, write, outs):
    blocks = []
    for shape, dim in outs:
        block = tuple(n // 4 if d == dim else n for d, n in enumerate(shape))
        place = lambda at, ids, dim=dim, rank=len(shape): tuple(at if d == dim else 0 for d in range(rank))
        blocks.append(pl.BlockSpec(block, place))
    rank = groups[0].ndim
    return pl.pallas_call(
        functools.partial(assemble_kernel, write),
        out_shape=tuple(jax.ShapeDtypeStruct(shape, F32) for shape, _ in outs),
        grid_spec=pltpu.PrefetchScalarGridSpec(
            num_scalar_prefetch=1,
            grid=(4,),
            in_specs=[pl.BlockSpec(groups[0].shape, lambda at, ids: (0,) * rank)] * 4,
            out_specs=tuple(blocks),
        ),
        compiler_params=params(),
        cost_estimate=cost(5),
        name="assemble",
    )(ids, *groups)


def shift(values, axis, by):
    size = lax.axis_size(axis)
    return lax.ppermute(values, axis, [(i, (i + by) % size) for i in range(size)])


INNER_SWAP = [(1, 2), (2, 1)]
OUTWARD = [(1, 0), (2, 3)]


def at_end(axis):
    place = lax.axis_index(axis)
    return (place == 0) | (place == lax.axis_size(axis) - 1)


class LineGather:
    def __init__(self, values, axis):
        self.axis, self.own = axis, values
        self.near = swap(values, axis, 1)
        self.inner = lax.ppermute(values, axis, INNER_SWAP)

    def pass_on(self, *before):
        self.near, self.inner, *_ = together(self.near, self.inner, *before)
        self.far = lax.ppermute(self.near, self.axis, INNER_SWAP)
        self.outer = lax.ppermute(self.inner, self.axis, OUTWARD)

    def finish(self, *before):
        self.far, *_ = together(self.far, *before)
        last = lax.ppermute(self.far, self.axis, OUTWARD)
        end = at_end(self.axis)
        return jnp.where(end, self.outer, self.far), jnp.where(end, last, self.inner)


INWARD = [(0, 1), (3, 2)]


class Returns:
    def __init__(self, own, axis):
        self.axis, self.line = axis, lax.axis_size(axis) == 4
        self.sums, self.sent = [own], []

    def add(self, k, values, *hold):
        if not self.line:
            self.sums.append(shift(values, self.axis, -k))
        elif k == 1:
            self.near = values
            self.sent = [lax.ppermute(values, self.axis, INWARD)]
            self.sums += self.sent
        elif k == 2:
            if hold:
                values, *_ = lax.optimization_barrier((values, *hold))
            self.through = lax.ppermute(values, self.axis, INWARD)
            inner = lax.ppermute(values, self.axis, INNER_SWAP)
            self.sent = [self.through, inner]
            self.outward = add_rounded(self.near, inner)
        else:
            self.sums.append(swap(add_rounded(values, self.through), self.axis, 3))

    def send_outward(self, *before):
        if self.line:
            outward, *_ = lax.optimization_barrier((self.outward, *before))
            self.sums.append(lax.ppermute(outward, self.axis, OUTWARD))
            self.sent.append(self.sums[-1])


def ring_gather(values, axis):
    size = lax.axis_size(axis)
    found = {0: values}
    ahead = behind = values
    for k in range(1, (size + 1) // 2):
        ahead, behind = shift(ahead, axis, 1), shift(behind, axis, -1)
        found[k], found[size - k] = ahead, behind
    if size % 2 == 0:
        cut = middle_cut(values.shape[0])
        found[size // 2] = jnp.concatenate(
            [shift(ahead[:cut], axis, 1), shift(behind[cut:], axis, -1)], axis=0
        )
    return [found[k] for k in range(size)]


def middle_cut(rows):
    return rows // 16 * 8


def swap(values, axis, bit):
    return lax.ppermute(values, axis, [(i, i ^ bit) for i in range(lax.axis_size(axis))])


def axis_bit(axis, bit):
    return ((lax.axis_index(axis) // bit) % 2).astype(jnp.int32)


def halves(values, axis, bit):
    mine = axis_bit(axis, bit)
    size = values.shape[0] // 2
    part = lambda which: lax.dynamic_slice_in_dim(values, which * size, size, 0)
    return part(mine), part(1 - mine)


def add_rounded(one, other):
    return (one.astype(F32) + other.astype(F32)).astype(one.dtype)


def together(*trees):
    return lax.optimization_barrier(trees)


class PieceSum:
    def __init__(self, core_sum, axis):
        self.axis = axis
        bits = [1 << b for b in range(1, lax.axis_size(axis).bit_length() - 1)]
        self.orders = (bits, bits[::-1])
        self.steps = len(bits)
        self.pieces = 1 << self.steps
        self.parts = (core_sum[: self.pieces], core_sum[self.pieces :])

    def down(self, step):
        done = []
        for part, order in zip(self.parts, self.orders):
            keep, give = halves(part, self.axis, order[step])
            done.append(add_rounded(keep, swap(give, self.axis, order[step])))
        self.parts = tuple(done)

    def up(self, step):
        self.parts = tuple(
            jnp.concatenate([part, swap(part, self.axis, order[::-1][step])], axis=0)
            for part, order in zip(self.parts, self.orders)
        )

    def place(self, write, outs, got):
        ids = [axis_bit(self.axis, 1)]
        for order in self.orders:
            ids.append(sum(axis_bit(self.axis, bit) * (self.pieces >> at + 1) for at, bit in enumerate(order)))
        return assemble(jnp.stack(ids), (*self.parts, *got), write, outs)


def sum_gradients(expert, dense_keep, dense_send, small, shared_rows, expert_out, dense_out, parts):
    rep, exp = "rep", "exp"
    last = expert.steps - 1
    expert.down(0)
    expert.parts, dense_send, small = together(expert.parts, dense_send, small)
    for step in range(1, last + 1):
        expert.down(step)
    dense_sum = add_rounded(dense_keep, swap(dense_send, rep, 1))
    small = small + swap(small, rep, 1)

    expert.parts, dense_sum, small = together(expert.parts, dense_sum, small)
    dense = PieceSum(dense_sum, rep)
    for step in range(last):
        expert.up(step)
        dense.down(step)
        small = small + swap(small, rep, 2 << step)
        expert.parts, dense.parts, small = together(expert.parts, dense.parts, small)
    dense.down(last)
    small = small + swap(small, rep, 2 << last)

    dense.parts, small, expert.parts, parts = together(dense.parts, small, expert.parts, parts)
    expert.up(last)
    shape = (2, -1, *dense.parts[0].shape[1:])
    joined = jnp.concatenate(dense.parts, axis=0).reshape(-1, shape[-1])
    share = share_sum(joined, exp)
    share, small = together(share, small)
    joined = share_collect(share, exp).reshape(shape)
    shared = small[:shared_rows]
    shared = sum([shift(shared, exp, k) for k in range(1, lax.axis_size(exp))], shared)
    dense.parts = (joined[0], joined[1])

    dense.parts, shared, expert.parts = together(dense.parts, shared, expert.parts)
    got = [swap(part, rep, 1) for part in expert.parts]
    for step in range(last):
        dense.up(step)
    dense.parts, got, expert.parts = together(dense.parts, got, expert.parts)
    dense.up(last)
    placed = expert.place(*expert_out, got)
    dense.parts, placed = together(dense.parts, placed)
    got = [swap(part, rep, 1) for part in dense.parts]
    return placed, dense.place(*dense_out, got), shared, small[shared_rows:], parts


def share_sum(values, axis):
    size, me = lax.axis_size(axis), lax.axis_index(axis)
    share = values.shape[0] // size
    take = lambda owner: lax.dynamic_slice_in_dim(values, (owner % size) * share, share, 0)
    total = take(me).astype(F32)
    for k in range(1, size):
        total = total + shift(take(me + k), axis, k).astype(F32)
    return total.astype(values.dtype)


def share_collect(share, axis):
    size, me = lax.axis_size(axis), lax.axis_index(axis)
    rows = share.shape[0]
    result = jnp.zeros((size * rows, share.shape[1]), share.dtype)
    result = lax.dynamic_update_slice_in_dim(result, share, me * rows, 0)
    for k in range(1, size):
        result = lax.dynamic_update_slice_in_dim(result, shift(share, axis, k), ((me - k) % size) * rows, 0)
    return result


def on_device(
    inputs,
    routes,
    ln1_gain,
    ln1_bias,
    w_qkv,
    query_bias,
    value_bias,
    w_out,
    out_bias,
    ln2_gain,
    ln2_bias,
    router,
    experts_in,
    experts_in_bias,
    experts_out,
    experts_out_bias,
    cotangent,
):
    toks, width = inputs.shape
    experts = router.shape[1]
    hidden_units = experts_in.shape[2]
    me = lax.axis_index("exp").astype(jnp.int32).reshape(1)
    core = axis_bit("rep", 1).reshape(1)
    vecs = jnp.stack(
        [ln1_gain, ln1_bias, query_bias, value_bias, out_bias, ln2_gain, ln2_bias, jnp.zeros_like(ln1_gain)]
    )
    tail = -(-toks // 16) * 16
    named = jnp.full((tail - toks + ROUTE_ROWS, width), -1.0, BF16)
    named = named.at[tail - toks : tail - toks + routes.shape[1], :toks].set(routes.T.astype(BF16))

    pieces = lax.axis_size("rep")
    up_rows = jnp.concatenate([cotangent, named], axis=0)
    line = lax.axis_size("exp") == 4
    up_line = LineGather(up_rows, "exp") if line else None
    qkv, ctx, hidden, mixed = attend(inputs, vecs, w_qkv, w_out)
    mixed_line = LineGather(mixed, "exp") if line else None

    router_t = router.T.astype(F32)
    w_in, w_mid = experts_in[0], experts_out[0]
    run_block = lambda rows, up, after, micros: expert_block(
        me, rows, up, router, router_t, w_in, experts_in_bias, w_mid, experts_out_bias, after, micros
    )
    if line:
        up_line.pass_on()
        blocks = [run_block(mixed, up_rows, (up_line.near, up_line.inner), OWN_COST)]
        mixed_line.pass_on(blocks[0][0])
        mixes, ups = [mixed, mixed_line.near], [up_rows, up_line.near]
    else:
        mixes, ups = ring_gather(mixed, "exp"), ring_gather(up_rows, "exp")
        blocks = [run_block(mixed, up_rows, (), OWN_COST)]
    last = lax.axis_size("exp") - 1
    backs, parts = Returns(blocks[0][1], "exp"), Returns(blocks[0][0], "exp")
    sums, early = None, ()
    for k in range(1, last + 1):
        blocks.append(run_block(mixes[k], ups[k], early, NEAR_COST if k == 1 else OTHER_COST))
        if k == 1 and last == 3:
            ups += up_line.finish(blocks[1][0])
            mixes += mixed_line.finish(blocks[1][0])
        hold = (mixes[last], ups[last]) if k == last - 1 else ()
        backs.add(k, blocks[k][1], *hold)
        if k < last:
            parts.add(k, blocks[k][0], *hold)
        if k == last - 2:
            listed = lambda which: [mixes[j] if which is None else blocks[j][which] for j in range(k + 1)]
            sums = partial_grads(listed(None), listed(3), listed(2), listed(4))
            early = (sums[0],)
            near_sent = (*backs.sent, *parts.sent)
        elif k == last - 1:
            early, middle_sent = near_sent, tuple(backs.sent)
    backs.send_outward(blocks[last][1])
    _, _, activs, gpres, geouts, grouters, gin_bias, gout_bias = zip(*blocks)
    final = lambda half, after: final_grads(
        half, mixes[-2:], gpres[-2:], activs[-2:], geouts[-2:], sums, pieces, after
    )
    send = final(1 - core, middle_sent)
    keep = final(core, (send,))
    core_sum = add_rounded(keep, swap(send, "rep", 1))
    expert = PieceSum(core_sum, "rep")

    smalls = [part for trio in zip(grouters, gin_bias, gout_bias) for part in trio]
    shared_rows = 8 + -(-experts // 8) * 8
    small_rows = shared_rows + -(-(hidden_units // width + 1) // 8) * 8
    grad_inputs, dense_keep, dense_send, small = attend_back(
        core, backs.sums, cotangent, inputs, hidden, qkv, ctx, vecs, w_qkv, w_out,
        smalls, small_rows, pieces, (core_sum, marker(MARK_COST, *backs.sums[1:])),
    )
    parts.add(last, together(blocks[last][0], grad_inputs)[0])
    parts.send_outward(grad_inputs)
    (grad_experts_in, grad_experts_out), (grad_qkv, grad_out), small, own, returned = sum_gradients(
        expert,
        dense_keep,
        dense_send,
        small,
        shared_rows,
        (write_expert, (((width, hidden_units), 0), ((hidden_units // width, width, width), 1))),
        (write_dense, (((width, 3 * width), 0), ((width, width), 0))),
        parts.sums,
    )
    result = sum((values.astype(F32) for values in returned), hidden).astype(BF16)
    return (
        result,
        grad_inputs,
        small[0],
        small[1],
        grad_qkv,
        small[2],
        small[3],
        grad_out,
        small[4],
        small[5],
        small[6],
        small[8 : 8 + experts].T,
        grad_experts_in[None],
        own[: hidden_units // width].reshape(1, hidden_units),
        grad_experts_out.reshape(1, hidden_units, width),
        own[hidden_units // width : hidden_units // width + 1],
    )


def solution(mesh):
    tokens = P(("rep", "exp"), None)
    expert3, expert2 = P("exp", None, None), P("exp", None)
    return jax.shard_map(
        on_device,
        mesh=mesh,
        in_specs=(tokens, tokens) + (P(),) * 10 + (expert3, expert2) * 2 + (tokens,),
        out_specs=(tokens, tokens) + (P(),) * 10 + (expert3, expert2) * 2,
        check_vma=False,
    )
```

```python
import functools

import jax
import jax.numpy as jnp
from jax import lax
from jax.experimental import pallas as pl
from jax.experimental.pallas import tpu as pltpu
from jax.sharding import PartitionSpec as P

HEADS = 12
HEAD_DIM = 64
SEQ = 197
NORM_EPS = 1e-06
F32 = jnp.float32
BF16 = jnp.bfloat16
LANES = 128
PAIR = LANES // HEAD_DIM
SEQ_PAD = 208
FF_TILE = 768
ROUTE_ROWS = 16
VMEM_BYTES = 58 * 2**20
COST_FLOPS = 4e8
OWN_COST = 24
NEAR_COST = 24
OTHER_COST = 1
PARTIAL_COST = 1
FINAL_COST = 4
BACK_COST = 28
MARK_COST = 400
TAIL_SCALE = 0.305
TAIL_COEFS = (
    0.1216396663821839,
    0.12246803351870969,
    0.10341227166034979,
    0.12105264456174025,
    -0.03803921974174099,
    0.18578799927872533,
    -0.1530311110530253,
    0.03670976324394601,
)
INV_SQRT_2PI = 0.3989422804014327
VECS = ("g1", "b1", "qb", "vb", "ob", "g2", "b2", "none")


def dot(lhs, rhs):
    return lax.dot_general(lhs, rhs, (((1,), (0,)), ((), ())), preferred_element_type=F32)


def dot_rt(lhs, rhs):
    return lax.dot_general(lhs, rhs, (((1,), (1,)), ((), ())), preferred_element_type=F32)


def dot_lt(lhs, rhs):
    return lax.dot_general(lhs, rhs, (((0,), (0,)), ((), ())), preferred_element_type=F32)


def row_mean(values):
    return jnp.mean(values, axis=-1, keepdims=True)


def unit_norm(values):
    centred = values - row_mean(values)
    scale = lax.rsqrt(row_mean(centred * centred) + NORM_EPS)
    return centred * scale, scale


def column_sum(values):
    return jnp.sum(values, axis=0, keepdims=True)


def gelu_parts(pre):
    size = jnp.abs(pre)
    bell = jnp.exp(pre * pre * -0.5)
    frac = 1.0 / (1.0 + TAIL_SCALE * size)
    poly = jnp.full_like(pre, TAIL_COEFS[-1])
    for coef in TAIL_COEFS[-2::-1]:
        poly = poly * frac + coef
    tail = bell * (poly * frac)
    return jnp.where(pre >= 0, 1.0 - tail, tail), bell * INV_SQRT_2PI


def pair_masks(rows):
    lane = lax.broadcasted_iota(jnp.int32, (rows, LANES), 1)
    return [(lane >= h * HEAD_DIM) & (lane < (h + 1) * HEAD_DIM) for h in range(PAIR)]


def stack_heads(values, masks):
    return jnp.concatenate([jnp.where(m, values, 0.0) for m in masks], axis=0).astype(BF16)


def unstack_heads(values, masks):
    rows = values.shape[0] // PAIR
    picked = values[:rows]
    for h in range(1, PAIR):
        picked = jnp.where(masks[h], values[h * rows : (h + 1) * rows], picked)
    return picked


def probabilities(scores):
    key_id = lax.broadcasted_iota(jnp.int32, scores.shape, 1)
    scores = jnp.where(key_id < SEQ, scores, -1e30)
    weights = jnp.exp(scores - jnp.max(scores, axis=-1, keepdims=True))
    return weights * (1.0 / jnp.sum(weights, axis=-1, keepdims=True))


class Fetch:
    def __init__(self, pairs, sems, first=0):
        self.copies = [
            pltpu.make_async_copy(source, target, sems.at[first + at]) for at, (source, target) in enumerate(pairs)
        ]
        for copy in self.copies:
            copy.start()

    def wait(self, *which):
        for at in which:
            self.copies[at].wait()


def attend_kernel(
    x_ref, vecs_ref, wqkv_ref, wout_ref,
    qkv_ref, ctx_ref, hidden_ref, mixed_ref,
    qkv_s, ctx_s,
):
    toks, width = x_ref.shape
    spare = qkv_s.shape[0] - toks
    x = x_ref[...].astype(F32)
    vec = lambda name: vecs_ref[VECS.index(name) : VECS.index(name) + 1, :]
    unit, _ = unit_norm(x)
    normed = (unit * vec("g1") + vec("b1")).astype(BF16)
    for part, bias in ((0, "qb"), (1, None), (2, "vb")):
        cols = pl.ds(part * width, width)
        joined = dot(normed, wqkv_ref[:, cols])
        if bias is not None:
            joined = joined + vec(bias)
        joined = joined.astype(BF16)
        qkv_ref[:, cols] = joined
        qkv_s[0:toks, cols] = joined.astype(F32)
    qkv_s[toks:, :] = jnp.zeros((spare, 3 * width), F32)
    masks = pair_masks(SEQ_PAD)
    for img in range(toks // SEQ):
        rows = pl.ds(img * SEQ, SEQ_PAD)
        for at in range(0, width, LANES):
            query = stack_heads(qkv_s[rows, at : at + LANES], masks)
            key = qkv_s[rows, width + at : width + at + LANES].astype(BF16)
            value = qkv_s[rows, 2 * width + at : 2 * width + at + LANES].astype(BF16)
            probs = probabilities(dot_rt(query, key) * HEAD_DIM**-0.5).astype(BF16)
            ctx_s[rows, at : at + LANES] = unstack_heads(dot(probs, value), masks)
    ctx = ctx_s[0:toks, :].astype(BF16)
    ctx_ref[...] = ctx
    hidden = x + dot(ctx, wout_ref[...]) + vec("ob")
    hidden_ref[...] = hidden
    unit2, _ = unit_norm(hidden)
    mixed_ref[...] = (unit2 * vec("g2") + vec("b2")).astype(BF16)


def expert_kernel(
    waits, me_ref, *refs,
):
    expert_body(me_ref, *refs[:8], *refs[8 + waits :])


def expert_body(
    me_ref,
    x_ref, up_ref, router_ref, router_t_ref, win_ref, bin_ref, wout_ref, bout_ref,
    part_ref, back_ref, activ_ref, gpre_ref, geout_ref, grouter_ref, gin_bias_ref, gout_bias_ref,
    out_s, back_s, probs_s, gate_s,
):
    step = pl.program_id(0)
    me = me_ref[0]
    toks = x_ref.shape[0]
    tail = up_ref.shape[0] - ROUTE_ROWS

    @pl.when(step == 0)
    def _():
        named = column_sum((up_ref[tail:, :].astype(F32) == me.astype(F32)).astype(F32))
        named = jnp.transpose(jnp.broadcast_to(named, (8, named.shape[1])))[:toks, 0:1]
        logits = dot(x_ref[...], router_ref[...])
        weights = jnp.exp(logits - jnp.max(logits, axis=-1, keepdims=True))
        probs = weights / jnp.sum(weights, axis=-1, keepdims=True)
        probs_s[...] = probs
        mine = lax.broadcasted_iota(jnp.int32, probs.shape, 1) == me
        gate = jnp.sum(jnp.where(mine, probs, 0.0), axis=-1, keepdims=True) * named
        gate_s[...] = gate
        geout = (gate * up_ref[0:toks, :].astype(F32)).astype(BF16)
        geout_ref[...] = geout
        gout_bias_ref[...] = column_sum(geout.astype(F32))
        out_s[...] = jnp.zeros_like(out_s)
        back_s[...] = jnp.zeros_like(back_s)

    pre = dot(x_ref[...], win_ref[...]) + bin_ref[...]
    phi, bell = gelu_parts(pre)
    activ = (pre * phi).astype(BF16)
    activ_ref[...] = activ
    gpre = (dot_rt(geout_ref[...], wout_ref[...]) * (phi + pre * bell)).astype(BF16)
    gpre_ref[...] = gpre
    gin_bias_ref[...] = column_sum(gpre.astype(F32))
    out_s[...] += dot(activ, wout_ref[...])
    back_s[...] += dot_rt(gpre, win_ref[...])

    @pl.when(step == pl.num_programs(0) - 1)
    def _():
        expert_out = (out_s[...] + bout_ref[...]).astype(BF16).astype(F32)
        gate = gate_s[...]
        probs = probs_s[...]
        part_ref[...] = (gate * expert_out).astype(BF16)
        route_grad = jnp.sum(up_ref[0:toks, :].astype(F32) * expert_out, axis=-1, keepdims=True)
        mine = (lax.broadcasted_iota(jnp.int32, probs.shape, 1) == me).astype(F32)
        glogits = gate * route_grad * (mine - probs)
        back = back_s[...].astype(BF16).astype(F32)
        for other in range(probs.shape[1]):
            back = back + glogits[:, other : other + 1] * router_t_ref[other : other + 1, :]
        back_ref[...] = back.astype(BF16)
        coarse = glogits.astype(BF16)
        fine = (glogits - coarse.astype(F32)).astype(BF16)
        grouter_ref[...] = dot_lt(coarse, x_ref[...]) + dot_lt(fine, x_ref[...])


def partial_grads_kernel(count, *refs):
    totals = [None, None]
    for k in range(count):
        rows, gpre, activ, geout = (refs[which * count + k][...] for which in range(4))
        for at, term in enumerate((dot_lt(rows, gpre), dot_lt(activ, geout))):
            totals[at] = term if totals[at] is None else totals[at] + term
    refs = refs[4 * count :]
    for at in range(2):
        refs[at][...] = totals[at]


def final_grads_kernel(count, half_ref, *refs):
    grad_ref = refs[-1]
    pieces, _, share, _ = grad_ref.shape
    grad_in, grad_out = refs[4 * count][...], refs[4 * count + 1][...]
    for k in range(count):
        rows, gpre, activ, geout = (refs[which * count + k][...] for which in range(4))
        grad_in = grad_in + dot_lt(rows, gpre)
        grad_out = grad_out + dot_lt(activ, geout)
    for piece in range(pieces):
        grad_ref[piece, 0] = grad_in[piece * share : (piece + 1) * share].astype(BF16)
        grad_ref[piece, 1] = grad_out[piece * share : (piece + 1) * share].astype(BF16)


def assemble_kernel(write, ids_ref, *refs):
    outs = refs[4:]
    at = pl.program_id(0)
    chosen = ((at // 2) ^ ids_ref[0]) * 2 + at % 2
    for which in range(4):

        @pl.when(chosen == which)
        def _(which=which):
            for piece in range(refs[which].shape[0]):
                write(refs[which][piece ^ ids_ref[1 + which % 2]].astype(F32), piece, *outs)


def write_dense(values, piece, qkv_ref, out_ref):
    share, cut = values.shape[0], qkv_ref.shape[1]
    rows = slice(piece * share, (piece + 1) * share)
    qkv_ref[rows, :] = values[:, :cut]
    out_ref[rows, :] = values[:, cut:]


def write_expert(values, piece, in_ref, out_ref):
    share, width = values.shape[1], out_ref.shape[2]
    rows = slice(piece * share, (piece + 1) * share)
    in_ref[rows, :] = values[0]
    for tile in range(out_ref.shape[0]):
        out_ref[tile, rows, :] = values[1, :, tile * width : (tile + 1) * width]


def attend_back_kernel(
    count, sums, core_ref, vecs_ref, *refs,
):
    loaded = sums + 7
    *refs, sems = refs
    refs, held = refs[:-loaded], refs[-loaded:]
    *refs, ginput_ref, keep_hbm, send_hbm, small_ref, qkv_s, gctx_s, gjoin_s, keep_ref, send_ref = refs
    fetch = Fetch(zip(refs[:loaded], held), sems)
    refs = refs[loaded:]
    gmix_refs = held[:sums]
    hidden_ref, up_ref, wout_ref, ctx_ref, qkv_ref, x_ref, wqkv_ref = held[sums:]
    fetch.wait(*range(sums + 2))
    toks, width = x_ref.shape
    spare = qkv_s.shape[0] - toks
    vec = lambda name: vecs_ref[VECS.index(name) : VECS.index(name) + 1, :]

    def put(values, start):
        cols = slice(start, start + values.shape[1])
        pieces, share = keep_ref.shape[:2]
        for first, halves in ((0, (keep_ref, send_ref)), (1, (send_ref, keep_ref))):

            @pl.when(core_ref[0] == first)
            def _(halves=halves):
                for piece in range(2 * pieces):
                    rows = slice(piece * share, (piece + 1) * share)
                    halves[piece // pieces][piece % pieces, :, cols] = values[rows].astype(BF16)

    gmix = gmix_refs[0][...].astype(F32)
    for ref in gmix_refs[1:]:
        gmix = gmix + ref[...].astype(F32)
    unit2, scale2 = unit_norm(hidden_ref[...])
    grad_g2 = column_sum(gmix * unit2)
    grad_b2 = column_sum(gmix)
    m2 = gmix * vec("g2")
    ghidden = up_ref[...].astype(F32) + scale2 * (m2 - row_mean(m2) - unit2 * row_mean(m2 * unit2))
    gatt = ghidden.astype(BF16)
    fetch.wait(sums + 2, sums + 3)
    grad_ob = column_sum(gatt.astype(F32))
    put(dot_lt(ctx_ref[...], gatt), 3 * width)
    gctx_s[0:toks, :] = dot_rt(gatt, wout_ref[...]).astype(BF16).astype(F32)
    gctx_s[toks:, :] = jnp.zeros((spare, width), F32)
    fetch.wait(sums + 4)
    qkv_s[0:toks, :] = qkv_ref[...].astype(F32)
    qkv_s[toks:, :] = jnp.zeros((spare, 3 * width), F32)
    masks = pair_masks(SEQ_PAD)
    row_ok = lax.broadcasted_iota(jnp.int32, (SEQ_PAD, 1), 0) < SEQ
    for img in range(toks // SEQ):
        rows = pl.ds(img * SEQ, SEQ_PAD)
        for at in range(0, width, LANES):
            query = stack_heads(jnp.where(row_ok, qkv_s[rows, at : at + LANES], 0.0), masks)
            key = qkv_s[rows, width + at : width + at + LANES].astype(BF16)
            value = qkv_s[rows, 2 * width + at : 2 * width + at + LANES].astype(BF16)
            gctx = stack_heads(jnp.where(row_ok, gctx_s[rows, at : at + LANES], 0.0), masks)
            probs = probabilities(dot_rt(query, key) * HEAD_DIM**-0.5)
            gvalue = dot_lt(probs.astype(BF16), gctx)
            gweights = dot_rt(gctx, value)
            inner = jnp.sum(gweights * probs, axis=-1, keepdims=True)
            gscores = (probs * (gweights - inner)).astype(BF16)
            gquery = unstack_heads(dot(gscores, key), masks) * HEAD_DIM**-0.5
            gkey = dot_lt(gscores, query) * HEAD_DIM**-0.5
            gjoin_s[rows, at : at + LANES] = gquery
            gjoin_s[rows, width + at : width + at + LANES] = gkey
            gjoin_s[rows, 2 * width + at : 2 * width + at + LANES] = gvalue
    gjoin = gjoin_s[0:toks, :].astype(BF16)
    grad_qb = column_sum(gjoin[:, :width].astype(F32))
    grad_vb = column_sum(gjoin[:, 2 * width :].astype(F32))
    fetch.wait(sums + 5, sums + 6)
    x = x_ref[...].astype(F32)
    unit1, scale1 = unit_norm(x)
    normed = (unit1 * vec("g1") + vec("b1")).astype(BF16)
    put(dot_lt(normed, gjoin), 0)
    store = Fetch(((keep_ref, keep_hbm), (send_ref, send_hbm)), sems, loaded)
    gnormed = dot_rt(gjoin, wqkv_ref[...])
    grad_g1 = column_sum(gnormed * unit1)
    grad_b1 = column_sum(gnormed)
    m1 = gnormed * vec("g1")
    ginput = ghidden + scale1 * (m1 - row_mean(m1) - unit1 * row_mean(m1 * unit1))
    ginput_ref[...] = ginput.astype(BF16)
    for at, small in enumerate((grad_g1, grad_b1, grad_qb, grad_vb, grad_ob, grad_g2, grad_b2)):
        small_ref[at : at + 1, :] = small
    small_ref[7:, :] = jnp.zeros((small_ref.shape[0] - 7, width), F32)
    total = lambda which: sum((ref[...] for ref in refs[which:count:3][1:]), refs[which][...])
    router_sum, in_sum, out_sum = (total(which) for which in range(3))
    small_ref[8 : 8 + router_sum.shape[0], :] = router_sum
    at = 8 + -(-router_sum.shape[0] // 8) * 8
    for tile in range(in_sum.shape[1] // width):
        small_ref[at + tile : at + tile + 1, :] = in_sum[:, tile * width : (tile + 1) * width]
    at += in_sum.shape[1] // width
    small_ref[at : at + 1, :] = out_sum
    store.wait(0, 1)


def params(**more):
    return pltpu.CompilerParams(vmem_limit_bytes=VMEM_BYTES, **more)


def cost(micros):
    return pl.CostEstimate(flops=int(micros * COST_FLOPS), bytes_accessed=1024, transcendentals=0)


def whole():
    return pl.BlockSpec(memory_space=pltpu.VMEM)


def outside():
    return pl.BlockSpec(memory_space=pl.ANY)


def scalars():
    return pl.BlockSpec(memory_space=pltpu.SMEM)


def attend(inputs, vecs, w_qkv, w_out):
    toks, width = inputs.shape
    padded = -(-(toks - SEQ + SEQ_PAD) // 16) * 16
    return pl.pallas_call(
        attend_kernel,
        out_shape=(
            jax.ShapeDtypeStruct((toks, 3 * width), BF16),
            jax.ShapeDtypeStruct((toks, width), BF16),
            jax.ShapeDtypeStruct((toks, width), F32),
            jax.ShapeDtypeStruct((toks, width), BF16),
        ),
        in_specs=[whole()] * 4,
        out_specs=(whole(),) * 4,
        scratch_shapes=[pltpu.VMEM((padded, 3 * width), F32), pltpu.VMEM((padded, width), F32)],
        compiler_params=params(),
        cost_estimate=cost(12),
        name="attend",
    )(inputs, vecs, w_qkv, w_out)


def attend_back(core, gmixes, up, inputs, hidden, qkv, ctx, vecs, w_qkv, w_out, smalls, small_rows, pieces, after):
    toks, width = inputs.shape
    padded = -(-(toks - SEQ + SEQ_PAD) // 16) * 16
    loaded = (*gmixes, hidden, up, w_out, ctx, qkv, inputs, w_qkv)
    half = jax.ShapeDtypeStruct((pieces, width // (2 * pieces), 4 * width), BF16)
    return pl.pallas_call(
        functools.partial(attend_back_kernel, len(smalls), len(gmixes)),
        out_shape=(
            jax.ShapeDtypeStruct((toks, width), BF16),
            half,
            half,
            jax.ShapeDtypeStruct((small_rows, width), F32),
        ),
        in_specs=[scalars(), whole()]
        + [outside()] * len(loaded)
        + [whole()] * len(smalls)
        + [outside()] * len(after),
        out_specs=(whole(), outside(), outside(), whole()),
        scratch_shapes=[
            pltpu.VMEM((padded, 3 * width), F32),
            pltpu.VMEM((padded, width), F32),
            pltpu.VMEM((padded, 3 * width), F32),
            pltpu.VMEM(half.shape, BF16),
            pltpu.VMEM(half.shape, BF16),
            *(pltpu.VMEM(array.shape, array.dtype) for array in loaded),
            pltpu.SemaphoreType.DMA((len(loaded) + 2,)),
        ],
        compiler_params=params(),
        cost_estimate=cost(BACK_COST),
        name="attend_back",
    )(core, vecs, *loaded, *smalls, *after)


def marker_kernel(*refs):
    refs[-1][...] = jnp.zeros_like(refs[-1])


def marker(micros, *arrays):
    return pl.pallas_call(
        marker_kernel,
        out_shape=jax.ShapeDtypeStruct((8, LANES), F32),
        in_specs=[outside()] * len(arrays),
        out_specs=whole(),
        compiler_params=params(),
        cost_estimate=cost(micros),
        name="marker",
    )(*arrays)


def expert_block(me, rows, up, router, router_t, w_in, b_in, w_out, b_out, after=(), micros=1):
    toks, width = rows.shape
    experts = router.shape[1]
    hidden = w_in.shape[1]
    fixed = lambda shape: pl.BlockSpec(shape, lambda f, m: (0, 0))
    return pl.pallas_call(
        functools.partial(expert_kernel, len(after)),
        out_shape=(
            jax.ShapeDtypeStruct((toks, width), BF16),
            jax.ShapeDtypeStruct((toks, width), BF16),
            jax.ShapeDtypeStruct((toks, hidden), BF16),
            jax.ShapeDtypeStruct((toks, hidden), BF16),
            jax.ShapeDtypeStruct((toks, width), BF16),
            jax.ShapeDtypeStruct((experts, width), F32),
            jax.ShapeDtypeStruct((1, hidden), F32),
            jax.ShapeDtypeStruct((1, width), F32),
        ),
        grid_spec=pltpu.PrefetchScalarGridSpec(
            num_scalar_prefetch=1,
            grid=(hidden // FF_TILE,),
            in_specs=[
                fixed((toks, width)),
                fixed(up.shape),
                fixed(router.shape),
                fixed(router_t.shape),
                pl.BlockSpec((width, FF_TILE), lambda f, m: (0, f)),
                pl.BlockSpec((1, FF_TILE), lambda f, m: (0, f)),
                pl.BlockSpec((FF_TILE, width), lambda f, m: (f, 0)),
                fixed((1, width)),
            ]
            + [pl.BlockSpec(memory_space=pl.ANY)] * len(after),
            out_specs=(
                fixed((toks, width)),
                fixed((toks, width)),
                pl.BlockSpec((toks, FF_TILE), lambda f, m: (0, f)),
                pl.BlockSpec((toks, FF_TILE), lambda f, m: (0, f)),
                fixed((toks, width)),
                fixed((experts, width)),
                pl.BlockSpec((1, FF_TILE), lambda f, m: (0, f)),
                fixed((1, width)),
            ),
            scratch_shapes=[
                pltpu.VMEM((toks, width), F32),
                pltpu.VMEM((toks, width), F32),
                pltpu.VMEM((toks, experts), F32),
                pltpu.VMEM((toks, 1), F32),
            ],
        ),
        compiler_params=params(),
        cost_estimate=cost(micros),
        name="expert_block",
    )(me, rows, up, router, router_t, w_in, b_in, w_out, b_out, *after)


def partial_grads(rows, gpres, activs, geouts):
    count = len(rows)
    toks, width = rows[0].shape
    hidden = gpres[0].shape[1]
    fixed = pl.BlockSpec((toks, width), lambda f: (0, 0))
    tile = pl.BlockSpec((toks, width), lambda f: (0, f))
    total = pl.BlockSpec((width, width), lambda f: (0, f))
    return pl.pallas_call(
        functools.partial(partial_grads_kernel, count),
        out_shape=(jax.ShapeDtypeStruct((width, hidden), F32),) * 2,
        grid=(hidden // width,),
        in_specs=[fixed] * count + [tile] * (2 * count) + [fixed] * count,
        out_specs=(total,) * 2,
        compiler_params=params(),
        cost_estimate=cost(PARTIAL_COST),
        name="partial_grads",
    )(*rows, *gpres, *activs, *geouts)


def final_grads(half, rows, gpres, activs, geouts, started, pieces, after=()):
    count = len(rows)
    toks, width = rows[0].shape
    hidden = gpres[0].shape[1]
    share = width // (2 * pieces)
    total = pl.BlockSpec((width // 2, width), lambda f, h: (h[0], f))
    return pl.pallas_call(
        functools.partial(final_grads_kernel, count),
        out_shape=jax.ShapeDtypeStruct((pieces, 2, share, hidden), BF16),
        grid_spec=pltpu.PrefetchScalarGridSpec(
            num_scalar_prefetch=1,
            grid=(hidden // width,),
            in_specs=[pl.BlockSpec((toks, width // 2), lambda f, h: (0, h[0]))] * count
            + [pl.BlockSpec((toks, width), lambda f, h: (0, f))] * count
            + [pl.BlockSpec((toks, width // 2), lambda f, h: (0, 2 * f + h[0]))] * count
            + [pl.BlockSpec((toks, width), lambda f, h: (0, 0))] * count
            + [total] * 2
            + [pl.BlockSpec(memory_space=pl.ANY)] * len(after),
            out_specs=pl.BlockSpec((pieces, 2, share, width), lambda f, h: (0, 0, 0, f)),
        ),
        compiler_params=params(),
        cost_estimate=cost(FINAL_COST),
        name="final_grads",
    )(half, *rows, *gpres, *activs, *geouts, *started, *after)


def assemble(ids, groups, write, outs):
    blocks = []
    for shape, dim in outs:
        block = tuple(n // 4 if d == dim else n for d, n in enumerate(shape))
        place = lambda at, ids, dim=dim, rank=len(shape): tuple(at if d == dim else 0 for d in range(rank))
        blocks.append(pl.BlockSpec(block, place))
    rank = groups[0].ndim
    return pl.pallas_call(
        functools.partial(assemble_kernel, write),
        out_shape=tuple(jax.ShapeDtypeStruct(shape, F32) for shape, _ in outs),
        grid_spec=pltpu.PrefetchScalarGridSpec(
            num_scalar_prefetch=1,
            grid=(4,),
            in_specs=[pl.BlockSpec(groups[0].shape, lambda at, ids: (0,) * rank)] * 4,
            out_specs=tuple(blocks),
        ),
        compiler_params=params(),
        cost_estimate=cost(5),
        name="assemble",
    )(ids, *groups)


def shift(values, axis, by):
    size = lax.axis_size(axis)
    return lax.ppermute(values, axis, [(i, (i + by) % size) for i in range(size)])


INNER_SWAP = [(1, 2), (2, 1)]
OUTWARD = [(1, 0), (2, 3)]


def at_end(axis):
    place = lax.axis_index(axis)
    return (place == 0) | (place == lax.axis_size(axis) - 1)


class LineGather:
    def __init__(self, values, axis):
        self.axis, self.own = axis, values
        self.near = swap(values, axis, 1)
        self.inner = lax.ppermute(values, axis, INNER_SWAP)

    def pass_on(self, *before):
        self.near, self.inner, *_ = together(self.near, self.inner, *before)
        self.far = lax.ppermute(self.near, self.axis, INNER_SWAP)
        self.outer = lax.ppermute(self.inner, self.axis, OUTWARD)

    def finish(self, *before):
        self.far, *_ = together(self.far, *before)
        last = lax.ppermute(self.far, self.axis, OUTWARD)
        end = at_end(self.axis)
        return jnp.where(end, self.outer, self.far), jnp.where(end, last, self.inner)


INWARD = [(0, 1), (3, 2)]


class Returns:
    def __init__(self, own, axis):
        self.axis, self.line = axis, lax.axis_size(axis) == 4
        self.sums, self.sent = [own], []

    def add(self, k, values, *hold):
        if not self.line:
            self.sums.append(shift(values, self.axis, -k))
        elif k == 1:
            self.near = values
            self.sent = [lax.ppermute(values, self.axis, INWARD)]
            self.sums += self.sent
        elif k == 2:
            if hold:
                values, *_ = lax.optimization_barrier((values, *hold))
            self.through = lax.ppermute(values, self.axis, INWARD)
            inner = lax.ppermute(values, self.axis, INNER_SWAP)
            self.sent = [self.through, inner]
            self.outward = add_rounded(self.near, inner)
        else:
            self.sums.append(swap(add_rounded(values, self.through), self.axis, 3))

    def send_outward(self, *before):
        if self.line:
            outward, *_ = lax.optimization_barrier((self.outward, *before))
            self.sums.append(lax.ppermute(outward, self.axis, OUTWARD))
            self.sent.append(self.sums[-1])


def ring_gather(values, axis):
    size = lax.axis_size(axis)
    found = {0: values}
    ahead = behind = values
    for k in range(1, (size + 1) // 2):
        ahead, behind = shift(ahead, axis, 1), shift(behind, axis, -1)
        found[k], found[size - k] = ahead, behind
    if size % 2 == 0:
        cut = middle_cut(values.shape[0])
        found[size // 2] = jnp.concatenate(
            [shift(ahead[:cut], axis, 1), shift(behind[cut:], axis, -1)], axis=0
        )
    return [found[k] for k in range(size)]


def middle_cut(rows):
    return rows // 16 * 8


def swap(values, axis, bit):
    return lax.ppermute(values, axis, [(i, i ^ bit) for i in range(lax.axis_size(axis))])


def axis_bit(axis, bit):
    return ((lax.axis_index(axis) // bit) % 2).astype(jnp.int32)


def halves(values, axis, bit):
    mine = axis_bit(axis, bit)
    size = values.shape[0] // 2
    part = lambda which: lax.dynamic_slice_in_dim(values, which * size, size, 0)
    return part(mine), part(1 - mine)


def add_rounded(one, other):
    return (one.astype(F32) + other.astype(F32)).astype(one.dtype)


def together(*trees):
    return lax.optimization_barrier(trees)


class PieceSum:
    def __init__(self, core_sum, axis):
        self.axis = axis
        bits = [1 << b for b in range(1, lax.axis_size(axis).bit_length() - 1)]
        self.orders = (bits, bits[::-1])
        self.steps = len(bits)
        self.pieces = 1 << self.steps
        self.parts = (core_sum[: self.pieces], core_sum[self.pieces :])

    def down(self, step):
        done = []
        for part, order in zip(self.parts, self.orders):
            keep, give = halves(part, self.axis, order[step])
            done.append(add_rounded(keep, swap(give, self.axis, order[step])))
        self.parts = tuple(done)

    def up(self, step):
        self.parts = tuple(
            jnp.concatenate([part, swap(part, self.axis, order[::-1][step])], axis=0)
            for part, order in zip(self.parts, self.orders)
        )

    def place(self, write, outs, got):
        ids = [axis_bit(self.axis, 1)]
        for order in self.orders:
            ids.append(sum(axis_bit(self.axis, bit) * (self.pieces >> at + 1) for at, bit in enumerate(order)))
        return assemble(jnp.stack(ids), (*self.parts, *got), write, outs)


def sum_gradients(expert, dense_keep, dense_send, small, shared_rows, expert_out, dense_out, parts):
    rep, exp = "rep", "exp"
    last = expert.steps - 1
    expert.down(0)
    expert.parts, dense_send, small = together(expert.parts, dense_send, small)
    for step in range(1, last + 1):
        expert.down(step)
    dense_sum = add_rounded(dense_keep, swap(dense_send, rep, 1))
    small = small + swap(small, rep, 1)

    expert.parts, dense_sum, small = together(expert.parts, dense_sum, small)
    dense = PieceSum(dense_sum, rep)
    for step in range(last):
        expert.up(step)
        dense.down(step)
        small = small + swap(small, rep, 2 << step)
        expert.parts, dense.parts, small = together(expert.parts, dense.parts, small)
    dense.down(last)
    small = small + swap(small, rep, 2 << last)

    dense.parts, small, expert.parts, parts = together(dense.parts, small, expert.parts, parts)
    expert.up(last)
    shape = (2, -1, *dense.parts[0].shape[1:])
    joined = jnp.concatenate(dense.parts, axis=0).reshape(-1, shape[-1])
    share = share_sum(joined, exp)
    share, small = together(share, small)
    joined = share_collect(share, exp).reshape(shape)
    shared = small[:shared_rows]
    shared = sum([shift(shared, exp, k) for k in range(1, lax.axis_size(exp))], shared)
    dense.parts = (joined[0], joined[1])

    dense.parts, shared, expert.parts = together(dense.parts, shared, expert.parts)
    got = [swap(part, rep, 1) for part in expert.parts]
    for step in range(last):
        dense.up(step)
    dense.parts, got, expert.parts = together(dense.parts, got, expert.parts)
    dense.up(last)
    placed = expert.place(*expert_out, got)
    dense.parts, placed = together(dense.parts, placed)
    got = [swap(part, rep, 1) for part in dense.parts]
    return placed, dense.place(*dense_out, got), shared, small[shared_rows:], parts


def share_sum(values, axis):
    size, me = lax.axis_size(axis), lax.axis_index(axis)
    share = values.shape[0] // size
    take = lambda owner: lax.dynamic_slice_in_dim(values, (owner % size) * share, share, 0)
    total = take(me).astype(F32)
    for k in range(1, size):
        total = total + shift(take(me + k), axis, k).astype(F32)
    return total.astype(values.dtype)


def share_collect(share, axis):
    size, me = lax.axis_size(axis), lax.axis_index(axis)
    rows = share.shape[0]
    result = jnp.zeros((size * rows, share.shape[1]), share.dtype)
    result = lax.dynamic_update_slice_in_dim(result, share, me * rows, 0)
    for k in range(1, size):
        result = lax.dynamic_update_slice_in_dim(result, shift(share, axis, k), ((me - k) % size) * rows, 0)
    return result


def on_device(
    inputs,
    routes,
    ln1_gain,
    ln1_bias,
    w_qkv,
    query_bias,
    value_bias,
    w_out,
    out_bias,
    ln2_gain,
    ln2_bias,
    router,
    experts_in,
    experts_in_bias,
    experts_out,
    experts_out_bias,
    cotangent,
):
    toks, width = inputs.shape
    experts = router.shape[1]
    hidden_units = experts_in.shape[2]
    me = lax.axis_index("exp").astype(jnp.int32).reshape(1)
    core = axis_bit("rep", 1).reshape(1)
    vecs = jnp.stack(
        [ln1_gain, ln1_bias, query_bias, value_bias, out_bias, ln2_gain, ln2_bias, jnp.zeros_like(ln1_gain)]
    )
    tail = -(-toks // 16) * 16
    named = jnp.full((tail - toks + ROUTE_ROWS, width), -1.0, BF16)
    named = named.at[tail - toks : tail - toks + routes.shape[1], :toks].set(routes.T.astype(BF16))

    pieces = lax.axis_size("rep")
    up_rows = jnp.concatenate([cotangent, named], axis=0)
    line = lax.axis_size("exp") == 4
    up_line = LineGather(up_rows, "exp") if line else None
    qkv, ctx, hidden, mixed = attend(inputs, vecs, w_qkv, w_out)
    mixed_line = LineGather(mixed, "exp") if line else None

    router_t = router.T.astype(F32)
    w_in, w_mid = experts_in[0], experts_out[0]
    run_block = lambda rows, up, after, micros: expert_block(
        me, rows, up, router, router_t, w_in, experts_in_bias, w_mid, experts_out_bias, after, micros
    )
    if line:
        up_line.pass_on()
        blocks = [run_block(mixed, up_rows, (up_line.near, up_line.inner), OWN_COST)]
        mixed_line.pass_on(blocks[0][0])
        mixes, ups = [mixed, mixed_line.near], [up_rows, up_line.near]
    else:
        mixes, ups = ring_gather(mixed, "exp"), ring_gather(up_rows, "exp")
        blocks = [run_block(mixed, up_rows, (), OWN_COST)]
    last = lax.axis_size("exp") - 1
    backs, parts = Returns(blocks[0][1], "exp"), Returns(blocks[0][0], "exp")
    sums, early = None, ()
    for k in range(1, last + 1):
        blocks.append(run_block(mixes[k], ups[k], early, NEAR_COST if k == 1 else OTHER_COST))
        if k == 1 and last == 3:
            sums = partial_grads(*([x[j] for j in range(2)] for x in (mixes, *zip(*[(b[3], b[2], b[4]) for b in blocks]))))
            ups += up_line.finish(sums[0])
            mixes += mixed_line.finish(sums[0])
        hold = (mixes[last], ups[last]) if k == last - 1 else ()
        backs.add(k, blocks[k][1], *hold)
        if k < last:
            parts.add(k, blocks[k][0], *hold)
        if k == last - 2:
            listed = lambda which: [mixes[j] if which is None else blocks[j][which] for j in range(k + 1)]
            sums = sums or partial_grads(listed(None), listed(3), listed(2), listed(4))
            early = (sums[0],)
            near_sent = (*backs.sent, *parts.sent)
        elif k == last - 1:
            early, middle_sent = near_sent, tuple(backs.sent)
    backs.send_outward(blocks[last][1])
    _, _, activs, gpres, geouts, grouters, gin_bias, gout_bias = zip(*blocks)
    final = lambda half, after: final_grads(
        half, mixes[-2:], gpres[-2:], activs[-2:], geouts[-2:], sums, pieces, after
    )
    send = final(1 - core, middle_sent)
    keep = final(core, (send,))
    core_sum = add_rounded(keep, swap(send, "rep", 1))
    expert = PieceSum(core_sum, "rep")

    smalls = [part for trio in zip(grouters, gin_bias, gout_bias) for part in trio]
    shared_rows = 8 + -(-experts // 8) * 8
    small_rows = shared_rows + -(-(hidden_units // width + 1) // 8) * 8
    grad_inputs, dense_keep, dense_send, small = attend_back(
        core, backs.sums, cotangent, inputs, hidden, qkv, ctx, vecs, w_qkv, w_out,
        smalls, small_rows, pieces, (core_sum, marker(MARK_COST, *backs.sums[1:])),
    )
    parts.add(last, together(blocks[last][0], grad_inputs)[0])
    parts.send_outward(grad_inputs)
    (grad_experts_in, grad_experts_out), (grad_qkv, grad_out), small, own, returned = sum_gradients(
        expert,
        dense_keep,
        dense_send,
        small,
        shared_rows,
        (write_expert, (((width, hidden_units), 0), ((hidden_units // width, width, width), 1))),
        (write_dense, (((width, 3 * width), 0), ((width, width), 0))),
        parts.sums,
    )
    result = sum((values.astype(F32) for values in returned), hidden).astype(BF16)
    return (
        result,
        grad_inputs,
        small[0],
        small[1],
        grad_qkv,
        small[2],
        small[3],
        grad_out,
        small[4],
        small[5],
        small[6],
        small[8 : 8 + experts].T,
        grad_experts_in[None],
        own[: hidden_units // width].reshape(1, hidden_units),
        grad_experts_out.reshape(1, hidden_units, width),
        own[hidden_units // width : hidden_units // width + 1],
    )


def solution(mesh):
    tokens = P(("rep", "exp"), None)
    expert3, expert2 = P("exp", None, None), P("exp", None)
    return jax.shard_map(
        on_device,
        mesh=mesh,
        in_specs=(tokens, tokens) + (P(),) * 10 + (expert3, expert2) * 2 + (tokens,),
        out_specs=(tokens, tokens) + (P(),) * 10 + (expert3, expert2) * 2,
        check_vma=False,
    )
```
